32 devices in a mesh: ctx: 8 (over y, x, core), head: 4 (over z).
Axes of the slice: x: 2, y: 2, z: 4, core: 2. Of those that a mesh axis runs over, the one named last changes fastest.
Arguments:
- queries: bfloat16 [8192, 8192], P('ctx', 'head'), may hold values from -6 to 6
- key_rows: bfloat16 [8192, 8192], P('ctx', 'head'), may hold values from -6 to 6
- values: bfloat16 [8192, 8192], P('ctx', 'head'), may hold values from -32 to 32, as said below
- gate_input: bfloat16 [8192, 8192], P('ctx', 'head'), may hold values from -6 to 6
- norm_gain: float32 [8192], P('head'), may hold values from 0.1 to 1.9
- session_of: int32 [8], replicated, may hold values from 0 to 1, as said below
Outputs:
- attended: bfloat16 [8192, 8192], P('ctx', 'head')
The draws below stay inside these ranges and needn't reach their ends.
Inputs may be any that keep to these rules, and one draw needn't show every extreme that they name: `session_of`: session numbers never fall along the blocks; one session holds exactly 6 consecutive blocks and the other the remaining 8 - 6. `values`: values are of order one to some tens.
All inputs are finite; a program needn't handle non-finite values.
Results may differ from the reference program's by a relative error of at most 0.0049.
Values sent between devices are 32-bit elements; how exact they have to be, the bound alone decides.
No kernel may reach another device: no remote copies, remote signals or barrier semaphores. Data moves between devices by JAX's collectives and lax.ppermute only.
A program may use at most 128 MiB of HBM per device.

```python
import jax
import jax.numpy as jnp
from jax import lax

HEADS = 64
HEAD_DIM = 128
TOK_DEV = 1024
TOKENS = 8192
MOST_DEV = 6
N_CTX = 8


def draw_values(key, part):
    first_key, second_key = jax.random.split(key, 2)
    width = HEADS * HEAD_DIM
    head_of = jnp.arange(width) // HEAD_DIM
    jitter = jnp.exp(jax.random.uniform(second_key, (HEADS,), minval=-0.35, maxval=0.35))
    rising = 10.0 ** (0.5 * head_of.astype(jnp.float32) / max(HEADS - 1, 1))
    column_scale = rising * jitter[head_of]
    base = jnp.clip(jax.random.normal(first_key, (TOKENS, width)), -6.0, 6.0)
    return (base * column_scale[None, :]).astype(jnp.float32).astype(jnp.bfloat16)


def draw_session_of(key, part):
    flip_key = jax.random.fold_in(key, 17)
    flip = jax.random.randint(flip_key, (), 0, 2).astype(jnp.int32)
    first_length = jnp.where(flip == 1, MOST_DEV, N_CTX - MOST_DEV).astype(jnp.int32)
    places = jnp.arange(N_CTX).astype(jnp.int32)
    return (places >= first_length).astype(jnp.int32)


def levels(key, shape, shards, smallest, largest):
    def one(position, shards_of):
        heights = jax.random.uniform(jax.random.fold_in(jax.random.fold_in(key, 6), position), (shards_of,), jnp.float32, smallest / len(shards), largest / len(shards))
        return jnp.repeat(jnp.exp(heights), shape[position] // shards_of).reshape((-1,) + (1,) * (len(shape) - position - 1))

    gain = one(*shards[0])
    for cut in shards[1:]:
        gain = gain * one(*cut)
    return gain


def gaussian(rng, dims, deviation, reach, cuts=(), kind=jnp.bfloat16):
    array = jax.random.normal(rng, dims, jnp.float32) * deviation
    if len(cuts) > 0:
        array = levels(rng, dims, cuts, -0.22, 0.18) * array
    return jnp.clip(array, min=-reach, max=reach).astype(kind)


def setup_inputs(seed: int = 0) -> dict:
    seeds = jax.random.split(jax.random.key(seed), 7)
    return {
        "queries": gaussian(seeds[0], (TOKENS, HEADS * HEAD_DIM), 1.0, 6.0, ((0, 8), (1, 4))),
        "key_rows": gaussian(seeds[1], (TOKENS, HEADS * HEAD_DIM), 1.0, 6.0, ((0, 8), (1, 4))),
        "values": draw_values(jax.random.fold_in(seeds[6], 71), 0),
        "gate_input": gaussian(seeds[3], (TOKENS, HEADS * HEAD_DIM), 1.0, 6.0, ((0, 8), (1, 4))),
        "norm_gain": jnp.clip(1.0 + 0.18 * jax.random.normal(seeds[4], (HEADS * HEAD_DIM,), jnp.float32), 0.1, 1.9),
        "session_of": draw_session_of(jax.random.fold_in(seeds[6], 71), 0),
    }


def reference(queries, key_rows, values, gate_input, norm_gain, session_of):
    shape4 = (N_CTX, TOK_DEV, HEADS, HEAD_DIM)
    qq = queries.reshape(shape4)
    kk = key_rows.reshape(shape4)
    vv = values.reshape(shape4)
    states = jnp.einsum('cthd,cthe->chde', kk.astype(jnp.float32), vv.astype(jnp.float32))

    def walk(carry, item):
        running, previous = carry
        state_now, tag, index = item
        first = jnp.logical_or(index == 0, tag != previous)
        running = jnp.where(first, jnp.zeros_like(running), running)
        return ((running + state_now, tag), running)
    init = (jnp.zeros((HEADS, HEAD_DIM, HEAD_DIM), jnp.float32), jnp.zeros((), jnp.int32))
    items = (states, session_of.astype(jnp.int32), jnp.arange(N_CTX).astype(jnp.int32))
    _, prefix = lax.scan(walk, init, items)
    prefix = lax.optimization_barrier(prefix.astype(jnp.bfloat16))
    positions = jnp.arange(TOK_DEV)
    causal = positions[:, None] >= positions[None, :]

    def one_block(args):
        qb, kb, vb, pb = args
        qf = qb.astype(jnp.float32)
        scores = jnp.einsum('thd,shd->hts', qf, kb.astype(jnp.float32))
        scores = jnp.where(causal[None], scores, 0.0).astype(jnp.bfloat16)
        scores = lax.optimization_barrier(scores)
        inner = jnp.einsum('hts,she->the', scores.astype(jnp.float32), vb.astype(jnp.float32))
        outer = jnp.einsum('thd,hde->the', qf, pb.astype(jnp.float32))
        return inner + outer
    mixed = lax.map(one_block, (qq, kk, vv, prefix)).reshape(TOKENS, HEADS * HEAD_DIM)
    power = lax.optimization_barrier(jnp.mean(mixed * mixed, axis=1, keepdims=True))
    normed = mixed * lax.rsqrt(power + 1e-06) * norm_gain[None, :]
    return (normed * jax.nn.sigmoid(gate_input.astype(jnp.float32))).astype(jnp.bfloat16)
```

```python
import jax
import jax.numpy as jnp
from jax import lax
from jax.experimental import pallas as pl
from jax.experimental.pallas import tpu as pltpu
from jax.sharding import PartitionSpec as P

HEAD_DIM = 128
PAIR = 2 * HEAD_DIM
CHUNK = 256
MIB = 1024 * 1024
F32 = jnp.float32
BF16 = jnp.bfloat16


def params(mib):
    return pltpu.CompilerParams(vmem_limit_bytes=mib * MIB)


def dot_tn(a, b):
    return lax.dot_general(a, b, (((0,), (0,)), ((), ())), preferred_element_type=F32)


def dot_nt(a, b):
    return lax.dot_general(a, b, (((1,), (1,)), ((), ())), preferred_element_type=F32)


def dot_nn(a, b):
    return lax.dot_general(a, b, (((1,), (0,)), ((), ())), preferred_element_type=F32)


def states_kernel(first_ref, key_ref, value_ref, state_ref):
    for h in range(key_ref.shape[1] // HEAD_DIM):
        cols = slice(h * HEAD_DIM, (h + 1) * HEAD_DIM)
        state_ref[cols, :] = dot_tn(key_ref[:, cols], value_ref[:, cols])


def half_states(first, key_rows, values):
    tokens, width = key_rows.shape
    steps = width // 2 // PAIR
    block = pl.BlockSpec((tokens, PAIR), lambda i, first_ref: (0, first_ref[0] * steps + i))
    return pl.pallas_call(
        states_kernel,
        grid_spec=pltpu.PrefetchScalarGridSpec(
            num_scalar_prefetch=1,
            grid=(steps,),
            in_specs=[block, block],
            out_specs=pl.BlockSpec((PAIR, HEAD_DIM), lambda i, first_ref: (i, 0)),
        ),
        out_shape=jax.ShapeDtypeStruct((width // 2, HEAD_DIM), F32),
        compiler_params=params(16),
        cost_estimate=pl.CostEstimate(
            flops=tokens * width * HEAD_DIM, bytes_accessed=2 * tokens * width, transcendentals=0
        ),
        name="states",
    )(first, key_rows, values)


def inner_kernel(query_ref, key_ref, value_ref, inner_ref):
    tokens = query_ref.shape[0]
    rows_at = lax.broadcasted_iota(jnp.int32, (CHUNK, CHUNK), 0)
    cols_at = lax.broadcasted_iota(jnp.int32, (CHUNK, CHUNK), 1)
    causal = rows_at >= cols_at
    for h in range(query_ref.shape[1] // HEAD_DIM):
        cols = slice(h * HEAD_DIM, (h + 1) * HEAD_DIM)
        before = None
        for c in range(tokens // CHUNK):
            rows = slice(c * CHUNK, (c + 1) * CHUNK)
            query, key, value = query_ref[rows, cols], key_ref[rows, cols], value_ref[rows, cols]
            scores = jnp.where(causal, dot_nt(query, key), 0.0).astype(BF16)
            out = dot_nn(scores, value)
            if before is not None:
                out += dot_nn(query, before.astype(BF16))
            inner_ref[rows, cols] = out
            if c + 1 < tokens // CHUNK:
                state = dot_tn(key, value)
                before = state if before is None else before + state


def inner_part(queries, key_rows, values, part, parts):
    tokens, width = queries.shape
    steps = width // parts // PAIR
    block = pl.BlockSpec((tokens, PAIR), lambda i: (0, part * steps + i))
    return pl.pallas_call(
        inner_kernel,
        grid=(steps,),
        in_specs=[block, block, block],
        out_specs=pl.BlockSpec((tokens, PAIR), lambda i: (0, i)),
        out_shape=jax.ShapeDtypeStruct((tokens, width // parts), F32),
        compiler_params=params(24),
        cost_estimate=pl.CostEstimate(
            flops=tokens * width // parts * 6 * CHUNK,
            bytes_accessed=10 * tokens * width // parts,
            transcendentals=0,
        ),
        name="inner",
    )(queries, key_rows, values)


def mixed_kernel(query_ref, inner_ref, prefix_ref, mixed_ref, power_ref, total_ref):
    step = pl.program_id(0)
    squares = None
    for h in range(query_ref.shape[1] // HEAD_DIM):
        cols = slice(h * HEAD_DIM, (h + 1) * HEAD_DIM)
        mixed = inner_ref[:, cols] + dot_nn(query_ref[:, cols], prefix_ref[cols, :].astype(BF16))
        mixed_ref[:, cols] = mixed
        square = mixed * mixed
        squares = square if squares is None else squares + square

    @pl.when(step == 0)
    def _():
        total_ref[...] = squares

    @pl.when(step > 0)
    def _():
        total_ref[...] += squares

    @pl.when(step == pl.num_programs(0) - 1)
    def _():
        power_ref[...] = jnp.sum(jnp.transpose(total_ref[...]), axis=0, keepdims=True)


def mix(queries, inner, prefix):
    tokens, width = queries.shape
    block = pl.BlockSpec((tokens, PAIR), lambda i: (0, i))
    return pl.pallas_call(
        mixed_kernel,
        grid=(width // PAIR,),
        in_specs=[block, block, pl.BlockSpec((PAIR, HEAD_DIM), lambda i: (i, 0))],
        out_specs=[block, pl.BlockSpec((1, tokens), lambda i: (0, 0))],
        out_shape=[
            jax.ShapeDtypeStruct((tokens, width), F32),
            jax.ShapeDtypeStruct((1, tokens), F32),
        ],
        scratch_shapes=[pltpu.VMEM((tokens, HEAD_DIM), F32)],
        compiler_params=params(24),
        cost_estimate=pl.CostEstimate(
            flops=2 * tokens * width * HEAD_DIM, bytes_accessed=10 * tokens * width, transcendentals=0
        ),
        name="mix",
    )(queries, inner, prefix)


def gate_kernel(mixed_ref, gate_ref, gain_ref, gated_ref):
    gate = gate_ref[...].astype(F32)
    gated_ref[...] = mixed_ref[...] * gain_ref[...] * jax.nn.sigmoid(gate)


def gate(mixed, gate_input, norm_gain):
    tokens, width = mixed.shape
    block = pl.BlockSpec((tokens, PAIR), lambda i: (0, i))
    return pl.pallas_call(
        gate_kernel,
        grid=(width // PAIR,),
        in_specs=[block, block, pl.BlockSpec((1, PAIR), lambda i: (0, i))],
        out_specs=block,
        out_shape=jax.ShapeDtypeStruct((tokens, width), F32),
        compiler_params=params(24),
        cost_estimate=pl.CostEstimate(
            flops=8 * tokens * width, bytes_accessed=10 * tokens * width, transcendentals=tokens * width
        ),
        name="gate",
    )(mixed, gate_input, norm_gain.reshape(1, width))


def scale_kernel(features, gated_ref, power_ref, out_ref):
    power = jnp.broadcast_to(power_ref[...], (HEAD_DIM, power_ref.shape[1]))
    factor = lax.rsqrt(jnp.transpose(power) / features + 1e-06)
    for h in range(gated_ref.shape[1] // HEAD_DIM):
        cols = slice(h * HEAD_DIM, (h + 1) * HEAD_DIM)
        out_ref[:, cols] = (gated_ref[:, cols] * factor).astype(BF16)


def scale(gated, power, features):
    tokens, width = gated.shape
    rows = tokens // 8
    block = pl.BlockSpec((rows, width), lambda i: (i, 0))
    return pl.pallas_call(
        lambda *refs: scale_kernel(features, *refs),
        grid=(tokens // rows,),
        in_specs=[block, pl.BlockSpec((1, rows), lambda i: (0, i))],
        out_specs=block,
        out_shape=jax.ShapeDtypeStruct((tokens, width), BF16),
        compiler_params=params(24),
        cost_estimate=pl.CostEstimate(
            flops=2 * tokens * width, bytes_accessed=6 * tokens * width, transcendentals=0
        ),
        name="scale",
    )(gated, power)


def swap(count, bit):
    return [(i, i ^ bit) for i in range(count)]


def chip_prefix(keep, send, session_of, blocks):
    place = lax.axis_index("ctx")
    core = place % 2
    chip = place // 2

    def flag(condition):
        return jnp.where(condition, 1.0, 0.0).astype(F32)

    def first_of(c):
        return session_of[2 * c]

    def last_of(c):
        return session_of[2 * c + 1]

    def need(dest, source):
        return flag(jnp.logical_and(source < dest, first_of(dest) == last_of(source)))

    whole = flag(first_of(chip) == last_of(chip))
    got = lax.ppermute(send, "ctx", swap(blocks, 1))
    own_weight = jnp.where(core == 0, whole, 1.0)
    got_weight = jnp.where(core == 0, 1.0, whole)
    chip_sum = own_weight * keep + got_weight * got
    return core, chip, need, whole, got, chip_sum


def on_device(blocks, features, queries, key_rows, values, gate_input, norm_gain, session_of):
    tokens, width = queries.shape
    place = lax.axis_index("ctx")
    core = place % 2
    as_index = core.astype(jnp.int32).reshape(1)
    send = half_states(1 - as_index, key_rows, values)
    keep = half_states(as_index, key_rows, values)
    core, chip, need, whole, got, chip_sum = chip_prefix(keep, send, session_of, blocks)
    inner = inner_part(queries, key_rows, values, 0, 1)

    if blocks == 8:
        first_step = [(i, i ^ (2 if i % 2 == 0 else 4)) for i in range(blocks)]
        second_step = [(i, i ^ (4 if i % 2 == 0 else 2)) for i in range(blocks)]
        partner = jnp.where(core == 0, chip ^ 1, chip ^ 2)
        dest = jnp.where(core == 0, chip ^ 2, chip ^ 1)
        there = lax.ppermute(chip_sum, "ctx", first_step)
        onward = need(dest, chip) * chip_sum + need(dest, partner) * there
        mine = need(chip, partner) * there
        prefix = mine + lax.ppermute(onward, "ctx", second_step)
    else:
        total = chip_sum
        prefix = jnp.zeros_like(chip_sum)
        bit = 1
        while 2 * bit < blocks:
            there = lax.ppermute(total, "ctx", swap(blocks, 2 * bit))
            partner = chip ^ bit
            lower = partner < chip
            last_here = chip | (bit - 1)
            last_there = partner | (bit - 1)
            same_group_end = session_of[2 * last_here + 1] == session_of[2 * last_there + 1]
            reaches = session_of[2 * last_there + 1] == session_of[2 * chip]
            prefix = prefix + jnp.where(jnp.logical_and(lower, reaches), 1.0, 0.0) * there
            joined = jnp.where(same_group_end, 1.0, 0.0)
            total = jnp.where(lower, total + joined * there, joined * total + there)
            bit *= 2

    back = prefix + jnp.where(core == 0, 1.0, 0.0) * keep
    other = lax.ppermute(back, "ctx", swap(blocks, 1))
    mine = jnp.where(core == 0, 1.0, whole) * (prefix + jnp.where(core == 0, 0.0, 1.0) * got)
    other = jnp.where(core == 0, 1.0, whole) * other
    low = jnp.where(core == 0, mine, other)
    high = jnp.where(core == 0, other, mine)
    prefix = jnp.concatenate([low, high], axis=0).astype(BF16)

    mixed, power = mix(queries, inner, prefix)
    count = features // width
    bit = 1
    while bit < count:
        power = power + lax.ppermute(power, "head", swap(count, bit))
        bit *= 2
    gated = gate(mixed, gate_input, norm_gain)
    return scale(gated, power, features)


def solution(mesh):
    blocks = mesh.shape["ctx"]

    def whole(queries, key_rows, values, gate_input, norm_gain, session_of):
        features = queries.shape[1]
        return jax.shard_map(
            lambda *args: on_device(blocks, features, *args),
            mesh=mesh,
            in_specs=(
                P("ctx", "head"),
                P("ctx", "head"),
                P("ctx", "head"),
                P("ctx", "head"),
                P("head"),
                P(),
            ),
            out_specs=P("ctx", "head"),
            check_vma=False,
        )(queries, key_rows, values, gate_input, norm_gain, session_of)

    return whole
```

```python
import jax
import jax.numpy as jnp
from jax import lax
from jax.experimental import pallas as pl
from jax.experimental.pallas import tpu as pltpu
from jax.sharding import PartitionSpec as P

HEAD_DIM = 128
CHUNK = 256
MIB = 1024 * 1024
F32 = jnp.float32
BF16 = jnp.bfloat16
WHOLE = pl.BlockSpec(memory_space=pltpu.VMEM)
SCALARS = pl.BlockSpec(memory_space=pltpu.SMEM)
ANYWHERE = pl.BlockSpec(memory_space=pl.ANY)


def params(mib):
    return pltpu.CompilerParams(vmem_limit_bytes=mib * MIB)


def in_hbm(x):
    return pltpu.with_memory_space_constraint(x, pltpu.HBM)


def in_vmem(x):
    return pltpu.with_memory_space_constraint(x, pltpu.VMEM)


def cost(flops, bytes_accessed):
    return pl.CostEstimate(flops=flops, bytes_accessed=bytes_accessed, transcendentals=0)


def dot_tn(a, b):
    return lax.dot_general(a, b, (((0,), (0,)), ((), ())), preferred_element_type=F32)


def dot_nt(a, b):
    return lax.dot_general(a, b, (((1,), (1,)), ((), ())), preferred_element_type=F32)


def dot_nn(a, b):
    return lax.dot_general(a, b, (((1,), (0,)), ((), ())), preferred_element_type=F32)


def head(h):
    return slice(h * HEAD_DIM, (h + 1) * HEAD_DIM)


def chunk(c):
    return slice(c * CHUNK, (c + 1) * CHUNK)


def columns(place_ref, mine, half):
    core = place_ref[0] & 1
    return pl.ds(pl.multiple_of((core if mine else 1 - core) * half, half), half)


def states_kernel(mine, place_ref, key_ref, value_ref, state_ref, before_ref, keys, vals, sems):
    tokens, half = keys.shape
    cols = columns(place_ref, mine, half)
    copies = []
    for c in range(tokens // CHUNK):
        for j, (source, to) in enumerate(((key_ref, keys), (value_ref, vals))):
            copies.append(pltpu.make_async_copy(source.at[chunk(c), cols], to.at[chunk(c), :], sems.at[2 * c + j]))
            copies[-1].start()
    for c in range(tokens // CHUNK):
        copies[2 * c].wait()
        copies[2 * c + 1].wait()
        for h in range(half // HEAD_DIM):
            new = dot_tn(keys[chunk(c), head(h)], vals[chunk(c), head(h)])
            if c == 0:
                state_ref[head(h), :] = new
            else:
                old = state_ref[head(h), :]
                at = (c - 1) * half + h * HEAD_DIM
                before_ref[at : at + HEAD_DIM, :] = old.astype(BF16)
                state_ref[head(h), :] = old + new


def half_states(place, key_rows, values, mine):
    tokens, width = key_rows.shape
    half = width // 2
    chunks = tokens // CHUNK
    return pl.pallas_call(
        lambda *refs: states_kernel(mine, *refs),
        in_specs=[SCALARS, ANYWHERE, ANYWHERE],
        out_specs=[WHOLE] * 4,
        out_shape=[
            pltpu.VMEM((half, HEAD_DIM), F32),
            pltpu.VMEM(((chunks - 1) * half, HEAD_DIM), BF16),
            pltpu.VMEM((tokens, half), BF16),
            pltpu.VMEM((tokens, half), BF16),
        ],
        scratch_shapes=[pltpu.SemaphoreType.DMA((2 * chunks,))],
        compiler_params=params(24),
        cost_estimate=cost(tokens * width * HEAD_DIM, 2 * tokens * width),
        name="states",
    )(place, in_hbm(key_rows), in_hbm(values))


def write_weights(place_ref, session_ref, weight_ref):
    place = place_ref[0]
    core = place & 1
    chip = lax.shift_right_logical(place, 1)

    def flag(condition):
        return jnp.where(condition, 1.0, 0.0).astype(F32)

    def need(to, source):
        same = session_ref[2 * to] == session_ref[2 * source + 1]
        return flag(jnp.logical_and(source < to, same))

    even = core == 0
    if session_ref.shape[0] == 8:
        partner = jnp.where(even, chip ^ 1, chip ^ 2)
        to = jnp.where(even, chip ^ 2, chip ^ 1)
        rows = [need(to, chip), need(to, partner), need(chip, partner), flag(even), flag(core == 1)]
    else:
        rows = [flag(even)] * 5
    for r, value in enumerate(rows):
        weight_ref[r : r + 1, :] = jnp.full((1, HEAD_DIM), value, F32)


def inner_kernel(
    mine, place_ref, session_ref, query_ref, gate_ref, gain_ref, key_ref, value_ref, before_ref,
    after_ref, inner_ref, query_out_ref, factor_ref, weight_ref, gates, sems,
):
    tokens, half = key_ref.shape
    cols = columns(place_ref, mine, half)
    copies = []
    for c in range(tokens // CHUNK):
        for j, (source, to) in enumerate(((query_ref, query_out_ref), (gate_ref, gates))):
            copies.append(pltpu.make_async_copy(source.at[chunk(c), cols], to.at[chunk(c), :], sems.at[2 * c + j]))
            copies[-1].start()
    write_weights(place_ref, session_ref, weight_ref)
    rows_at = lax.broadcasted_iota(jnp.int32, (CHUNK, CHUNK), 0)
    cols_at = lax.broadcasted_iota(jnp.int32, (CHUNK, CHUNK), 1)
    causal = rows_at >= cols_at
    gain = gain_ref[:, cols]
    for c in range(tokens // CHUNK):
        copies[2 * c].wait()
        for h in range(half // HEAD_DIM):
            query = query_out_ref[chunk(c), head(h)]
            scores = dot_nt(query, key_ref[chunk(c), head(h)])
            scores = jnp.where(causal, scores, 0.0).astype(BF16)
            out = dot_nn(scores, value_ref[chunk(c), head(h)])
            if c > 0:
                at = (c - 1) * half + h * HEAD_DIM
                out += dot_nn(query, before_ref[at : at + HEAD_DIM, :])
            inner_ref[chunk(c), head(h)] = out
        copies[2 * c + 1].wait()
        for h in range(half // HEAD_DIM):
            gate = gates[chunk(c), head(h)].astype(F32)
            factor_ref[chunk(c), head(h)] = (0.5 * gain[:, head(h)]) * (1.0 + jnp.tanh(0.5 * gate))


def half_inner(place, session_of, queries, gate_input, norm_gain, keys, vals, before, after, mine):
    tokens, width = queries.shape
    half = width // 2
    chunks = tokens // CHUNK
    return pl.pallas_call(
        lambda *refs: inner_kernel(mine, *refs),
        in_specs=[SCALARS, SCALARS, ANYWHERE, ANYWHERE, WHOLE, WHOLE, WHOLE, WHOLE, ANYWHERE],
        out_specs=[WHOLE] * 4,
        out_shape=[
            pltpu.VMEM((tokens, half), F32),
            pltpu.VMEM((tokens, half), BF16),
            pltpu.VMEM((tokens, half), F32),
            pltpu.VMEM((8, HEAD_DIM), F32),
        ],
        scratch_shapes=[pltpu.VMEM((tokens, half), BF16), pltpu.SemaphoreType.DMA((2 * chunks,))],
        compiler_params=params(32),
        cost_estimate=cost(tokens * width * 3 * CHUNK, 6 * tokens * width),
        name="inner",
    )(
        place, session_of, in_hbm(queries), in_hbm(gate_input), norm_gain.reshape(1, width),
        in_vmem(keys), in_vmem(vals), in_vmem(before), after,
    )


def pair_prefix(prefix_ref, h):
    zero = jnp.zeros((HEAD_DIM, HEAD_DIM), BF16)
    top = jnp.concatenate([prefix_ref[head(h), :].astype(BF16), zero], axis=1)
    low = jnp.concatenate([zero, prefix_ref[head(h + 1), :].astype(BF16)], axis=1)
    return jnp.concatenate([top, low], axis=0)


def mix_kernel(last, query_ref, inner_ref, prefix_ref, extra_ref, mixed_ref, result_ref):
    tokens, half = query_ref.shape
    blocks = [pair_prefix(prefix_ref, h) for h in range(0, half // HEAD_DIM, 2)]
    for c in range(tokens // CHUNK):
        squares = extra_ref[chunk(c), :] if last else None
        for p, block in enumerate(blocks):
            both = slice(2 * p * HEAD_DIM, (2 * p + 2) * HEAD_DIM)
            outer = dot_nn(query_ref[chunk(c), both], block)
            for j in range(2):
                at = head(2 * p + j)
                mixed = inner_ref[chunk(c), at] + outer[:, head(j)]
                square = mixed * mixed
                squares = square if squares is None else squares + square
                mixed_ref[chunk(c), at] = mixed if last else mixed * extra_ref[chunk(c), at]
        if last:
            result_ref[:, chunk(c)] = jnp.sum(jnp.transpose(squares), axis=0, keepdims=True)
        else:
            result_ref[chunk(c), :] = squares


def mix(queries, inner, prefix, extra, last):
    tokens, half = queries.shape
    return pl.pallas_call(
        lambda *refs: mix_kernel(last, *refs),
        in_specs=[WHOLE] * 4,
        out_specs=[WHOLE, WHOLE],
        out_shape=[
            pltpu.VMEM((tokens, half), F32),
            pltpu.VMEM((1, tokens) if last else (tokens, HEAD_DIM), F32),
        ],
        input_output_aliases={1: 0},
        compiler_params=params(24),
        cost_estimate=cost(2 * tokens * half * HEAD_DIM, 2 * tokens * half),
        name="mix",
    )(*[in_vmem(x) for x in (queries, inner, prefix, extra)])


def gate_kernel(mixed_ref, factor_ref, gated_ref):
    for c in range(mixed_ref.shape[0] // CHUNK):
        gated_ref[chunk(c), :] = mixed_ref[chunk(c), :] * factor_ref[chunk(c), :]


def gated(mixed, factor):
    return pl.pallas_call(
        gate_kernel,
        in_specs=[WHOLE, WHOLE],
        out_specs=WHOLE,
        out_shape=pltpu.VMEM(mixed.shape, F32),
        input_output_aliases={0: 0},
        compiler_params=params(24),
        cost_estimate=cost(mixed.size, 4 * mixed.size),
        name="gate",
    )(in_vmem(mixed), in_vmem(factor))


def scale_kernel(features, place_ref, mine_ref, other_ref, power_ref, out_ref, mine_out, other_out, sems):
    tokens, half = mine_ref.shape
    rows = HEAD_DIM
    copies = []
    for c in range(tokens // rows):
        at = slice(c * rows, (c + 1) * rows)
        power = jnp.broadcast_to(power_ref[:, at], (HEAD_DIM, rows))
        factor = lax.rsqrt(jnp.transpose(power) / features + 1e-06)
        for j, (source, to) in enumerate(((mine_ref, mine_out), (other_ref, other_out))):
            for h in range(half // HEAD_DIM):
                to[at, head(h)] = (source[at, head(h)] * factor).astype(BF16)
            cols = columns(place_ref, j == 0, half)
            copies.append(pltpu.make_async_copy(to.at[at, :], out_ref.at[at, cols], sems.at[2 * c + j]))
            copies[-1].start()
    for copy in copies:
        copy.wait()


def scale(place, mine, other, power, features):
    tokens, half = mine.shape
    return pl.pallas_call(
        lambda *refs: scale_kernel(features, *refs),
        in_specs=[SCALARS, WHOLE, WHOLE, WHOLE],
        out_specs=ANYWHERE,
        out_shape=jax.ShapeDtypeStruct((tokens, 2 * half), BF16),
        scratch_shapes=[
            pltpu.VMEM((tokens, half), BF16),
            pltpu.VMEM((tokens, half), BF16),
            pltpu.SemaphoreType.DMA((2 * tokens // HEAD_DIM,)),
        ],
        compiler_params=params(24),
        cost_estimate=cost(4 * tokens * half, 4 * tokens * half),
        name="scale",
    )(place, in_vmem(mine), in_vmem(other), in_vmem(power))


def swap(count, bit):
    return [(i, i ^ bit) for i in range(count)]


def general_prefix(blocks, chip, session_of, chip_sum):
    total = chip_sum
    prefix = jnp.zeros_like(chip_sum)
    bit = 1
    while 2 * bit < blocks:
        there = lax.ppermute(total, "ctx", swap(blocks, 2 * bit))
        partner = chip ^ bit
        lower = partner < chip
        end_here = session_of[2 * (chip | (bit - 1)) + 1]
        end_there = session_of[2 * (partner | (bit - 1)) + 1]
        reaches = jnp.logical_and(lower, end_there == session_of[2 * chip])
        prefix = prefix + jnp.where(reaches, 1.0, 0.0) * there
        joined = jnp.where(end_here == end_there, 1.0, 0.0)
        total = jnp.where(lower, total + joined * there, joined * total + there)
        bit *= 2
    return prefix


def on_device(blocks, features, queries, key_rows, values, gate_input, norm_gain, session_of):
    width = queries.shape[1]
    index = lax.axis_index("ctx").astype(jnp.int32)
    place = index.reshape(1)

    def inner_of(half, after, mine):
        _, before, keys, vals = half
        return half_inner(
            place, session_of, queries, gate_input, norm_gain, keys, vals, before, after, mine
        )

    sent = half_states(place, key_rows, values, False)
    got = lax.ppermute(sent[0], "ctx", swap(blocks, 1))
    kept = half_states(place, key_rows, values, True)
    chip_sum = kept[0] + got
    inner_mine, query_mine, factor_mine, weight = inner_of(kept, chip_sum, True)

    if blocks == 8:
        first_step = [(i, i ^ (2 if i % 2 == 0 else 4)) for i in range(blocks)]
        second_step = [(i, i ^ (4 if i % 2 == 0 else 2)) for i in range(blocks)]
        there = lax.ppermute(chip_sum, "ctx", first_step)
        onward = weight[0:1] * chip_sum + weight[1:2] * there
        arrived = lax.ppermute(onward, "ctx", second_step)
        inner_other, query_other, factor_other, weight = inner_of(sent, onward, False)
        prefix = weight[2:3] * there + arrived
    else:
        inner_other, query_other, factor_other, weight = inner_of(sent, chip_sum, False)
        prefix = general_prefix(blocks, index >> 1, session_of, chip_sum)

    core = index & 1
    even, odd = (weight[3:4], weight[4:5]) if blocks == 8 else ((1 - core).astype(F32), core.astype(F32))
    other = lax.ppermute(prefix + even * kept[0], "ctx", swap(blocks, 1))
    mine = prefix + odd * got
    mixed_mine, squares = mix(query_mine, inner_mine, mine, factor_mine, False)
    mixed_other, power = mix(query_other, inner_other, other, squares, True)
    bit = 1
    while bit < features // width:
        power = power + lax.ppermute(power, "head", swap(features // width, bit))
        bit *= 2
    return scale(place, mixed_mine, gated(mixed_other, factor_other), power, features)


def solution(mesh):
    blocks = mesh.shape["ctx"]

    def whole(queries, key_rows, values, gate_input, norm_gain, session_of):
        features = queries.shape[1]
        return jax.shard_map(
            lambda *args: on_device(blocks, features, *args),
            mesh=mesh,
            in_specs=(
                P("ctx", "head"),
                P("ctx", "head"),
                P("ctx", "head"),
                P("ctx", "head"),
                P("head"),
                P(),
            ),
            out_specs=P("ctx", "head"),
            check_vma=False,
        )(queries, key_rows, values, gate_input, norm_gain, session_of)

    return whole
```

```python
import jax
import jax.numpy as jnp
from jax import lax
from jax.experimental import pallas as pl
from jax.experimental.pallas import tpu as pltpu
from jax.sharding import PartitionSpec as P

HEAD_DIM = 128
CHUNK = 256
GROUPS = 2
MIB = 1024 * 1024
F32 = jnp.float32
BF16 = jnp.bfloat16
WHOLE = pl.BlockSpec(memory_space=pltpu.VMEM)
SCALARS = pl.BlockSpec(memory_space=pltpu.SMEM)
ANYWHERE = pl.BlockSpec(memory_space=pl.ANY)


def params(mib):
    return pltpu.CompilerParams(vmem_limit_bytes=mib * MIB)


def in_hbm(x):
    return pltpu.with_memory_space_constraint(x, pltpu.HBM)


def in_vmem(x):
    return pltpu.with_memory_space_constraint(x, pltpu.VMEM)


def cost(flops, bytes_accessed):
    return pl.CostEstimate(flops=flops, bytes_accessed=bytes_accessed, transcendentals=0)


def dot_tn(a, b):
    return lax.dot_general(a, b, (((0,), (0,)), ((), ())), preferred_element_type=F32)


def dot_nt(a, b):
    return lax.dot_general(a, b, (((1,), (1,)), ((), ())), preferred_element_type=F32)


def dot_nn(a, b):
    return lax.dot_general(a, b, (((1,), (0,)), ((), ())), preferred_element_type=F32)


def head(h):
    return slice(h * HEAD_DIM, (h + 1) * HEAD_DIM)


def chunk(c):
    return slice(c * CHUNK, (c + 1) * CHUNK)


def columns(place_ref, mine, half):
    core = place_ref[0] & 1
    return pl.ds(pl.multiple_of((core if mine else 1 - core) * half, half), half)


def states_kernel(mine, planned, groups, place_ref, key_ref, value_ref, *refs):
    if planned:
        session_ref, *refs = refs
    state_refs, refs = refs[:groups], refs[groups:]
    if planned:
        before_ref, keys, vals, weight_ref, sems, sessions, session_sem = refs
        session_copy = pltpu.make_async_copy(session_ref, sessions, session_sem)
        session_copy.start()
    else:
        before_ref, keys, vals, sems = refs
    tokens, half = keys.shape
    cols = columns(place_ref, mine, half)
    copies = []
    for c in range(tokens // CHUNK):
        for j, (source, to) in enumerate(((key_ref, keys), (value_ref, vals))):
            copies.append(pltpu.make_async_copy(source.at[chunk(c), cols], to.at[chunk(c), :], sems.at[2 * c + j]))
            copies[-1].start()
    if planned:
        session_copy.wait()
        write_weights(place_ref, sessions, weight_ref)
    for c in range(tokens // CHUNK):
        copies[2 * c].wait()
        copies[2 * c + 1].wait()
        for h in range(half // HEAD_DIM):
            new = dot_tn(keys[chunk(c), head(h)], vals[chunk(c), head(h)])
            per = half // HEAD_DIM // groups
            state_ref, rows = state_refs[h // per], head(h % per)
            if c == 0:
                state_ref[rows, :] = new
            else:
                old = state_ref[rows, :]
                at = (c - 1) * half + h * HEAD_DIM
                before_ref[at : at + HEAD_DIM, :] = old.astype(BF16)
                state_ref[rows, :] = old + new


def half_states(place, key_rows, values, mine, groups, session_of=None):
    tokens, width = key_rows.shape
    half = width // 2
    chunks = tokens // CHUNK
    planned = session_of is not None
    out_shape = [pltpu.VMEM((half // groups, HEAD_DIM), F32)] * groups + [
        pltpu.VMEM(((chunks - 1) * half, HEAD_DIM), BF16),
        pltpu.VMEM((tokens, half), BF16),
        pltpu.VMEM((tokens, half), BF16),
    ]
    scratch_shapes = [pltpu.SemaphoreType.DMA((2 * chunks,))]
    operands = [place, in_hbm(key_rows), in_hbm(values)]
    if planned:
        out_shape += [pltpu.VMEM((8, HEAD_DIM), F32)]
        scratch_shapes += [pltpu.SMEM(session_of.shape, jnp.int32), pltpu.SemaphoreType.DMA(())]
        operands += [in_hbm(session_of)]
    results = pl.pallas_call(
        lambda *refs: states_kernel(mine, planned, groups, *refs),
        in_specs=[SCALARS] + [ANYWHERE] * (len(operands) - 1),
        out_specs=[WHOLE] * len(out_shape),
        out_shape=out_shape,
        scratch_shapes=scratch_shapes,
        compiler_params=params(24),
        cost_estimate=cost(tokens * width * HEAD_DIM, 2 * tokens * width),
        name="states",
    )(*operands)
    return results[:groups], results[groups:]


def write_weights(place_ref, session_ref, weight_ref):
    place = place_ref[0]
    core = place & 1
    chip = lax.shift_right_logical(place, 1)

    def flag(condition):
        return jnp.where(condition, 1.0, 0.0).astype(F32)

    def need(to, source):
        same = session_ref[2 * to] == session_ref[2 * source + 1]
        return flag(jnp.logical_and(source < to, same))

    even = core == 0
    partner = jnp.where(even, chip ^ 1, chip ^ 2)
    to = jnp.where(even, chip ^ 2, chip ^ 1)
    rows = [flag(even), flag(core == 1), need(to, chip), need(to, partner), need(chip, partner)]
    for r, value in enumerate(rows):
        weight_ref[r : r + 1, :] = jnp.full((1, HEAD_DIM), value, F32)


def half_heads(place_ref, mine, half):
    start = (place_ref[0] & 1 if mine else 1 - (place_ref[0] & 1)) * half
    return lambda h: pl.ds(pl.multiple_of(start + h * HEAD_DIM, HEAD_DIM), HEAD_DIM)


def inner_kernel(mine, place_ref, query_ref, key_ref, value_ref, before_ref, after_ref, inner_ref, zero_ref):
    tokens, half = key_ref.shape
    heads = range(half // HEAD_DIM)
    columns_of = half_heads(place_ref, mine, half)
    zero_ref[...] = jnp.zeros_like(zero_ref)
    rows_at = lax.broadcasted_iota(jnp.int32, (CHUNK, CHUNK), 0)
    cols_at = lax.broadcasted_iota(jnp.int32, (CHUNK, CHUNK), 1)
    causal = rows_at >= cols_at
    for c in range(tokens // CHUNK):
        scores = []
        for h in heads:
            full = dot_nt(query_ref[chunk(c), columns_of(h)], key_ref[chunk(c), head(h)])
            scores.append(jnp.where(causal, full, 0.0).astype(BF16))
        for h in heads:
            left, right = scores[h], value_ref[chunk(c), head(h)]
            if c > 0:
                at = (c - 1) * half + h * HEAD_DIM
                left = jnp.concatenate([left, query_ref[chunk(c), columns_of(h)]], axis=1)
                right = jnp.concatenate([right, before_ref[at : at + HEAD_DIM, :]], axis=0)
            inner_ref[chunk(c), head(h)] = dot_nn(left, right)


def half_inner(place, queries, half_of_heads, after, mine):
    before, keys, vals = half_of_heads[:3]
    tokens, half = keys.shape
    return pl.pallas_call(
        lambda *refs: inner_kernel(mine, *refs),
        in_specs=[SCALARS, WHOLE, WHOLE, WHOLE, WHOLE, ANYWHERE],
        out_specs=[WHOLE] * 2,
        out_shape=[pltpu.VMEM((tokens, half), F32), pltpu.VMEM((1, HEAD_DIM), F32)],
        compiler_params=params(24),
        cost_estimate=cost(tokens * half * 6 * CHUNK, 12 * tokens * half),
        name="inner",
    )(place, in_vmem(queries), in_vmem(keys), in_vmem(vals), in_vmem(before), after)


def mix_kernel(mine, heads, first, last, place_ref, query_ref, inner_ref, prefix_ref, *refs):
    extra_ref, mixed_ref, result_ref = (None, *refs) if first else refs
    tokens, half = inner_ref.shape
    columns_of = half_heads(place_ref, mine, half)
    blocks = [prefix_ref[head(h - heads[0]), :].astype(BF16) for h in heads]
    for c in range(tokens // CHUNK):
        squares = None if first else extra_ref[chunk(c), :]
        for h, block in zip(heads, blocks):
            mixed = inner_ref[chunk(c), head(h)] + dot_nn(query_ref[chunk(c), columns_of(h)], block)
            square = mixed * mixed
            squares = square if squares is None else squares + square
            mixed_ref[chunk(c), head(h)] = mixed
        if last:
            result_ref[:, chunk(c)] = jnp.sum(jnp.transpose(squares), axis=0, keepdims=True)
        else:
            result_ref[chunk(c), :] = squares


def mix(place, queries, inner, prefix, squares, mine, group, last):
    tokens, half = inner.shape
    count = prefix.shape[0] // HEAD_DIM
    heads = range(group * count, (group + 1) * count)
    first = squares is None
    operands = [queries, inner, prefix] + ([] if first else [squares])
    return pl.pallas_call(
        lambda *refs: mix_kernel(mine, heads, first, last, *refs),
        in_specs=[SCALARS] + [WHOLE] * len(operands),
        out_specs=[WHOLE, WHOLE],
        out_shape=[
            pltpu.VMEM((tokens, half), F32),
            pltpu.VMEM((1, tokens) if last else (tokens, HEAD_DIM), F32),
        ],
        input_output_aliases={2: 0},
        compiler_params=params(24),
        cost_estimate=cost(2 * tokens * prefix.size, 2 * tokens * half),
        name="mix",
    )(place, *[in_vmem(x) for x in operands])


def gate_kernel(mine, place_ref, mixed_ref, gate_ref, gain_ref, after_ref, gated_ref, zero_ref):
    tokens, half = mixed_ref.shape
    zero_ref[...] = jnp.zeros_like(zero_ref)
    rows = HEAD_DIM
    columns_of = half_heads(place_ref, mine, half)

    def step(i, carry):
        at = pl.ds(pl.multiple_of(i * rows, rows), rows)
        for h in range(half // HEAD_DIM):
            gate = gate_ref[at, columns_of(h)].astype(F32)
            factor = (0.5 * gain_ref[:, columns_of(h)]) * (1.0 + jnp.tanh(0.5 * gate))
            gated_ref[at, head(h)] = mixed_ref[at, head(h)] * factor
        return carry

    lax.fori_loop(0, tokens // rows, step, 0)


def gated(place, mixed, gate_input, norm_gain, after, mine):
    tokens, width = gate_input.shape
    return pl.pallas_call(
        lambda *refs: gate_kernel(mine, *refs),
        in_specs=[SCALARS, WHOLE, WHOLE, WHOLE, ANYWHERE],
        out_specs=[WHOLE, WHOLE],
        out_shape=[pltpu.VMEM(mixed.shape, F32), pltpu.VMEM((1, tokens), F32)],
        input_output_aliases={1: 0},
        compiler_params=params(24),
        cost_estimate=cost(16 * mixed.size, 4 * mixed.size),
        name="gate",
    )(place, in_vmem(mixed), in_vmem(gate_input), norm_gain.reshape(1, width), after)


def scale_kernel(features, place_ref, mine_ref, other_ref, power_ref, out_ref, mine_out, other_out, sems):
    tokens, half = mine_ref.shape
    rows = HEAD_DIM
    copies = []
    for c in range(tokens // rows):
        at = slice(c * rows, (c + 1) * rows)
        power = jnp.broadcast_to(power_ref[:, at], (HEAD_DIM, rows))
        factor = lax.rsqrt(jnp.transpose(power) / features + 1e-06)
        for j, (source, to) in enumerate(((mine_ref, mine_out), (other_ref, other_out))):
            for h in range(half // HEAD_DIM):
                to[at, head(h)] = (source[at, head(h)] * factor).astype(BF16)
            cols = columns(place_ref, j == 0, half)
            copies.append(pltpu.make_async_copy(to.at[at, :], out_ref.at[at, cols], sems.at[2 * c + j]))
            copies[-1].start()
    for copy in copies:
        copy.wait()


def scale(place, mine, other, power, features):
    tokens, half = mine.shape
    return pl.pallas_call(
        lambda *refs: scale_kernel(features, *refs),
        in_specs=[SCALARS, WHOLE, WHOLE, WHOLE],
        out_specs=ANYWHERE,
        out_shape=pltpu.HBM((tokens, 2 * half), BF16),
        scratch_shapes=[
            pltpu.VMEM((tokens, half), BF16),
            pltpu.VMEM((tokens, half), BF16),
            pltpu.SemaphoreType.DMA((2 * tokens // HEAD_DIM,)),
        ],
        compiler_params=params(24),
        cost_estimate=cost(4 * tokens * half, 4 * tokens * half),
        name="scale",
    )(place, in_vmem(mine), in_vmem(other), in_vmem(power))


def swap(count, bit):
    return [(i, i ^ bit) for i in range(count)]


def general_prefix(blocks, chip, session_of, chip_sum):
    total = chip_sum
    prefix = jnp.zeros_like(chip_sum)
    bit = 1
    while 2 * bit < blocks:
        there = lax.ppermute(total, "ctx", swap(blocks, 2 * bit))
        partner = chip ^ bit
        lower = partner < chip
        end_here = session_of[2 * (chip | (bit - 1)) + 1]
        end_there = session_of[2 * (partner | (bit - 1)) + 1]
        reaches = jnp.logical_and(lower, end_there == session_of[2 * chip])
        prefix = prefix + jnp.where(reaches, 1.0, 0.0) * there
        joined = jnp.where(end_here == end_there, 1.0, 0.0)
        total = jnp.where(lower, total + joined * there, joined * total + there)
        bit *= 2
    return prefix


def zero_after(x):
    def kernel(after_ref, zero_ref):
        zero_ref[...] = jnp.zeros_like(zero_ref)

    return pl.pallas_call(
        kernel,
        in_specs=[ANYWHERE],
        out_specs=WHOLE,
        out_shape=pltpu.VMEM((1, HEAD_DIM), F32),
        compiler_params=params(1),
        name="then",
    )(x)


def two_steps(sums, weight, between, beside):
    there = [lax.ppermute(x, "ctx", [(i, i ^ (2 if i % 2 == 0 else 4)) for i in range(8)]) for x in sums]
    zero = between(sums[0])
    onward = []
    for x, y in zip(sums, there):
        onward.append(weight[2:3] * x + weight[3:4] * y + zero)
        zero = zero_after(onward[-1])
    arrived = [lax.ppermute(x, "ctx", [(i, i ^ (4 if i % 2 == 0 else 2)) for i in range(8)]) for x in onward]
    zero = beside(onward[-1])
    prefixes = []
    for x, y in zip(there, arrived):
        prefixes.append(weight[4:5] * x + y + zero)
        zero = zero_after(prefixes[-1])
    return prefixes


def on_device(blocks, features, queries, key_rows, values, gate_input, norm_gain, session_of):
    width = queries.shape[1]
    index = lax.axis_index("ctx").astype(jnp.int32)
    place = index.reshape(1)
    group_rows = width // 2 // GROUPS

    (sent,), sent_half = half_states(place, key_rows, values, False, 1, session_of if blocks == 8 else None)
    got = lax.ppermute(sent, "ctx", swap(blocks, 1))
    kept, kept_half = half_states(place, key_rows, values, True, GROUPS)
    got = [got[g * group_rows : (g + 1) * group_rows] for g in range(GROUPS)]
    sums = [x + y for x, y in zip(kept, got)]
    inner = {}

    def inner_of(half, mine):
        def run(after):
            inner[mine], zero = half_inner(place, queries, half, after, mine)
            return zero

        return run

    if blocks == 8:
        weight = sent_half[3]
        prefixes = two_steps(sums, weight, inner_of(kept_half, True), inner_of(sent_half, False))
        even, odd = weight[0:1], weight[1:2]
    else:
        zero = inner_of(kept_half, True)(sums[0]) + inner_of(sent_half, False)(sums[0])
        prefixes = [general_prefix(blocks, index >> 1, session_of, x) + zero for x in sums]
        odd = (index & 1).astype(F32)
        even = 1.0 - odd

    squares = None
    for g, prefix in enumerate(prefixes):
        other = lax.ppermute(prefix + even * kept[g], "ctx", swap(blocks, 1))
        inner[True], squares = mix(place, queries, inner[True], prefix + odd * got[g], squares, True, g, False)
        inner[False], squares = mix(place, queries, inner[False], other, squares, False, g, g == GROUPS - 1)
    power = squares
    gated_other, zero = gated(place, inner[False], gate_input, norm_gain, power, False)
    power = power + lax.ppermute(power, "head", swap(features // width, 1)) + zero
    gated_mine, zero = gated(place, inner[True], gate_input, norm_gain, power, True)
    bit = 2
    while bit < features // width:
        power = power + lax.ppermute(power, "head", swap(features // width, bit))
        bit *= 2
    return scale(place, gated_mine, gated_other, power + zero, features)


def solution(mesh):
    blocks = mesh.shape["ctx"]

    def whole(queries, key_rows, values, gate_input, norm_gain, session_of):
        features = queries.shape[1]
        return jax.shard_map(
            lambda *args: on_device(blocks, features, *args),
            mesh=mesh,
            in_specs=(
                P("ctx", "head"),
                P("ctx", "head"),
                P("ctx", "head"),
                P("ctx", "head"),
                P("head"),
                P(),
            ),
            out_specs=P("ctx", "head"),
            check_vma=False,
        )(queries, key_rows, values, gate_input, norm_gain, session_of)

    return whole
```

```python
import jax
import jax.numpy as jnp
from jax import lax
from jax.experimental import pallas as pl
from jax.experimental.pallas import tpu as pltpu
from jax.sharding import PartitionSpec as P

HEAD_DIM = 128
CHUNK = 256
GROUPS = 2
MIB = 1024 * 1024
F32 = jnp.float32
BF16 = jnp.bfloat16
WHOLE = pl.BlockSpec(memory_space=pltpu.VMEM)
SCALARS = pl.BlockSpec(memory_space=pltpu.SMEM)
ANYWHERE = pl.BlockSpec(memory_space=pl.ANY)


def params(mib):
    return pltpu.CompilerParams(vmem_limit_bytes=mib * MIB)


def in_hbm(x):
    return pltpu.with_memory_space_constraint(x, pltpu.HBM)


def in_vmem(x):
    return pltpu.with_memory_space_constraint(x, pltpu.VMEM)


def cost(flops, bytes_accessed):
    return pl.CostEstimate(flops=flops, bytes_accessed=bytes_accessed, transcendentals=0)


def dot_tn(a, b):
    return lax.dot_general(a, b, (((0,), (0,)), ((), ())), preferred_element_type=F32)


def dot_nt(a, b):
    return lax.dot_general(a, b, (((1,), (1,)), ((), ())), preferred_element_type=F32)


def dot_nn(a, b):
    return lax.dot_general(a, b, (((1,), (0,)), ((), ())), preferred_element_type=F32)


def head(h):
    return slice(h * HEAD_DIM, (h + 1) * HEAD_DIM)


def chunk(c):
    return slice(c * CHUNK, (c + 1) * CHUNK)


def columns(place_ref, mine, half):
    core = place_ref[0] & 1
    return pl.ds(pl.multiple_of((core if mine else 1 - core) * half, half), half)


def states_kernel(mine, planned, groups, place_ref, key_ref, value_ref, *refs):
    if planned:
        session_ref, *refs = refs
    state_refs, refs = refs[:groups], refs[groups:]
    if planned:
        before_ref, keys, vals, weight_ref, sems, sessions, session_sem = refs
        session_copy = pltpu.make_async_copy(session_ref, sessions, session_sem)
        session_copy.start()
    else:
        before_ref, keys, vals, sems = refs
    tokens, half = keys.shape
    cols = columns(place_ref, mine, half)
    copies = []
    for c in range(tokens // CHUNK):
        for j, (source, to) in enumerate(((key_ref, keys), (value_ref, vals))):
            copies.append(pltpu.make_async_copy(source.at[chunk(c), cols], to.at[chunk(c), :], sems.at[2 * c + j]))
            copies[-1].start()
    if planned:
        session_copy.wait()
        write_weights(place_ref, sessions, weight_ref)
    for c in range(tokens // CHUNK):
        copies[2 * c].wait()
        copies[2 * c + 1].wait()
        for h in range(half // HEAD_DIM):
            new = dot_tn(keys[chunk(c), head(h)], vals[chunk(c), head(h)])
            per = half // HEAD_DIM // groups
            state_ref, rows = state_refs[h // per], head(h % per)
            if c == 0:
                state_ref[rows, :] = new
            else:
                old = state_ref[rows, :]
                at = (c - 1) * half + h * HEAD_DIM
                before_ref[at : at + HEAD_DIM, :] = old.astype(BF16)
                state_ref[rows, :] = old + new


def half_states(place, key_rows, values, mine, groups, session_of=None):
    tokens, width = key_rows.shape
    half = width // 2
    chunks = tokens // CHUNK
    planned = session_of is not None
    out_shape = [pltpu.VMEM((half // groups, HEAD_DIM), F32)] * groups + [
        pltpu.VMEM(((chunks - 1) * half, HEAD_DIM), BF16),
        pltpu.VMEM((tokens, half), BF16),
        pltpu.VMEM((tokens, half), BF16),
    ]
    scratch_shapes = [pltpu.SemaphoreType.DMA((2 * chunks,))]
    operands = [place, in_hbm(key_rows), in_hbm(values)]
    if planned:
        out_shape += [pltpu.VMEM((8, HEAD_DIM), F32)]
        scratch_shapes += [pltpu.SMEM(session_of.shape, jnp.int32), pltpu.SemaphoreType.DMA(())]
        operands += [in_hbm(session_of)]
    results = pl.pallas_call(
        lambda *refs: states_kernel(mine, planned, groups, *refs),
        in_specs=[SCALARS] + [ANYWHERE] * (len(operands) - 1),
        out_specs=[WHOLE] * len(out_shape),
        out_shape=out_shape,
        scratch_shapes=scratch_shapes,
        compiler_params=params(8),
        cost_estimate=cost(tokens * width * HEAD_DIM, 2 * tokens * width),
        name="states",
    )(*operands)
    return results[:groups], results[groups:]


def write_weights(place_ref, session_ref, weight_ref):
    place = place_ref[0]
    core = place & 1
    chip = lax.shift_right_logical(place, 1)

    def flag(condition):
        return jnp.where(condition, 1.0, 0.0).astype(F32)

    def need(to, source):
        same = session_ref[2 * to] == session_ref[2 * source + 1]
        return flag(jnp.logical_and(source < to, same))

    even = core == 0
    partner = jnp.where(even, chip ^ 1, chip ^ 2)
    to = jnp.where(even, chip ^ 2, chip ^ 1)
    rows = [flag(even), flag(core == 1), need(to, chip), need(to, partner), need(chip, partner)]
    for r, value in enumerate(rows):
        weight_ref[r : r + 1, :] = jnp.full((1, HEAD_DIM), value, F32)


def half_heads(place_ref, mine, half):
    start = (place_ref[0] & 1 if mine else 1 - (place_ref[0] & 1)) * half
    return lambda h: pl.ds(pl.multiple_of(start + h * HEAD_DIM, HEAD_DIM), HEAD_DIM)


def inner_kernel(mine, place_ref, query_ref, key_ref, value_ref, before_ref, after_ref, inner_ref, zero_ref):
    tokens, half = key_ref.shape
    heads = range(half // HEAD_DIM)
    columns_of = half_heads(place_ref, mine, half)
    zero_ref[...] = jnp.zeros_like(zero_ref)
    rows_at = lax.broadcasted_iota(jnp.int32, (CHUNK, CHUNK), 0)
    cols_at = lax.broadcasted_iota(jnp.int32, (CHUNK, CHUNK), 1)
    causal = rows_at >= cols_at
    for c in range(tokens // CHUNK):
        scores = []
        for h in heads:
            full = dot_nt(query_ref[chunk(c), columns_of(h)], key_ref[chunk(c), head(h)])
            scores.append(jnp.where(causal, full, 0.0).astype(BF16))
        for h in heads:
            left, right = scores[h], value_ref[chunk(c), head(h)]
            if c > 0:
                at = (c - 1) * half + h * HEAD_DIM
                left = jnp.concatenate([left, query_ref[chunk(c), columns_of(h)]], axis=1)
                right = jnp.concatenate([right, before_ref[at : at + HEAD_DIM, :]], axis=0)
            inner_ref[chunk(c), head(h)] = dot_nn(left, right)


def half_inner(place, queries, half_of_heads, after, mine):
    before, keys, vals = half_of_heads[:3]
    tokens, half = keys.shape
    return pl.pallas_call(
        lambda *refs: inner_kernel(mine, *refs),
        in_specs=[SCALARS, WHOLE, WHOLE, WHOLE, WHOLE, ANYWHERE],
        out_specs=[WHOLE] * 2,
        out_shape=[pltpu.VMEM((tokens, half), F32), pltpu.VMEM((1, HEAD_DIM), F32)],
        compiler_params=params(8),
        cost_estimate=cost(tokens * half * 6 * CHUNK, 12 * tokens * half),
        name="inner",
    )(place, in_vmem(queries), in_vmem(keys), in_vmem(vals), in_vmem(before), after)


def mix_kernel(mine, heads, first, last, place_ref, query_ref, inner_ref, prefix_ref, *refs):
    extra_ref, mixed_ref, result_ref = (None, *refs) if first else refs
    tokens, half = inner_ref.shape
    columns_of = half_heads(place_ref, mine, half)
    blocks = [prefix_ref[head(j), :].astype(BF16) for j in range(len(heads))]
    for c in range(tokens // CHUNK):
        squares = None if first else extra_ref[chunk(c), :]
        for j, h in enumerate(heads):
            mixed = inner_ref[chunk(c), head(h)] + dot_nn(query_ref[chunk(c), columns_of(h)], blocks[j])
            square = mixed * mixed
            squares = square if squares is None else squares + square
            mixed_ref[chunk(c), head(j)] = mixed
        if last:
            result_ref[:, chunk(c)] = jnp.sum(jnp.transpose(squares), axis=0, keepdims=True)
        else:
            result_ref[chunk(c), :] = squares


def mix(place, queries, inner, prefix, squares, mine, group, last):
    tokens, half = inner.shape
    count = prefix.shape[0] // HEAD_DIM
    heads = range(group * count, (group + 1) * count)
    first = squares is None
    operands = [queries, inner, prefix] + ([] if first else [squares])
    return pl.pallas_call(
        lambda *refs: mix_kernel(mine, heads, first, last, *refs),
        in_specs=[SCALARS] + [WHOLE] * len(operands),
        out_specs=[WHOLE, WHOLE],
        out_shape=[
            pltpu.VMEM((tokens, count * HEAD_DIM), F32),
            pltpu.VMEM((1, tokens) if last else (tokens, HEAD_DIM), F32),
        ],
        compiler_params=params(8),
        cost_estimate=cost(2 * tokens * prefix.size, 2 * tokens * half),
        name="mix",
    )(place, *[in_vmem(x) for x in operands])


def gate_kernel(mine, place_ref, gate_ref, gain_ref, after_ref, *refs):
    *mixed_refs, gated_ref, zero_ref = refs
    tokens, half = gated_ref.shape
    zero_ref[...] = jnp.zeros_like(zero_ref)
    rows = HEAD_DIM
    columns_of = half_heads(place_ref, mine, half)
    per = half // HEAD_DIM // len(mixed_refs)

    def step(i, carry):
        at = pl.ds(pl.multiple_of(i * rows, rows), rows)
        for h in range(half // HEAD_DIM):
            gate = gate_ref[at, columns_of(h)].astype(F32)
            factor = (0.5 * gain_ref[:, columns_of(h)]) * (1.0 + jnp.tanh(0.5 * gate))
            gated_ref[at, head(h)] = mixed_refs[h // per][at, head(h % per)] * factor
        return carry

    lax.fori_loop(0, tokens // rows, step, 0)


def gated(place, mixed, gate_input, norm_gain, after, mine):
    tokens, width = gate_input.shape
    return pl.pallas_call(
        lambda *refs: gate_kernel(mine, *refs),
        in_specs=[SCALARS, WHOLE, WHOLE, ANYWHERE] + [WHOLE] * len(mixed),
        out_specs=[WHOLE, WHOLE],
        out_shape=[pltpu.VMEM((tokens, width // 2), F32), pltpu.VMEM((1, tokens), F32)],
        compiler_params=params(8),
        cost_estimate=cost(8 * tokens * width, 2 * tokens * width),
        name="gate",
    )(place, in_vmem(gate_input), norm_gain.reshape(1, width), after, *[in_vmem(x) for x in mixed])


def scale_kernel(features, place_ref, mine_ref, other_ref, power_ref, out_ref, mine_out, other_out, sems):
    tokens, half = mine_ref.shape
    rows = HEAD_DIM
    copies = []
    for c in range(tokens // rows):
        at = slice(c * rows, (c + 1) * rows)
        power = jnp.broadcast_to(power_ref[:, at], (HEAD_DIM, rows))
        factor = lax.rsqrt(jnp.transpose(power) / features + 1e-06)
        for j, (source, to) in enumerate(((mine_ref, mine_out), (other_ref, other_out))):
            for h in range(half // HEAD_DIM):
                to[at, head(h)] = (source[at, head(h)] * factor).astype(BF16)
            cols = columns(place_ref, j == 0, half)
            copies.append(pltpu.make_async_copy(to.at[at, :], out_ref.at[at, cols], sems.at[2 * c + j]))
            copies[-1].start()
    for copy in copies:
        copy.wait()


def scale(place, mine, other, power, features):
    tokens, half = mine.shape
    return pl.pallas_call(
        lambda *refs: scale_kernel(features, *refs),
        in_specs=[SCALARS, WHOLE, WHOLE, WHOLE],
        out_specs=ANYWHERE,
        out_shape=pltpu.HBM((tokens, 2 * half), BF16),
        scratch_shapes=[
            pltpu.VMEM((tokens, half), BF16),
            pltpu.VMEM((tokens, half), BF16),
            pltpu.SemaphoreType.DMA((2 * tokens // HEAD_DIM,)),
        ],
        compiler_params=params(8),
        cost_estimate=cost(4 * tokens * half, 4 * tokens * half),
        name="scale",
    )(place, in_vmem(mine), in_vmem(other), in_vmem(power))


def swap(count, bit):
    return [(i, i ^ bit) for i in range(count)]


def general_prefix(blocks, chip, session_of, chip_sum):
    total = chip_sum
    prefix = jnp.zeros_like(chip_sum)
    bit = 1
    while 2 * bit < blocks:
        there = lax.ppermute(total, "ctx", swap(blocks, 2 * bit))
        partner = chip ^ bit
        lower = partner < chip
        end_here = session_of[2 * (chip | (bit - 1)) + 1]
        end_there = session_of[2 * (partner | (bit - 1)) + 1]
        reaches = jnp.logical_and(lower, end_there == session_of[2 * chip])
        prefix = prefix + jnp.where(reaches, 1.0, 0.0) * there
        joined = jnp.where(end_here == end_there, 1.0, 0.0)
        total = jnp.where(lower, total + joined * there, joined * total + there)
        bit *= 2
    return prefix


def zero_after(x):
    def kernel(after_ref, zero_ref):
        zero_ref[...] = jnp.zeros_like(zero_ref)

    return pl.pallas_call(
        kernel,
        in_specs=[ANYWHERE],
        out_specs=WHOLE,
        out_shape=pltpu.VMEM((1, HEAD_DIM), F32),
        compiler_params=params(1),
        name="then",
    )(x)


def two_steps(sums, weight, between, beside):
    there = [lax.ppermute(x, "ctx", [(i, i ^ (2 if i % 2 == 0 else 4)) for i in range(8)]) for x in sums]
    zero = between(sums[0])
    onward = []
    for x, y in zip(sums, there):
        onward.append(weight[2:3] * x + weight[3:4] * y + zero)
        zero = zero_after(onward[-1])
    arrived = [lax.ppermute(x, "ctx", [(i, i ^ (4 if i % 2 == 0 else 2)) for i in range(8)]) for x in onward]
    zero = beside(onward[-1])
    return [weight[4:5] * x + y + zero for x, y in zip(there, arrived)]


def on_device(blocks, features, queries, key_rows, values, gate_input, norm_gain, session_of):
    width = queries.shape[1]
    index = lax.axis_index("ctx").astype(jnp.int32)
    place = index.reshape(1)
    group_rows = width // 2 // GROUPS

    (sent,), sent_half = half_states(place, key_rows, values, False, 1, session_of if blocks == 8 else None)
    got = lax.ppermute(sent, "ctx", swap(blocks, 1))
    kept, kept_half = half_states(place, key_rows, values, True, GROUPS)
    got = [got[g * group_rows : (g + 1) * group_rows] for g in range(GROUPS)]
    sums = [x + y for x, y in zip(kept, got)]
    inner = {}

    def inner_of(half, mine):
        def run(after):
            inner[mine], zero = half_inner(place, queries, half, after, mine)
            return zero

        return run

    if blocks == 8:
        weight = sent_half[3]
        prefixes = two_steps(sums, weight, inner_of(kept_half, True), inner_of(sent_half, False))
        even, odd = weight[0:1], weight[1:2]
    else:
        zero = inner_of(kept_half, True)(sums[0]) + inner_of(sent_half, False)(sums[0])
        prefixes = [general_prefix(blocks, index >> 1, session_of, x) + zero for x in sums]
        odd = (index & 1).astype(F32)
        even = 1.0 - odd

    mixed = {True: [], False: []}
    squares = None
    zero = jnp.zeros((1, HEAD_DIM), F32)
    for g, prefix in enumerate(prefixes):
        prefix = prefix + zero
        other = lax.ppermute(prefix + even * kept[g], "ctx", swap(blocks, 1))
        part, squares = mix(place, queries, inner[True], prefix + odd * got[g], squares, True, g, False)
        mixed[True].append(part)
        zero = zero_after(squares)
        part, squares = mix(place, queries, inner[False], other, squares, False, g, g == GROUPS - 1)
        mixed[False].append(part)
    power = squares
    gated_other, zero = gated(place, mixed[False], gate_input, norm_gain, power, False)
    power = power + lax.ppermute(power, "head", swap(features // width, 1)) + zero
    gated_mine, zero = gated(place, mixed[True], gate_input, norm_gain, power, True)
    bit = 2
    while bit < features // width:
        power = power + lax.ppermute(power, "head", swap(features // width, bit))
        bit *= 2
    return scale(place, gated_mine, gated_other, power + zero, features)


def solution(mesh):
    blocks = mesh.shape["ctx"]

    def whole(queries, key_rows, values, gate_input, norm_gain, session_of):
        features = queries.shape[1]
        return jax.shard_map(
            lambda *args: on_device(blocks, features, *args),
            mesh=mesh,
            in_specs=(
                P("ctx", "head"),
                P("ctx", "head"),
                P("ctx", "head"),
                P("ctx", "head"),
                P("head"),
                P(),
            ),
            out_specs=P("ctx", "head"),
            check_vma=False,
        )(queries, key_rows, values, gate_input, norm_gain, session_of)

    return whole
```

```python
import jax
import jax.numpy as jnp
from jax import lax
from jax.experimental import pallas as pl
from jax.experimental.pallas import tpu as pltpu
from jax.sharding import PartitionSpec as P

HEAD_DIM = 128
CHUNK = 256
GROUPS = 2
MIB = 1024 * 1024
F32 = jnp.float32
BF16 = jnp.bfloat16
WHOLE = pl.BlockSpec(memory_space=pltpu.VMEM)
SCALARS = pl.BlockSpec(memory_space=pltpu.SMEM)
ANYWHERE = pl.BlockSpec(memory_space=pl.ANY)


def params(mib):
    return pltpu.CompilerParams(vmem_limit_bytes=mib * MIB)


def in_hbm(x):
    return pltpu.with_memory_space_constraint(x, pltpu.HBM)


def in_vmem(x):
    return pltpu.with_memory_space_constraint(x, pltpu.VMEM)


def cost(flops, bytes_accessed):
    return pl.CostEstimate(flops=flops, bytes_accessed=bytes_accessed, transcendentals=0)


def dot_tn(a, b):
    return lax.dot_general(a, b, (((0,), (0,)), ((), ())), preferred_element_type=F32)


def dot_nt(a, b):
    return lax.dot_general(a, b, (((1,), (1,)), ((), ())), preferred_element_type=F32)


def dot_nn(a, b):
    return lax.dot_general(a, b, (((1,), (0,)), ((), ())), preferred_element_type=F32)


def head(h):
    return slice(h * HEAD_DIM, (h + 1) * HEAD_DIM)


def chunk(c):
    return slice(c * CHUNK, (c + 1) * CHUNK)


def columns(place_ref, mine, half):
    core = place_ref[0] & 1
    return pl.ds(pl.multiple_of((core if mine else 1 - core) * half, half), half)


def group_sizes(heads):
    return [(heads + GROUPS - 1 - g) // GROUPS for g in range(GROUPS)]


def fetch(copies, sems, place_ref, mine, pairs, chunks, base=0):
    for c in chunks:
        for source, to in pairs:
            cols = columns(place_ref, mine, to.shape[1])
            rows = slice((c - base) * CHUNK, (c - base + 1) * CHUNK)
            copies.append(pltpu.make_async_copy(source.at[chunk(c), cols], to.at[rows, :], sems.at[len(copies)]))
            copies[-1].start()


def add_chunk(c, keys, vals, rows, state_refs, before_ref):
    half = keys.shape[1]
    h = 0
    for state_ref in state_refs:
        for j in range(state_ref.shape[0] // HEAD_DIM):
            new = dot_tn(keys[rows, head(h)], vals[rows, head(h)])
            if c == 0:
                state_ref[head(j), :] = new
            else:
                old = state_ref[head(j), :]
                at = (c - 1) * half + h * HEAD_DIM
                before_ref[at : at + HEAD_DIM, :] = old.astype(BF16)
                state_ref[head(j), :] = old + new
            h += 1


def sent_kernel(place_ref, session_ref, key_ref, value_ref, state_ref, before_ref, keys, vals,
                next_keys, next_vals, weight_ref, sems, sessions, session_sem):
    chunks = keys.shape[0] // CHUNK
    early = next_keys.shape[0] // CHUNK
    session_copy = pltpu.make_async_copy(session_ref, sessions, session_sem)
    session_copy.start()
    copies = []
    fetch(copies, sems, place_ref, False, ((key_ref, keys), (value_ref, vals)), range(chunks))
    fetch(copies, sems, place_ref, True, ((key_ref, next_keys), (value_ref, next_vals)), range(early))
    session_copy.wait()
    write_weights(place_ref, sessions, weight_ref)
    for c in range(chunks):
        copies[2 * c].wait()
        copies[2 * c + 1].wait()
        add_chunk(c, keys, vals, chunk(c), [state_ref], before_ref)
    for copy in copies[2 * chunks :]:
        copy.wait()


def sent_states(place, session_of, key_rows, values):
    tokens, width = key_rows.shape
    half = width // 2
    chunks = tokens // CHUNK
    early = chunks // 2
    return pl.pallas_call(
        sent_kernel,
        in_specs=[SCALARS] + [ANYWHERE] * 3,
        out_specs=[WHOLE] * 7,
        out_shape=[
            pltpu.VMEM((half, HEAD_DIM), F32),
            pltpu.VMEM(((chunks - 1) * half, HEAD_DIM), BF16),
            pltpu.VMEM((tokens, half), BF16),
            pltpu.VMEM((tokens, half), BF16),
            pltpu.VMEM((early * CHUNK, half), BF16),
            pltpu.VMEM((early * CHUNK, half), BF16),
            pltpu.VMEM((8, HEAD_DIM), F32),
        ],
        scratch_shapes=[
            pltpu.SemaphoreType.DMA((2 * chunks + 2 * early,)),
            pltpu.SMEM(session_of.shape, jnp.int32),
            pltpu.SemaphoreType.DMA(()),
        ],
        compiler_params=params(8),
        cost_estimate=cost(tokens * width * HEAD_DIM, 3 * tokens * width),
        name="states",
    )(place, in_hbm(session_of), in_hbm(key_rows), in_hbm(values))


def kept_kernel(place_ref, key_ref, value_ref, query_ref, first_keys, first_vals, *refs):
    *state_refs, before_ref, keys, vals, queries, sems = refs
    early = first_keys.shape[0] // CHUNK
    chunks = early + keys.shape[0] // CHUNK
    copies = []
    fetch(copies, sems, place_ref, True, ((key_ref, keys), (value_ref, vals)), range(early, chunks), early)
    fetch(copies, sems, place_ref, True, ((query_ref, queries),), range(early))
    for c in range(early):
        add_chunk(c, first_keys, first_vals, chunk(c), state_refs, before_ref)
    for c in range(early, chunks):
        copies[2 * (c - early)].wait()
        copies[2 * (c - early) + 1].wait()
        add_chunk(c, keys, vals, chunk(c - early), state_refs, before_ref)
    for copy in copies[2 * (chunks - early) :]:
        copy.wait()


def kept_states(place, key_rows, values, queries, first_keys, first_vals):
    tokens, width = key_rows.shape
    half = width // 2
    chunks = tokens // CHUNK
    late = tokens - first_keys.shape[0]
    sizes = group_sizes(half // HEAD_DIM)
    out_shape = [pltpu.VMEM((n * HEAD_DIM, HEAD_DIM), F32) for n in sizes] + [
        pltpu.VMEM(((chunks - 1) * half, HEAD_DIM), BF16),
        pltpu.VMEM((late, half), BF16),
        pltpu.VMEM((late, half), BF16),
        pltpu.VMEM((tokens - late, half), BF16),
    ]
    results = pl.pallas_call(
        kept_kernel,
        in_specs=[SCALARS] + [ANYWHERE] * 3 + [WHOLE] * 2,
        out_specs=[WHOLE] * len(out_shape),
        out_shape=out_shape,
        scratch_shapes=[pltpu.SemaphoreType.DMA((chunks + late // CHUNK,))],
        compiler_params=params(8),
        cost_estimate=cost(tokens * width * HEAD_DIM, tokens * width),
        name="states",
    )(place, in_hbm(key_rows), in_hbm(values), in_hbm(queries), in_vmem(first_keys), in_vmem(first_vals))
    return results[: len(sizes)], results[len(sizes) :]


def write_weights(place_ref, session_ref, weight_ref):
    place = place_ref[0]
    core = place & 1
    chip = lax.shift_right_logical(place, 1)

    def flag(condition):
        return jnp.where(condition, 1.0, 0.0).astype(F32)

    def need(to, source):
        same = session_ref[2 * to] == session_ref[2 * source + 1]
        return flag(jnp.logical_and(source < to, same))

    even = core == 0
    rows = [flag(even), flag(core == 1)]
    if session_ref.shape[0] == 8:
        partner = jnp.where(even, chip ^ 1, chip ^ 2)
        to = jnp.where(even, chip ^ 2, chip ^ 1)
        rows += [need(to, chip), need(to, partner), need(chip, partner)]
    for r, value in enumerate(rows):
        weight_ref[r : r + 1, :] = jnp.full((1, HEAD_DIM), value, F32)


def half_heads(place_ref, mine, half):
    start = (place_ref[0] & 1 if mine else 1 - (place_ref[0] & 1)) * half
    return lambda h: pl.ds(pl.multiple_of(start + h * HEAD_DIM, HEAD_DIM), HEAD_DIM)


def chunk_in(refs, c):
    for ref in refs:
        chunks = ref.shape[0] // CHUNK
        if c < chunks:
            return ref, chunk(c)
        c -= chunks


def inner_body(chunks, waits, query_refs, key_refs, value_refs, before_ref, inner_refs, zero_ref):
    zero_ref[...] = jnp.zeros_like(zero_ref)
    rows_at = lax.broadcasted_iota(jnp.int32, (CHUNK, CHUNK), 0)
    cols_at = lax.broadcasted_iota(jnp.int32, (CHUNK, CHUNK), 1)
    causal = rows_at >= cols_at
    homes = [(ref, j) for ref in inner_refs for j in range(ref.shape[1] // HEAD_DIM)]
    half = len(homes) * HEAD_DIM
    for c in range(chunks):
        if c in waits:
            waits[c].wait()
        (query_ref, q), (key_ref, k), (value_ref, v) = (chunk_in(x, c) for x in (query_refs, key_refs, value_refs))
        scores = []
        for h in range(len(homes)):
            full = dot_nt(query_ref[q, head(h)], key_ref[k, head(h)])
            scores.append(jnp.where(causal, full, 0.0).astype(BF16))
        for h, (inner_ref, j) in enumerate(homes):
            left, right = scores[h], value_ref[v, head(h)]
            if c > 0:
                at = (c - 1) * half + h * HEAD_DIM
                left = jnp.concatenate([left, query_ref[q, head(h)]], axis=1)
                right = jnp.concatenate([right, before_ref[at : at + HEAD_DIM, :]], axis=0)
            inner_ref[chunk(c), head(j)] = dot_nn(left, right)


def mine_kernel(place_ref, query_ref, after_ref, first_queries, key_first, key_late, value_first, value_late,
                before_ref, late_queries, other_queries, *refs):
    *inner_refs, zero_ref, sems = refs
    chunks = other_queries.shape[0] // CHUNK
    early = first_queries.shape[0] // CHUNK
    copies = []
    fetch(copies, sems, place_ref, True, ((query_ref, late_queries),), range(early, chunks), early)
    fetch(copies, sems, place_ref, False, ((query_ref, other_queries),), range(chunks))
    waits = {c: copies[c - early] for c in range(early, chunks)}
    inner_body(
        chunks, waits, (first_queries, late_queries), (key_first, key_late), (value_first, value_late),
        before_ref, inner_refs, zero_ref,
    )
    for copy in copies[chunks - early :]:
        copy.wait()


def mine_inner(place, queries, first_queries, keys, vals, before, after, sizes):
    tokens, width = queries.shape
    half = width // 2
    late = tokens - first_queries.shape[0]
    out_shape = [pltpu.VMEM((late, half), BF16), pltpu.VMEM((tokens, half), BF16)]
    out_shape += [pltpu.VMEM((tokens, n * HEAD_DIM), F32) for n in sizes] + [pltpu.VMEM((1, HEAD_DIM), F32)]
    return pl.pallas_call(
        mine_kernel,
        in_specs=[SCALARS, ANYWHERE, ANYWHERE] + [WHOLE] * 6,
        out_specs=[WHOLE] * len(out_shape),
        out_shape=out_shape,
        scratch_shapes=[pltpu.SemaphoreType.DMA(((late + tokens) // CHUNK,))],
        compiler_params=params(8),
        cost_estimate=cost(tokens * half * 6 * CHUNK, 12 * tokens * half),
        name="inner",
    )(place, in_hbm(queries), after, *[in_vmem(x) for x in (first_queries, *keys, *vals, before)])


def other_kernel(after_ref, query_ref, key_ref, value_ref, before_ref, *refs):
    *inner_refs, zero_ref = refs
    chunks = query_ref.shape[0] // CHUNK
    inner_body(chunks, {}, (query_ref,), (key_ref,), (value_ref,), before_ref, inner_refs, zero_ref)


def other_inner(queries, keys, vals, before, after, sizes):
    tokens, half = queries.shape
    out_shape = [pltpu.VMEM((tokens, n * HEAD_DIM), F32) for n in sizes] + [pltpu.VMEM((1, HEAD_DIM), F32)]
    return pl.pallas_call(
        other_kernel,
        in_specs=[ANYWHERE] + [WHOLE] * 4,
        out_specs=[WHOLE] * len(out_shape),
        out_shape=out_shape,
        compiler_params=params(8),
        cost_estimate=cost(tokens * half * 6 * CHUNK, 12 * tokens * half),
        name="inner",
    )(after, *[in_vmem(x) for x in (queries, keys, vals, before)])


def mix_kernel(parts, first_head, first, last, *refs):
    query_refs, (inner_ref, prefix_ref, *refs) = refs[:parts], refs[parts:]
    extra_ref, mixed_ref, result_ref = (None, *refs) if first else refs
    heads = range(inner_ref.shape[1] // HEAD_DIM)
    blocks = [prefix_ref[head(j), :].astype(BF16) for j in heads]
    for c in range(inner_ref.shape[0] // CHUNK):
        squares = None if first else extra_ref[chunk(c), :]
        query_ref, q = chunk_in(query_refs, c)
        for j in heads:
            mixed = inner_ref[chunk(c), head(j)] + dot_nn(query_ref[q, head(first_head + j)], blocks[j])
            square = mixed * mixed
            squares = square if squares is None else squares + square
            mixed_ref[chunk(c), head(j)] = mixed
        if last:
            result_ref[:, chunk(c)] = jnp.sum(jnp.transpose(squares), axis=0, keepdims=True)
        else:
            result_ref[chunk(c), :] = squares


def mix(queries, inner_group, prefix, squares, first_head, last):
    tokens = inner_group.shape[0]
    first = squares is None
    operands = [*queries, inner_group, prefix] + ([] if first else [squares])
    return pl.pallas_call(
        lambda *refs: mix_kernel(len(queries), first_head, first, last, *refs),
        in_specs=[WHOLE] * len(operands),
        out_specs=[WHOLE, WHOLE],
        out_shape=[
            pltpu.VMEM(inner_group.shape, F32),
            pltpu.VMEM((1, tokens) if last else (tokens, HEAD_DIM), F32),
        ],
        compiler_params=params(8),
        cost_estimate=cost(2 * tokens * prefix.size, 12 * inner_group.size),
        name="mix",
    )(*[in_vmem(x) for x in operands])


def gate_kernel(mine, place_ref, gate_ref, gain_ref, after_ref, *refs):
    *mixed_refs, gated_ref, zero_ref = refs
    tokens, half = gated_ref.shape
    zero_ref[...] = jnp.zeros_like(zero_ref)
    rows = HEAD_DIM
    columns_of = half_heads(place_ref, mine, half)
    homes = [(ref, j) for ref in mixed_refs for j in range(ref.shape[1] // HEAD_DIM)]

    def step(i, carry):
        at = pl.ds(pl.multiple_of(i * rows, rows), rows)
        for h, (mixed_ref, j) in enumerate(homes):
            gate = gate_ref[at, columns_of(h)].astype(F32)
            factor = (0.5 * gain_ref[:, columns_of(h)]) * (1.0 + jnp.tanh(0.5 * gate))
            gated_ref[at, head(h)] = mixed_ref[at, head(j)] * factor
        return carry

    lax.fori_loop(0, tokens // rows, step, 0)


def gated(place, mixed, gate_input, norm_gain, after, mine):
    tokens, width = gate_input.shape
    return pl.pallas_call(
        lambda *refs: gate_kernel(mine, *refs),
        in_specs=[SCALARS, WHOLE, WHOLE, ANYWHERE] + [WHOLE] * len(mixed),
        out_specs=[WHOLE, WHOLE],
        out_shape=[pltpu.VMEM((tokens, width // 2), F32), pltpu.VMEM((1, tokens), F32)],
        compiler_params=params(8),
        cost_estimate=cost(8 * tokens * width, 2 * tokens * width),
        name="gate",
    )(place, in_vmem(gate_input), norm_gain.reshape(1, width), after, *[in_vmem(x) for x in mixed])


def scale_kernel(features, place_ref, mine_ref, other_ref, power_ref, out_ref, mine_out, other_out, sems):
    tokens, half = mine_ref.shape
    rows = HEAD_DIM
    copies = []
    for c in range(tokens // rows):
        at = slice(c * rows, (c + 1) * rows)
        power = jnp.broadcast_to(power_ref[:, at], (HEAD_DIM, rows))
        factor = lax.rsqrt(jnp.transpose(power) / features + 1e-06)
        for j, (source, to) in enumerate(((mine_ref, mine_out), (other_ref, other_out))):
            for h in range(half // HEAD_DIM):
                to[at, head(h)] = (source[at, head(h)] * factor).astype(BF16)
            cols = columns(place_ref, j == 0, half)
            copies.append(pltpu.make_async_copy(to.at[at, :], out_ref.at[at, cols], sems.at[2 * c + j]))
            copies[-1].start()
    for copy in copies:
        copy.wait()


def scale(place, mine, other, power, features):
    tokens, half = mine.shape
    return pl.pallas_call(
        lambda *refs: scale_kernel(features, *refs),
        in_specs=[SCALARS, WHOLE, WHOLE, WHOLE],
        out_specs=ANYWHERE,
        out_shape=pltpu.HBM((tokens, 2 * half), BF16),
        scratch_shapes=[
            pltpu.VMEM((tokens, half), BF16),
            pltpu.VMEM((tokens, half), BF16),
            pltpu.SemaphoreType.DMA((2 * tokens // HEAD_DIM,)),
        ],
        compiler_params=params(8),
        cost_estimate=cost(4 * tokens * half, 4 * tokens * half),
        name="scale",
    )(place, in_vmem(mine), in_vmem(other), in_vmem(power))


def swap(count, bit):
    return [(i, i ^ bit) for i in range(count)]


def general_prefix(blocks, chip, session_of, chip_sum):
    total = chip_sum
    prefix = jnp.zeros_like(chip_sum)
    bit = 1
    while 2 * bit < blocks:
        there = lax.ppermute(total, "ctx", swap(blocks, 2 * bit))
        partner = chip ^ bit
        lower = partner < chip
        end_here = session_of[2 * (chip | (bit - 1)) + 1]
        end_there = session_of[2 * (partner | (bit - 1)) + 1]
        reaches = jnp.logical_and(lower, end_there == session_of[2 * chip])
        prefix = prefix + jnp.where(reaches, 1.0, 0.0) * there
        joined = jnp.where(end_here == end_there, 1.0, 0.0)
        total = jnp.where(lower, total + joined * there, joined * total + there)
        bit *= 2
    return prefix


def zero_after(x):
    def kernel(after_ref, zero_ref):
        zero_ref[...] = jnp.zeros_like(zero_ref)

    return pl.pallas_call(
        kernel,
        in_specs=[ANYWHERE],
        out_specs=WHOLE,
        out_shape=pltpu.VMEM((1, HEAD_DIM), F32),
        compiler_params=params(1),
        name="then",
    )(x)


def two_steps(sums, weight, between, beside):
    there = [lax.ppermute(x, "ctx", [(i, i ^ (2 if i % 2 == 0 else 4)) for i in range(8)]) for x in sums]
    zero = between(sums[0])
    onward = []
    for x, y in zip(sums, there):
        onward.append(weight[2:3] * x + weight[3:4] * y + zero)
        zero = zero_after(onward[-1])
    arrived = [lax.ppermute(x, "ctx", [(i, i ^ (4 if i % 2 == 0 else 2)) for i in range(8)]) for x in onward]
    zero = beside(onward[-1])
    return [weight[4:5] * x + y + zero for x, y in zip(there, arrived)]


def on_device(blocks, features, queries, key_rows, values, gate_input, norm_gain, session_of):
    width = queries.shape[1]
    index = lax.axis_index("ctx").astype(jnp.int32)
    place = index.reshape(1)
    sizes = group_sizes(width // 2 // HEAD_DIM)
    starts = [sum(sizes[:g]) for g in range(GROUPS)]

    sent, sent_before, sent_keys, sent_vals, first_keys, first_vals, weight = sent_states(
        place, session_of, key_rows, values
    )
    got = lax.ppermute(sent, "ctx", swap(blocks, 1))
    kept, (kept_before, late_keys, late_vals, first_queries) = kept_states(
        place, key_rows, values, queries, first_keys, first_vals
    )
    got = [got[at * HEAD_DIM : (at + n) * HEAD_DIM] for at, n in zip(starts, sizes)]
    sums = [x + y for x, y in zip(kept, got)]
    inside, held = {}, {}

    def mine_inside(after):
        keys, vals = (first_keys, late_keys), (first_vals, late_vals)
        late_queries, other_queries, *inside[True], zero = mine_inner(
            place, queries, first_queries, keys, vals, kept_before, after, sizes
        )
        held[True], held[False] = (first_queries, late_queries), (other_queries,)
        return zero

    def other_inside(after):
        *inside[False], zero = other_inner(*held[False], sent_keys, sent_vals, sent_before, after, sizes)
        return zero

    if blocks == 8:
        prefixes = two_steps(sums, weight, mine_inside, other_inside)
    else:
        zero = mine_inside(sums[0]) + other_inside(sums[0])
        prefixes = [general_prefix(blocks, index >> 1, session_of, x) + zero for x in sums]
    even, odd = weight[0:1], weight[1:2]

    mixed = {True: [], False: []}
    squares = None
    zero = jnp.zeros((1, HEAD_DIM), F32)
    for g, prefix in enumerate(prefixes):
        prefix = prefix + zero
        other = lax.ppermute(prefix + even * kept[g], "ctx", swap(blocks, 1))
        mine = prefix + odd * got[g]
        part, squares = mix(held[True], inside[True][g], mine, squares, starts[g], False)
        mixed[True].append(part)
        zero = zero_after(squares)
        part, squares = mix(held[False], inside[False][g], other, squares, starts[g], g == GROUPS - 1)
        mixed[False].append(part)
    power = squares
    gated_other, zero = gated(place, mixed[False], gate_input, norm_gain, power, False)
    power = power + lax.ppermute(power, "head", swap(features // width, 1)) + zero
    gated_mine, zero = gated(place, mixed[True], gate_input, norm_gain, power, True)
    bit = 2
    while bit < features // width:
        power = power + lax.ppermute(power, "head", swap(features // width, bit))
        bit *= 2
    return scale(place, gated_mine, gated_other, power + zero, features)


def solution(mesh):
    blocks = mesh.shape["ctx"]

    def whole(queries, key_rows, values, gate_input, norm_gain, session_of):
        features = queries.shape[1]
        return jax.shard_map(
            lambda *args: on_device(blocks, features, *args),
            mesh=mesh,
            in_specs=(
                P("ctx", "head"),
                P("ctx", "head"),
                P("ctx", "head"),
                P("ctx", "head"),
                P("head"),
                P(),
            ),
            out_specs=P("ctx", "head"),
            check_vma=False,
        )(queries, key_rows, values, gate_input, norm_gain, session_of)

    return whole
```

```python
import jax
import jax.numpy as jnp
from jax import lax
from jax.experimental import pallas as pl
from jax.experimental.pallas import tpu as pltpu
from jax.sharding import PartitionSpec as P

HEAD_DIM = 128
CHUNK = 256
GROUPS = 2
MIB = 1024 * 1024
F32 = jnp.float32
BF16 = jnp.bfloat16
WHOLE = pl.BlockSpec(memory_space=pltpu.VMEM)
SCALARS = pl.BlockSpec(memory_space=pltpu.SMEM)
ANYWHERE = pl.BlockSpec(memory_space=pl.ANY)


def params(mib):
    return pltpu.CompilerParams(vmem_limit_bytes=mib * MIB)


def in_hbm(x):
    return pltpu.with_memory_space_constraint(x, pltpu.HBM)


def in_vmem(x):
    return pltpu.with_memory_space_constraint(x, pltpu.VMEM)


def cost(flops, bytes_accessed):
    return pl.CostEstimate(flops=flops, bytes_accessed=bytes_accessed, transcendentals=0)


def dot_tn(a, b):
    return lax.dot_general(a, b, (((0,), (0,)), ((), ())), preferred_element_type=F32)


def dot_nt(a, b):
    return lax.dot_general(a, b, (((1,), (1,)), ((), ())), preferred_element_type=F32)


def dot_nn(a, b):
    return lax.dot_general(a, b, (((1,), (0,)), ((), ())), preferred_element_type=F32)


def head(h):
    return slice(h * HEAD_DIM, (h + 1) * HEAD_DIM)


def chunk(c):
    return slice(c * CHUNK, (c + 1) * CHUNK)


def columns(place_ref, mine, half):
    core = place_ref[0] & 1
    return pl.ds(pl.multiple_of((core if mine else 1 - core) * half, half), half)


def group_sizes(heads):
    return [(heads + GROUPS - 1 - g) // GROUPS for g in range(GROUPS)]


def fetch(copies, sems, place_ref, mine, pairs, chunks, base=0):
    for c in chunks:
        for source, to in pairs:
            cols = columns(place_ref, mine, to.shape[1])
            rows = slice((c - base) * CHUNK, (c - base + 1) * CHUNK)
            copies.append(pltpu.make_async_copy(source.at[chunk(c), cols], to.at[rows, :], sems.at[len(copies)]))
            copies[-1].start()


def add_chunk(c, keys, vals, rows, state_refs, before_ref):
    half = keys.shape[1]
    h = 0
    for state_ref in state_refs:
        for j in range(state_ref.shape[0] // HEAD_DIM):
            new = dot_tn(keys[rows, head(h)], vals[rows, head(h)])
            if c == 0:
                state_ref[head(j), :] = new
            else:
                old = state_ref[head(j), :]
                at = (c - 1) * half + h * HEAD_DIM
                before_ref[at : at + HEAD_DIM, :] = old.astype(BF16)
                state_ref[head(j), :] = old + new
            h += 1


def sent_kernel(place_ref, session_ref, key_ref, value_ref, state_ref, before_ref, keys, vals,
                next_keys, next_vals, weight_ref, sems, sessions, session_sem):
    chunks = keys.shape[0] // CHUNK
    early = next_keys.shape[0] // CHUNK
    session_copy = pltpu.make_async_copy(session_ref, sessions, session_sem)
    session_copy.start()
    copies = []
    fetch(copies, sems, place_ref, False, ((key_ref, keys), (value_ref, vals)), range(chunks))
    fetch(copies, sems, place_ref, True, ((key_ref, next_keys), (value_ref, next_vals)), range(early))
    session_copy.wait()
    write_weights(place_ref, sessions, weight_ref)
    for c in range(chunks):
        copies[2 * c].wait()
        copies[2 * c + 1].wait()
        add_chunk(c, keys, vals, chunk(c), [state_ref], before_ref)
    for copy in copies[2 * chunks :]:
        copy.wait()


def sent_states(place, session_of, key_rows, values):
    tokens, width = key_rows.shape
    half = width // 2
    chunks = tokens // CHUNK
    early = chunks // 2
    return pl.pallas_call(
        sent_kernel,
        in_specs=[SCALARS] + [ANYWHERE] * 3,
        out_specs=[WHOLE] * 7,
        out_shape=[
            pltpu.VMEM((half, HEAD_DIM), F32),
            pltpu.VMEM(((chunks - 1) * half, HEAD_DIM), BF16),
            pltpu.VMEM((tokens, half), BF16),
            pltpu.VMEM((tokens, half), BF16),
            pltpu.VMEM((early * CHUNK, half), BF16),
            pltpu.VMEM((early * CHUNK, half), BF16),
            pltpu.VMEM((8, HEAD_DIM), F32),
        ],
        scratch_shapes=[
            pltpu.SemaphoreType.DMA((2 * chunks + 2 * early,)),
            pltpu.SMEM(session_of.shape, jnp.int32),
            pltpu.SemaphoreType.DMA(()),
        ],
        compiler_params=params(8),
        cost_estimate=cost(tokens * width * HEAD_DIM, 3 * tokens * width),
        name="states",
    )(place, in_hbm(session_of), in_hbm(key_rows), in_hbm(values))


def kept_kernel(place_ref, key_ref, value_ref, query_ref, first_keys, first_vals, *refs):
    *state_refs, before_ref, keys, vals, queries, sems = refs
    early = first_keys.shape[0] // CHUNK
    chunks = early + keys.shape[0] // CHUNK
    copies = []
    fetch(copies, sems, place_ref, True, ((key_ref, keys), (value_ref, vals)), range(early, chunks), early)
    fetch(copies, sems, place_ref, True, ((query_ref, queries),), range(early))
    for c in range(early):
        add_chunk(c, first_keys, first_vals, chunk(c), state_refs, before_ref)
    for c in range(early, chunks):
        copies[2 * (c - early)].wait()
        copies[2 * (c - early) + 1].wait()
        add_chunk(c, keys, vals, chunk(c - early), state_refs, before_ref)
    for copy in copies[2 * (chunks - early) :]:
        copy.wait()


def kept_states(place, key_rows, values, queries, first_keys, first_vals):
    tokens, width = key_rows.shape
    half = width // 2
    chunks = tokens // CHUNK
    late = tokens - first_keys.shape[0]
    sizes = group_sizes(half // HEAD_DIM)
    out_shape = [pltpu.VMEM((n * HEAD_DIM, HEAD_DIM), F32) for n in sizes] + [
        pltpu.VMEM(((chunks - 1) * half, HEAD_DIM), BF16),
        pltpu.VMEM((late, half), BF16),
        pltpu.VMEM((late, half), BF16),
        pltpu.VMEM((tokens - late, half), BF16),
    ]
    results = pl.pallas_call(
        kept_kernel,
        in_specs=[SCALARS] + [ANYWHERE] * 3 + [WHOLE] * 2,
        out_specs=[WHOLE] * len(out_shape),
        out_shape=out_shape,
        scratch_shapes=[pltpu.SemaphoreType.DMA((chunks + late // CHUNK,))],
        compiler_params=params(8),
        cost_estimate=cost(tokens * width * HEAD_DIM, tokens * width),
        name="states",
    )(place, in_hbm(key_rows), in_hbm(values), in_hbm(queries), in_vmem(first_keys), in_vmem(first_vals))
    return results[: len(sizes)], results[len(sizes) :]


def write_weights(place_ref, session_ref, weight_ref):
    place = place_ref[0]
    core = place & 1
    chip = lax.shift_right_logical(place, 1)

    def flag(condition):
        return jnp.where(condition, 1.0, 0.0).astype(F32)

    def need(to, source):
        same = session_ref[2 * to] == session_ref[2 * source + 1]
        return flag(jnp.logical_and(source < to, same))

    even = core == 0
    rows = [flag(even), flag(core == 1)]
    if session_ref.shape[0] == 8:
        partner = jnp.where(even, chip ^ 1, chip ^ 2)
        to = jnp.where(even, chip ^ 2, chip ^ 1)
        rows += [need(to, chip), need(to, partner), need(chip, partner)]
    for r, value in enumerate(rows):
        weight_ref[r : r + 1, :] = jnp.full((1, HEAD_DIM), value, F32)


def half_heads(place_ref, mine, half):
    start = (place_ref[0] & 1 if mine else 1 - (place_ref[0] & 1)) * half
    return lambda h: pl.ds(pl.multiple_of(start + h * HEAD_DIM, HEAD_DIM), HEAD_DIM)


def chunk_in(refs, c):
    for ref in refs:
        chunks = ref.shape[0] // CHUNK
        if c < chunks:
            return ref, chunk(c)
        c -= chunks


def inner_body(chunks, waits, query_refs, key_refs, value_refs, before_ref, inner_refs, zero_ref):
    zero_ref[...] = jnp.zeros_like(zero_ref)
    rows_at = lax.broadcasted_iota(jnp.int32, (CHUNK, CHUNK), 0)
    cols_at = lax.broadcasted_iota(jnp.int32, (CHUNK, CHUNK), 1)
    causal = rows_at >= cols_at
    homes = [(ref, j) for ref in inner_refs for j in range(ref.shape[1] // HEAD_DIM)]
    half = len(homes) * HEAD_DIM
    for c in range(chunks):
        if c in waits:
            waits[c].wait()
        (query_ref, q), (key_ref, k), (value_ref, v) = (chunk_in(x, c) for x in (query_refs, key_refs, value_refs))
        scores = []
        for h in range(len(homes)):
            full = dot_nt(query_ref[q, head(h)], key_ref[k, head(h)])
            scores.append(jnp.where(causal, full, 0.0).astype(BF16))
        for h, (inner_ref, j) in enumerate(homes):
            left, right = scores[h], value_ref[v, head(h)]
            if c > 0:
                at = (c - 1) * half + h * HEAD_DIM
                left = jnp.concatenate([left, query_ref[q, head(h)]], axis=1)
                right = jnp.concatenate([right, before_ref[at : at + HEAD_DIM, :]], axis=0)
            inner_ref[chunk(c), head(j)] = dot_nn(left, right)


def mine_kernel(place_ref, query_ref, after_ref, first_queries, key_first, key_late, value_first, value_late,
                before_ref, late_queries, other_queries, *refs):
    *inner_refs, zero_ref, sems = refs
    chunks = other_queries.shape[0] // CHUNK
    early = first_queries.shape[0] // CHUNK
    copies = []
    fetch(copies, sems, place_ref, True, ((query_ref, late_queries),), range(early, chunks), early)
    fetch(copies, sems, place_ref, False, ((query_ref, other_queries),), range(chunks))
    waits = {c: copies[c - early] for c in range(early, chunks)}
    inner_body(
        chunks, waits, (first_queries, late_queries), (key_first, key_late), (value_first, value_late),
        before_ref, inner_refs, zero_ref,
    )
    for copy in copies[chunks - early :]:
        copy.wait()


def mine_inner(place, queries, first_queries, keys, vals, before, after, sizes):
    tokens, width = queries.shape
    half = width // 2
    late = tokens - first_queries.shape[0]
    out_shape = [pltpu.VMEM((late, half), BF16), pltpu.VMEM((tokens, half), BF16)]
    out_shape += [pltpu.VMEM((tokens, n * HEAD_DIM), F32) for n in sizes] + [pltpu.VMEM((1, HEAD_DIM), F32)]
    return pl.pallas_call(
        mine_kernel,
        in_specs=[SCALARS, ANYWHERE, ANYWHERE] + [WHOLE] * 6,
        out_specs=[WHOLE] * len(out_shape),
        out_shape=out_shape,
        scratch_shapes=[pltpu.SemaphoreType.DMA(((late + tokens) // CHUNK,))],
        compiler_params=params(8),
        cost_estimate=cost(tokens * half * 6 * CHUNK, 12 * tokens * half),
        name="inner",
    )(place, in_hbm(queries), after, *[in_vmem(x) for x in (first_queries, *keys, *vals, before)])


def other_kernel(after_ref, query_ref, key_ref, value_ref, before_ref, *refs):
    *inner_refs, zero_ref = refs
    chunks = query_ref.shape[0] // CHUNK
    inner_body(chunks, {}, (query_ref,), (key_ref,), (value_ref,), before_ref, inner_refs, zero_ref)


def other_inner(queries, keys, vals, before, after, sizes):
    tokens, half = queries.shape
    out_shape = [pltpu.VMEM((tokens, n * HEAD_DIM), F32) for n in sizes] + [pltpu.VMEM((1, HEAD_DIM), F32)]
    return pl.pallas_call(
        other_kernel,
        in_specs=[ANYWHERE] + [WHOLE] * 4,
        out_specs=[WHOLE] * len(out_shape),
        out_shape=out_shape,
        compiler_params=params(8),
        cost_estimate=cost(tokens * half * 6 * CHUNK, 12 * tokens * half),
        name="inner",
    )(after, *[in_vmem(x) for x in (queries, keys, vals, before)])


def mix_kernel(parts, first_head, first, last, *refs):
    query_refs, (inner_ref, prefix_ref, *refs) = refs[:parts], refs[parts:]
    extra_ref, mixed_ref, result_ref = (None, *refs) if first else refs
    heads = range(inner_ref.shape[1] // HEAD_DIM)
    blocks = [prefix_ref[head(j), :].astype(BF16) for j in heads]
    for c in range(inner_ref.shape[0] // CHUNK):
        squares = None if first else extra_ref[chunk(c), :]
        query_ref, q = chunk_in(query_refs, c)
        for j in heads:
            mixed = inner_ref[chunk(c), head(j)] + dot_nn(query_ref[q, head(first_head + j)], blocks[j])
            square = mixed * mixed
            squares = square if squares is None else squares + square
            mixed_ref[chunk(c), head(j)] = mixed
        if last:
            result_ref[:, chunk(c)] = jnp.sum(jnp.transpose(squares), axis=0, keepdims=True)
        else:
            result_ref[chunk(c), :] = squares


def mix(queries, inner_group, prefix, squares, first_head, last):
    tokens = inner_group.shape[0]
    first = squares is None
    operands = [*queries, inner_group, prefix] + ([] if first else [squares])
    return pl.pallas_call(
        lambda *refs: mix_kernel(len(queries), first_head, first, last, *refs),
        in_specs=[WHOLE] * len(operands),
        out_specs=[WHOLE, WHOLE],
        out_shape=[
            pltpu.VMEM(inner_group.shape, F32),
            pltpu.VMEM((1, tokens) if last else (tokens, HEAD_DIM), F32),
        ],
        compiler_params=params(8),
        cost_estimate=cost(2 * tokens * prefix.size, 12 * inner_group.size),
        name="mix",
    )(*[in_vmem(x) for x in operands])


def gate_kernel(mine, place_ref, gate_ref, gain_ref, after_ref, *refs):
    *mixed_refs, gated_ref, zero_ref = refs
    tokens, half = gated_ref.shape
    zero_ref[...] = jnp.zeros_like(zero_ref)
    rows = HEAD_DIM
    columns_of = half_heads(place_ref, mine, half)
    homes = [(ref, j) for ref in mixed_refs for j in range(ref.shape[1] // HEAD_DIM)]

    def step(i, carry):
        at = pl.ds(pl.multiple_of(i * rows, rows), rows)
        for h, (mixed_ref, j) in enumerate(homes):
            gate = gate_ref[at, columns_of(h)].astype(F32)
            factor = (0.5 * gain_ref[:, columns_of(h)]) * (1.0 + jnp.tanh(0.5 * gate))
            gated_ref[at, head(h)] = mixed_ref[at, head(j)] * factor
        return carry

    lax.fori_loop(0, tokens // rows, step, 0)


def gated(place, mixed, gate_input, norm_gain, after, mine):
    tokens, width = gate_input.shape
    return pl.pallas_call(
        lambda *refs: gate_kernel(mine, *refs),
        in_specs=[SCALARS, WHOLE, WHOLE, ANYWHERE] + [WHOLE] * len(mixed),
        out_specs=[WHOLE, WHOLE],
        out_shape=[pltpu.VMEM((tokens, width // 2), F32), pltpu.VMEM((1, tokens), F32)],
        compiler_params=params(8),
        cost_estimate=cost(8 * tokens * width, 2 * tokens * width),
        name="gate",
    )(place, in_vmem(gate_input), norm_gain.reshape(1, width), after, *[in_vmem(x) for x in mixed])


def scale_kernel(features, place_ref, mine_ref, other_ref, power_ref, out_ref, mine_out, other_out, sems):
    tokens, half = mine_ref.shape
    rows = HEAD_DIM
    copies = []
    for c in range(tokens // rows):
        at = slice(c * rows, (c + 1) * rows)
        power = jnp.broadcast_to(power_ref[:, at], (HEAD_DIM, rows))
        factor = lax.rsqrt(jnp.transpose(power) / features + 1e-06)
        for j, (source, to) in enumerate(((mine_ref, mine_out), (other_ref, other_out))):
            for h in range(half // HEAD_DIM):
                to[at, head(h)] = (source[at, head(h)] * factor).astype(BF16)
            cols = columns(place_ref, j == 0, half)
            copies.append(pltpu.make_async_copy(to.at[at, :], out_ref.at[at, cols], sems.at[2 * c + j]))
            copies[-1].start()
    for copy in copies:
        copy.wait()


def scale(place, mine, other, power, features):
    tokens, half = mine.shape
    return pl.pallas_call(
        lambda *refs: scale_kernel(features, *refs),
        in_specs=[SCALARS, WHOLE, WHOLE, WHOLE],
        out_specs=ANYWHERE,
        out_shape=pltpu.HBM((tokens, 2 * half), BF16),
        scratch_shapes=[
            pltpu.VMEM((tokens, half), BF16),
            pltpu.VMEM((tokens, half), BF16),
            pltpu.SemaphoreType.DMA((2 * tokens // HEAD_DIM,)),
        ],
        compiler_params=params(8),
        cost_estimate=cost(4 * tokens * half, 4 * tokens * half),
        name="scale",
    )(place, in_vmem(mine), in_vmem(other), in_vmem(power))


def swap(count, bit):
    return [(i, i ^ bit) for i in range(count)]


def general_prefix(blocks, chip, session_of, chip_sum):
    total = chip_sum
    prefix = jnp.zeros_like(chip_sum)
    bit = 1
    while 2 * bit < blocks:
        there = lax.ppermute(total, "ctx", swap(blocks, 2 * bit))
        partner = chip ^ bit
        lower = partner < chip
        end_here = session_of[2 * (chip | (bit - 1)) + 1]
        end_there = session_of[2 * (partner | (bit - 1)) + 1]
        reaches = jnp.logical_and(lower, end_there == session_of[2 * chip])
        prefix = prefix + jnp.where(reaches, 1.0, 0.0) * there
        joined = jnp.where(end_here == end_there, 1.0, 0.0)
        total = jnp.where(lower, total + joined * there, joined * total + there)
        bit *= 2
    return prefix


def zero_after(x):
    def kernel(after_ref, zero_ref):
        zero_ref[...] = jnp.zeros_like(zero_ref)

    return pl.pallas_call(
        kernel,
        in_specs=[ANYWHERE],
        out_specs=WHOLE,
        out_shape=pltpu.VMEM((1, HEAD_DIM), F32),
        compiler_params=params(1),
        name="then",
    )(x)


def two_steps(sums, weight, between, beside):
    there = [lax.ppermute(x, "ctx", [(i, i ^ (2 if i % 2 == 0 else 4)) for i in range(8)]) for x in sums]
    zero = between(sums[0])
    onward = []
    for x, y in zip(sums, there):
        onward.append(weight[2:3] * x + weight[3:4] * y + zero)
        zero = zero_after(onward[-1])
    arrived = [lax.ppermute(x, "ctx", [(i, i ^ (4 if i % 2 == 0 else 2)) for i in range(8)]) for x in onward]
    zero = beside(onward[-1])
    return [weight[4:5] * x + y + zero for x, y in zip(there, arrived)]


def on_device(blocks, features, queries, key_rows, values, gate_input, norm_gain, session_of):
    width = queries.shape[1]
    index = lax.axis_index("ctx").astype(jnp.int32)
    place = index.reshape(1)
    sizes = group_sizes(width // 2 // HEAD_DIM)
    starts = [sum(sizes[:g]) for g in range(GROUPS)]

    sent, sent_before, sent_keys, sent_vals, first_keys, first_vals, weight = sent_states(
        place, session_of, key_rows, values
    )
    got = lax.ppermute(sent, "ctx", swap(blocks, 1))
    kept, (kept_before, late_keys, late_vals, first_queries) = kept_states(
        place, key_rows, values, queries, first_keys, first_vals
    )
    got = [got[at * HEAD_DIM : (at + n) * HEAD_DIM] for at, n in zip(starts, sizes)]
    sums = [x + y for x, y in zip(kept, got)]
    inside, held = {}, {}

    def mine_inside(after):
        keys, vals = (first_keys, late_keys), (first_vals, late_vals)
        late_queries, other_queries, *inside[True], zero = mine_inner(
            place, queries, first_queries, keys, vals, kept_before, after, sizes
        )
        held[True], held[False] = (first_queries, late_queries), (other_queries,)
        return zero

    def other_inside(after):
        *inside[False], zero = other_inner(*held[False], sent_keys, sent_vals, sent_before, after, sizes)
        return zero

    if blocks == 8:
        prefixes = two_steps(sums, weight, mine_inside, other_inside)
    else:
        zero = mine_inside(sums[0]) + other_inside(sums[0])
        prefixes = [general_prefix(blocks, index >> 1, session_of, x) + zero for x in sums]
    even, odd = weight[0:1], weight[1:2]

    mixed = {True: [], False: []}
    squares = None
    zero = jnp.zeros((1, HEAD_DIM), F32)
    for g, prefix in enumerate(prefixes):
        prefix = prefix + zero
        other = lax.ppermute(prefix + even * kept[g], "ctx", swap(blocks, 1))
        mine = prefix + odd * got[g]
        part, squares = mix(held[True], inside[True][g], mine, squares, starts[g], False)
        mixed[True].append(part)
        zero = zero_after(squares)
        part, squares = mix(held[False], inside[False][g], other, squares, starts[g], g == GROUPS - 1)
        mixed[False].append(part)
    power = squares
    count = features // width

    def crossed(bit):
        pairs = [(c * count + z, (c ^ 1) * count + (z ^ bit)) for c in range(blocks) for z in range(count)]
        return lax.ppermute(power, ("ctx", "head"), pairs) + lax.ppermute(power, "ctx", swap(blocks, 1))

    gated_other, zero = gated(place, mixed[False], gate_input, norm_gain, power, False)
    power = crossed(1) + zero
    gated_mine, zero = gated(place, mixed[True], gate_input, norm_gain, power, True)
    power = crossed(2) + zero
    bit, swapped = 4, False
    while bit < count:
        power = crossed(bit)
        bit, swapped = 2 * bit, not swapped
    if swapped:
        power = lax.ppermute(power, "ctx", swap(blocks, 1))
    return scale(place, gated_mine, gated_other, power, features)


def solution(mesh):
    blocks = mesh.shape["ctx"]

    def whole(queries, key_rows, values, gate_input, norm_gain, session_of):
        features = queries.shape[1]
        return jax.shard_map(
            lambda *args: on_device(blocks, features, *args),
            mesh=mesh,
            in_specs=(
                P("ctx", "head"),
                P("ctx", "head"),
                P("ctx", "head"),
                P("ctx", "head"),
                P("head"),
                P(),
            ),
            out_specs=P("ctx", "head"),
            check_vma=False,
        )(queries, key_rows, values, gate_input, norm_gain, session_of)

    return whole
```

```python
import jax
import jax.numpy as jnp
from jax import lax
from jax.experimental import pallas as pl
from jax.experimental.pallas import tpu as pltpu
from jax.sharding import PartitionSpec as P

HEAD_DIM = 128
CHUNK = 256
GROUPS = 2
MIB = 1024 * 1024
F32 = jnp.float32
BF16 = jnp.bfloat16
WHOLE = pl.BlockSpec(memory_space=pltpu.VMEM)
SCALARS = pl.BlockSpec(memory_space=pltpu.SMEM)
ANYWHERE = pl.BlockSpec(memory_space=pl.ANY)


def params(mib):
    return pltpu.CompilerParams(vmem_limit_bytes=mib * MIB)


def in_hbm(x):
    return pltpu.with_memory_space_constraint(x, pltpu.HBM)


def in_vmem(x):
    return pltpu.with_memory_space_constraint(x, pltpu.VMEM)


def cost(flops, bytes_accessed):
    return pl.CostEstimate(flops=flops, bytes_accessed=bytes_accessed, transcendentals=0)


def dot_tn(a, b):
    return lax.dot_general(a, b, (((0,), (0,)), ((), ())), preferred_element_type=F32)


def dot_nt(a, b):
    return lax.dot_general(a, b, (((1,), (1,)), ((), ())), preferred_element_type=F32)


def dot_nn(a, b):
    return lax.dot_general(a, b, (((1,), (0,)), ((), ())), preferred_element_type=F32)


def head(h):
    return slice(h * HEAD_DIM, (h + 1) * HEAD_DIM)


def chunk(c):
    return slice(c * CHUNK, (c + 1) * CHUNK)


def columns(place_ref, mine, half):
    core = place_ref[0] & 1
    return pl.ds(pl.multiple_of((core if mine else 1 - core) * half, half), half)


def group_sizes(heads):
    return [(heads + GROUPS - 1 - g) // GROUPS for g in range(GROUPS)]


def fetch(copies, sems, place_ref, mine, pairs, chunks, base=0):
    for c in chunks:
        for source, to in pairs:
            cols = columns(place_ref, mine, to.shape[1])
            rows = slice((c - base) * CHUNK, (c - base + 1) * CHUNK)
            copies.append(pltpu.make_async_copy(source.at[chunk(c), cols], to.at[rows, :], sems.at[len(copies)]))
            copies[-1].start()


def add_chunk(c, keys, vals, rows, state_refs, before_ref):
    half = keys.shape[1]
    h = 0
    for state_ref in state_refs:
        for j in range(state_ref.shape[0] // HEAD_DIM):
            new = dot_tn(keys[rows, head(h)], vals[rows, head(h)])
            if c == 0:
                state_ref[head(j), :] = new
            else:
                old = state_ref[head(j), :]
                at = (c - 1) * half + h * HEAD_DIM
                before_ref[at : at + HEAD_DIM, :] = old.astype(BF16)
                state_ref[head(j), :] = old + new
            h += 1


def sent_kernel(place_ref, session_ref, key_ref, value_ref, state_ref, before_ref, keys, vals,
                next_keys, next_vals, weight_ref, sems, sessions, session_sem):
    chunks = keys.shape[0] // CHUNK
    early = next_keys.shape[0] // CHUNK
    session_copy = pltpu.make_async_copy(session_ref, sessions, session_sem)
    session_copy.start()
    copies = []
    fetch(copies, sems, place_ref, False, ((key_ref, keys), (value_ref, vals)), range(chunks))
    fetch(copies, sems, place_ref, True, ((key_ref, next_keys), (value_ref, next_vals)), range(early))
    session_copy.wait()
    write_weights(place_ref, sessions, weight_ref)
    for c in range(chunks):
        copies[2 * c].wait()
        copies[2 * c + 1].wait()
        add_chunk(c, keys, vals, chunk(c), [state_ref], before_ref)
    for copy in copies[2 * chunks :]:
        copy.wait()


def sent_states(place, session_of, key_rows, values):
    tokens, width = key_rows.shape
    half = width // 2
    chunks = tokens // CHUNK
    early = chunks // 2
    return pl.pallas_call(
        sent_kernel,
        in_specs=[SCALARS] + [ANYWHERE] * 3,
        out_specs=[WHOLE] * 7,
        out_shape=[
            pltpu.VMEM((half, HEAD_DIM), F32),
            pltpu.VMEM(((chunks - 1) * half, HEAD_DIM), BF16),
            pltpu.VMEM((tokens, half), BF16),
            pltpu.VMEM((tokens, half), BF16),
            pltpu.VMEM((early * CHUNK, half), BF16),
            pltpu.VMEM((early * CHUNK, half), BF16),
            pltpu.VMEM((8, HEAD_DIM), F32),
        ],
        scratch_shapes=[
            pltpu.SemaphoreType.DMA((2 * chunks + 2 * early,)),
            pltpu.SMEM(session_of.shape, jnp.int32),
            pltpu.SemaphoreType.DMA(()),
        ],
        compiler_params=params(8),
        cost_estimate=cost(tokens * width * HEAD_DIM, 3 * tokens * width),
        name="states",
    )(place, in_hbm(session_of), in_hbm(key_rows), in_hbm(values))


def kept_kernel(place_ref, key_ref, value_ref, query_ref, first_keys, first_vals, *refs):
    *state_refs, before_ref, keys, vals, queries, sems = refs
    early = first_keys.shape[0] // CHUNK
    chunks = early + keys.shape[0] // CHUNK
    copies = []
    fetch(copies, sems, place_ref, True, ((key_ref, keys), (value_ref, vals)), range(early, chunks), early)
    fetch(copies, sems, place_ref, True, ((query_ref, queries),), range(early))
    for c in range(early):
        add_chunk(c, first_keys, first_vals, chunk(c), state_refs, before_ref)
    for c in range(early, chunks):
        copies[2 * (c - early)].wait()
        copies[2 * (c - early) + 1].wait()
        add_chunk(c, keys, vals, chunk(c - early), state_refs, before_ref)
    for copy in copies[2 * (chunks - early) :]:
        copy.wait()


def kept_states(place, key_rows, values, queries, first_keys, first_vals):
    tokens, width = key_rows.shape
    half = width // 2
    chunks = tokens // CHUNK
    late = tokens - first_keys.shape[0]
    sizes = group_sizes(half // HEAD_DIM)
    out_shape = [pltpu.VMEM((n * HEAD_DIM, HEAD_DIM), F32) for n in sizes] + [
        pltpu.VMEM(((chunks - 1) * half, HEAD_DIM), BF16),
        pltpu.VMEM((late, half), BF16),
        pltpu.VMEM((late, half), BF16),
        pltpu.VMEM((tokens - late, half), BF16),
    ]
    results = pl.pallas_call(
        kept_kernel,
        in_specs=[SCALARS] + [ANYWHERE] * 3 + [WHOLE] * 2,
        out_specs=[WHOLE] * len(out_shape),
        out_shape=out_shape,
        scratch_shapes=[pltpu.SemaphoreType.DMA((chunks + late // CHUNK,))],
        compiler_params=params(8),
        cost_estimate=cost(tokens * width * HEAD_DIM, tokens * width),
        name="states",
    )(place, in_hbm(key_rows), in_hbm(values), in_hbm(queries), in_vmem(first_keys), in_vmem(first_vals))
    return results[: len(sizes)], results[len(sizes) :]


def write_weights(place_ref, session_ref, weight_ref):
    place = place_ref[0]
    core = place & 1
    chip = lax.shift_right_logical(place, 1)

    def flag(condition):
        return jnp.where(condition, 1.0, 0.0).astype(F32)

    def need(to, source):
        same = session_ref[2 * to] == session_ref[2 * source + 1]
        return flag(jnp.logical_and(source < to, same))

    even = core == 0
    rows = [flag(even), flag(core == 1)]
    if session_ref.shape[0] == 8:
        partner = jnp.where(even, chip ^ 1, chip ^ 2)
        to = jnp.where(even, chip ^ 2, chip ^ 1)
        rows += [need(to, chip), need(to, partner), need(chip, partner)]
    for r, value in enumerate(rows):
        weight_ref[r : r + 1, :] = jnp.full((1, HEAD_DIM), value, F32)


def half_heads(place_ref, mine, half):
    start = (place_ref[0] & 1 if mine else 1 - (place_ref[0] & 1)) * half
    return lambda h: pl.ds(pl.multiple_of(start + h * HEAD_DIM, HEAD_DIM), HEAD_DIM)


def chunk_in(refs, c):
    for ref in refs:
        chunks = ref.shape[0] // CHUNK
        if c < chunks:
            return ref, chunk(c)
        c -= chunks


def inner_body(chunks, waits, query_refs, key_refs, value_refs, before_ref, inner_refs, zero_ref):
    zero_ref[...] = jnp.zeros_like(zero_ref)
    rows_at = lax.broadcasted_iota(jnp.int32, (CHUNK, CHUNK), 0)
    cols_at = lax.broadcasted_iota(jnp.int32, (CHUNK, CHUNK), 1)
    causal = rows_at >= cols_at
    homes = [(ref, j) for ref in inner_refs for j in range(ref.shape[1] // HEAD_DIM)]
    half = len(homes) * HEAD_DIM
    for c in range(chunks):
        if c in waits:
            waits[c].wait()
        (query_ref, q), (key_ref, k), (value_ref, v) = (chunk_in(x, c) for x in (query_refs, key_refs, value_refs))
        scores = []
        for h in range(len(homes)):
            full = dot_nt(query_ref[q, head(h)], key_ref[k, head(h)])
            scores.append(jnp.where(causal, full, 0.0).astype(BF16))
        for h, (inner_ref, j) in enumerate(homes):
            left, right = scores[h], value_ref[v, head(h)]
            if c > 0:
                at = (c - 1) * half + h * HEAD_DIM
                left = jnp.concatenate([left, query_ref[q, head(h)]], axis=1)
                right = jnp.concatenate([right, before_ref[at : at + HEAD_DIM, :]], axis=0)
            inner_ref[chunk(c), head(j)] = dot_nn(left, right)


def mine_kernel(place_ref, query_ref, after_ref, first_queries, key_first, key_late, value_first, value_late,
                before_ref, late_queries, other_queries, *refs):
    *inner_refs, zero_ref, sems = refs
    chunks = other_queries.shape[0] // CHUNK
    early = first_queries.shape[0] // CHUNK
    copies = []
    fetch(copies, sems, place_ref, True, ((query_ref, late_queries),), range(early, chunks), early)
    fetch(copies, sems, place_ref, False, ((query_ref, other_queries),), range(chunks))
    waits = {c: copies[c - early] for c in range(early, chunks)}
    inner_body(
        chunks, waits, (first_queries, late_queries), (key_first, key_late), (value_first, value_late),
        before_ref, inner_refs, zero_ref,
    )
    for copy in copies[chunks - early :]:
        copy.wait()


def mine_inner(place, queries, first_queries, keys, vals, before, after, sizes):
    tokens, width = queries.shape
    half = width // 2
    late = tokens - first_queries.shape[0]
    out_shape = [pltpu.VMEM((late, half), BF16), pltpu.VMEM((tokens, half), BF16)]
    out_shape += [pltpu.VMEM((tokens, n * HEAD_DIM), F32) for n in sizes] + [pltpu.VMEM((1, HEAD_DIM), F32)]
    return pl.pallas_call(
        mine_kernel,
        in_specs=[SCALARS, ANYWHERE, ANYWHERE] + [WHOLE] * 6,
        out_specs=[WHOLE] * len(out_shape),
        out_shape=out_shape,
        scratch_shapes=[pltpu.SemaphoreType.DMA(((late + tokens) // CHUNK,))],
        compiler_params=params(8),
        cost_estimate=cost(tokens * half * 6 * CHUNK, 12 * tokens * half),
        name="inner",
    )(place, in_hbm(queries), after, *[in_vmem(x) for x in (first_queries, *keys, *vals, before)])


def other_kernel(after_ref, query_ref, key_ref, value_ref, before_ref, *refs):
    *inner_refs, zero_ref = refs
    chunks = query_ref.shape[0] // CHUNK
    inner_body(chunks, {}, (query_ref,), (key_ref,), (value_ref,), before_ref, inner_refs, zero_ref)


def other_inner(queries, keys, vals, before, after, sizes):
    tokens, half = queries.shape
    out_shape = [pltpu.VMEM((tokens, n * HEAD_DIM), F32) for n in sizes] + [pltpu.VMEM((1, HEAD_DIM), F32)]
    return pl.pallas_call(
        other_kernel,
        in_specs=[ANYWHERE] + [WHOLE] * 4,
        out_specs=[WHOLE] * len(out_shape),
        out_shape=out_shape,
        compiler_params=params(8),
        cost_estimate=cost(tokens * half * 6 * CHUNK, 12 * tokens * half),
        name="inner",
    )(after, *[in_vmem(x) for x in (queries, keys, vals, before)])


def mix_kernel(parts, first_head, first, last, *refs):
    query_refs, (inner_ref, prefix_ref, *refs) = refs[:parts], refs[parts:]
    extra_ref, mixed_ref, result_ref = (None, *refs) if first else refs
    heads = range(inner_ref.shape[1] // HEAD_DIM)
    blocks = [prefix_ref[head(j), :].astype(BF16) for j in heads]
    for c in range(inner_ref.shape[0] // CHUNK):
        squares = None if first else extra_ref[chunk(c), :]
        query_ref, q = chunk_in(query_refs, c)
        for j in heads:
            mixed = inner_ref[chunk(c), head(j)] + dot_nn(query_ref[q, head(first_head + j)], blocks[j])
            square = mixed * mixed
            squares = square if squares is None else squares + square
            mixed_ref[chunk(c), head(j)] = mixed
        if last:
            result_ref[:, chunk(c)] = jnp.sum(jnp.transpose(squares), axis=0, keepdims=True)
        else:
            result_ref[chunk(c), :] = squares


def mix(queries, inner_group, prefix, squares, first_head, last):
    tokens = inner_group.shape[0]
    first = squares is None
    operands = [*queries, inner_group, prefix] + ([] if first else [squares])
    return pl.pallas_call(
        lambda *refs: mix_kernel(len(queries), first_head, first, last, *refs),
        in_specs=[WHOLE] * len(operands),
        out_specs=[WHOLE, WHOLE],
        out_shape=[
            pltpu.VMEM(inner_group.shape, F32),
            pltpu.VMEM((1, tokens) if last else (tokens, HEAD_DIM), F32),
        ],
        compiler_params=params(8),
        cost_estimate=cost(2 * tokens * prefix.size, 12 * inner_group.size),
        name="mix",
    )(*[in_vmem(x) for x in operands])


def gate_kernel(mine, place_ref, gate_ref, gain_ref, after_ref, *refs):
    *mixed_refs, gated_ref, zero_ref = refs
    tokens, half = gated_ref.shape
    zero_ref[...] = jnp.zeros_like(zero_ref)
    rows = HEAD_DIM
    columns_of = half_heads(place_ref, mine, half)
    homes = [(ref, j) for ref in mixed_refs for j in range(ref.shape[1] // HEAD_DIM)]

    def step(i, carry):
        at = pl.ds(pl.multiple_of(i * rows, rows), rows)
        for h, (mixed_ref, j) in enumerate(homes):
            gate = gate_ref[at, columns_of(h)].astype(F32)
            factor = (0.5 * gain_ref[:, columns_of(h)]) * (1.0 + jnp.tanh(0.5 * gate))
            gated_ref[at, head(h)] = mixed_ref[at, head(j)] * factor
        return carry

    lax.fori_loop(0, tokens // rows, step, 0)


def gated(place, mixed, gate_input, norm_gain, after, mine):
    tokens, width = gate_input.shape
    return pl.pallas_call(
        lambda *refs: gate_kernel(mine, *refs),
        in_specs=[SCALARS, WHOLE, WHOLE, ANYWHERE] + [WHOLE] * len(mixed),
        out_specs=[WHOLE, WHOLE],
        out_shape=[pltpu.VMEM((tokens, width // 2), F32), pltpu.VMEM((1, tokens), F32)],
        compiler_params=params(8),
        cost_estimate=cost(8 * tokens * width, 2 * tokens * width),
        name="gate",
    )(place, in_vmem(gate_input), norm_gain.reshape(1, width), after, *[in_vmem(x) for x in mixed])


def scale_kernel(features, place_ref, mine_ref, other_ref, power_ref, out_ref, mine_out, other_out, sems):
    tokens, half = mine_ref.shape
    rows = HEAD_DIM
    copies = []
    for c in range(tokens // rows):
        at = slice(c * rows, (c + 1) * rows)
        power = jnp.broadcast_to(power_ref[:, at], (HEAD_DIM, rows))
        factor = lax.rsqrt(jnp.transpose(power) / features + 1e-06)
        for j, (source, to) in enumerate(((mine_ref, mine_out), (other_ref, other_out))):
            for h in range(half // HEAD_DIM):
                to[at, head(h)] = (source[at, head(h)] * factor).astype(BF16)
            cols = columns(place_ref, j == 0, half)
            copies.append(pltpu.make_async_copy(to.at[at, :], out_ref.at[at, cols], sems.at[2 * c + j]))
            copies[-1].start()
    for copy in copies:
        copy.wait()


def scale(place, mine, other, power, features):
    tokens, half = mine.shape
    return pl.pallas_call(
        lambda *refs: scale_kernel(features, *refs),
        in_specs=[SCALARS, WHOLE, WHOLE, WHOLE],
        out_specs=ANYWHERE,
        out_shape=pltpu.HBM((tokens, 2 * half), BF16),
        scratch_shapes=[
            pltpu.VMEM((tokens, half), BF16),
            pltpu.VMEM((tokens, half), BF16),
            pltpu.SemaphoreType.DMA((2 * tokens // HEAD_DIM,)),
        ],
        compiler_params=params(8),
        cost_estimate=cost(4 * tokens * half, 4 * tokens * half),
        name="scale",
    )(place, in_vmem(mine), in_vmem(other), in_vmem(power))


def swap(count, bit):
    return [(i, i ^ bit) for i in range(count)]


def general_prefix(blocks, chip, session_of, chip_sum):
    total = chip_sum
    prefix = jnp.zeros_like(chip_sum)
    bit = 1
    while 2 * bit < blocks:
        there = lax.ppermute(total, "ctx", swap(blocks, 2 * bit))
        partner = chip ^ bit
        lower = partner < chip
        end_here = session_of[2 * (chip | (bit - 1)) + 1]
        end_there = session_of[2 * (partner | (bit - 1)) + 1]
        reaches = jnp.logical_and(lower, end_there == session_of[2 * chip])
        prefix = prefix + jnp.where(reaches, 1.0, 0.0) * there
        joined = jnp.where(end_here == end_there, 1.0, 0.0)
        total = jnp.where(lower, total + joined * there, joined * total + there)
        bit *= 2
    return prefix


def zero_after(x):
    def kernel(after_ref, zero_ref):
        zero_ref[...] = jnp.zeros_like(zero_ref)

    return pl.pallas_call(
        kernel,
        in_specs=[ANYWHERE],
        out_specs=WHOLE,
        out_shape=pltpu.VMEM((1, HEAD_DIM), F32),
        compiler_params=params(1),
        name="then",
    )(x)


def two_steps(sums, weight, between, beside):
    there = [lax.ppermute(x, "ctx", [(i, i ^ (2 if i % 2 == 0 else 4)) for i in range(8)]) for x in sums]
    zero = between(sums[0])
    onward = []
    for x, y in zip(sums, there):
        onward.append(weight[2:3] * x + weight[3:4] * y + zero)
        zero = zero_after(onward[-1])
    arrived = [lax.ppermute(x, "ctx", [(i, i ^ (5 if i % 2 == 0 else 3)) for i in range(8)]) for x in onward]
    zero = beside(onward[-1])
    return [weight[4:5] * x for x in there], [x + zero for x in arrived]


def on_device(blocks, features, queries, key_rows, values, gate_input, norm_gain, session_of):
    width = queries.shape[1]
    index = lax.axis_index("ctx").astype(jnp.int32)
    place = index.reshape(1)
    sizes = group_sizes(width // 2 // HEAD_DIM)
    starts = [sum(sizes[:g]) for g in range(GROUPS)]

    sent, sent_before, sent_keys, sent_vals, first_keys, first_vals, weight = sent_states(
        place, session_of, key_rows, values
    )
    got = lax.ppermute(sent, "ctx", swap(blocks, 1))
    kept, (kept_before, late_keys, late_vals, first_queries) = kept_states(
        place, key_rows, values, queries, first_keys, first_vals
    )
    got = [got[at * HEAD_DIM : (at + n) * HEAD_DIM] for at, n in zip(starts, sizes)]
    sums = [x + y for x, y in zip(kept, got)]
    inside, held = {}, {}

    def mine_inside(after):
        keys, vals = (first_keys, late_keys), (first_vals, late_vals)
        late_queries, other_queries, *inside[True], zero = mine_inner(
            place, queries, first_queries, keys, vals, kept_before, after, sizes
        )
        held[True], held[False] = (first_queries, late_queries), (other_queries,)
        return zero

    def other_inside(after):
        *inside[False], zero = other_inner(*held[False], sent_keys, sent_vals, sent_before, after, sizes)
        return zero

    if blocks == 8:
        own, arrived = two_steps(sums, weight, mine_inside, other_inside)
    else:
        zero = other_inside(mine_inside(sums[0]))
        own = [general_prefix(blocks, index >> 1, session_of, x) + zero for x in sums]
        arrived = [jnp.zeros_like(x) for x in sums]
    even, odd = weight[0:1], weight[1:2]
    others = [lax.ppermute(x + even * k, "ctx", swap(blocks, 1)) for x, k in zip(own, kept)]

    mixed = {True: [], False: []}
    parts, backs = [], []
    squares = None

    def swap_part(g, zero):
        parts.append(arrived[g] + zero)
        backs.append(lax.ppermute(parts[g], "ctx", swap(blocks, 1)))
        return zero_after(parts[g])

    def mix_group(mine, zero, last=False):
        nonlocal squares
        g = len(mixed[mine])
        prefix = own[g] + odd * got[g] + backs[g] if mine else others[g] + parts[g]
        part, squares = mix(held[mine], inside[mine][g], prefix + zero, squares, starts[g], last)
        mixed[mine].append(part)
        return zero_after(squares)

    zero = swap_part(0, jnp.zeros((1, HEAD_DIM), F32))
    for g in range(GROUPS):
        zero = mix_group(False, zero)
        if g + 1 < GROUPS:
            zero = swap_part(g + 1, zero)
        zero = mix_group(True, zero, g == GROUPS - 1)
    power = squares
    count = features // width

    def crossed(bit):
        pairs = [(c * count + z, (c ^ 1) * count + (z ^ bit)) for c in range(blocks) for z in range(count)]
        return lax.ppermute(power, ("ctx", "head"), pairs) + lax.ppermute(power, "ctx", swap(blocks, 1))

    gated_other, zero = gated(place, mixed[False], gate_input, norm_gain, power, False)
    power = crossed(1) + zero
    gated_mine, zero = gated(place, mixed[True], gate_input, norm_gain, power, True)
    power = crossed(2) + zero
    bit, swapped = 4, False
    while bit < count:
        power = crossed(bit)
        bit, swapped = 2 * bit, not swapped
    if swapped:
        power = lax.ppermute(power, "ctx", swap(blocks, 1))
    return scale(place, gated_mine, gated_other, power, features)


def solution(mesh):
    blocks = mesh.shape["ctx"]

    def whole(queries, key_rows, values, gate_input, norm_gain, session_of):
        features = queries.shape[1]
        return jax.shard_map(
            lambda *args: on_device(blocks, features, *args),
            mesh=mesh,
            in_specs=(
                P("ctx", "head"),
                P("ctx", "head"),
                P("ctx", "head"),
                P("ctx", "head"),
                P("head"),
                P(),
            ),
            out_specs=P("ctx", "head"),
            check_vma=False,
        )(queries, key_rows, values, gate_input, norm_gain, session_of)

    return whole
```

```python
import jax
import jax.numpy as jnp
from jax import lax
from jax.experimental import pallas as pl
from jax.experimental.pallas import tpu as pltpu
from jax.sharding import PartitionSpec as P

HEAD_DIM = 128
CHUNK = 256
GROUPS = 2
MIB = 1024 * 1024
F32 = jnp.float32
BF16 = jnp.bfloat16
WHOLE = pl.BlockSpec(memory_space=pltpu.VMEM)
SCALARS = pl.BlockSpec(memory_space=pltpu.SMEM)
ANYWHERE = pl.BlockSpec(memory_space=pl.ANY)


def params(mib):
    return pltpu.CompilerParams(vmem_limit_bytes=mib * MIB)


def in_hbm(x):
    return pltpu.with_memory_space_constraint(x, pltpu.HBM)


def in_vmem(x):
    return pltpu.with_memory_space_constraint(x, pltpu.VMEM)


def cost(flops, bytes_accessed):
    return pl.CostEstimate(flops=flops, bytes_accessed=bytes_accessed, transcendentals=0)


def dot_tn(a, b):
    return lax.dot_general(a, b, (((0,), (0,)), ((), ())), preferred_element_type=F32)


def dot_nt(a, b):
    return lax.dot_general(a, b, (((1,), (1,)), ((), ())), preferred_element_type=F32)


def dot_nn(a, b):
    return lax.dot_general(a, b, (((1,), (0,)), ((), ())), preferred_element_type=F32)


def head(h):
    return slice(h * HEAD_DIM, (h + 1) * HEAD_DIM)


def chunk(c):
    return slice(c * CHUNK, (c + 1) * CHUNK)


def columns(place_ref, mine, half):
    core = place_ref[0] & 1
    return pl.ds(pl.multiple_of((core if mine else 1 - core) * half, half), half)


def group_sizes(heads):
    return [(heads + GROUPS - 1 - g) // GROUPS for g in range(GROUPS)]


def fetch(copies, sems, place_ref, mine, pairs, chunks, base=0):
    for c in chunks:
        for source, to in pairs:
            cols = columns(place_ref, mine, to.shape[1])
            rows = slice((c - base) * CHUNK, (c - base + 1) * CHUNK)
            copies.append(pltpu.make_async_copy(source.at[chunk(c), cols], to.at[rows, :], sems.at[len(copies)]))
            copies[-1].start()


def add_chunk(c, keys, vals, rows, state_refs, before_ref):
    half = keys.shape[1]
    h = 0
    for state_ref in state_refs:
        for j in range(state_ref.shape[0] // HEAD_DIM):
            new = dot_tn(keys[rows, head(h)], vals[rows, head(h)])
            if c == 0:
                state_ref[head(j), :] = new
            else:
                old = state_ref[head(j), :]
                at = (c - 1) * half + h * HEAD_DIM
                before_ref[at : at + HEAD_DIM, :] = old.astype(BF16)
                state_ref[head(j), :] = old + new
            h += 1


def sent_kernel(place_ref, session_ref, key_ref, value_ref, state_ref, before_ref, keys, vals,
                next_keys, next_vals, weight_ref, sems, sessions, session_sem):
    chunks = keys.shape[0] // CHUNK
    early = next_keys.shape[0] // CHUNK
    session_copy = pltpu.make_async_copy(session_ref, sessions, session_sem)
    session_copy.start()
    copies = []
    fetch(copies, sems, place_ref, False, ((key_ref, keys), (value_ref, vals)), range(chunks))
    fetch(copies, sems, place_ref, True, ((key_ref, next_keys), (value_ref, next_vals)), range(early))
    session_copy.wait()
    write_weights(place_ref, sessions, weight_ref)
    for c in range(chunks):
        copies[2 * c].wait()
        copies[2 * c + 1].wait()
        add_chunk(c, keys, vals, chunk(c), [state_ref], before_ref)
    for copy in copies[2 * chunks :]:
        copy.wait()


def sent_states(place, session_of, key_rows, values):
    tokens, width = key_rows.shape
    half = width // 2
    chunks = tokens // CHUNK
    early = chunks // 2
    return pl.pallas_call(
        sent_kernel,
        in_specs=[SCALARS] + [ANYWHERE] * 3,
        out_specs=[WHOLE] * 7,
        out_shape=[
            pltpu.VMEM((half, HEAD_DIM), F32),
            pltpu.VMEM(((chunks - 1) * half, HEAD_DIM), BF16),
            pltpu.VMEM((tokens, half), BF16),
            pltpu.VMEM((tokens, half), BF16),
            pltpu.VMEM((early * CHUNK, half), BF16),
            pltpu.VMEM((early * CHUNK, half), BF16),
            pltpu.VMEM((8, HEAD_DIM), F32),
        ],
        scratch_shapes=[
            pltpu.SemaphoreType.DMA((2 * chunks + 2 * early,)),
            pltpu.SMEM(session_of.shape, jnp.int32),
            pltpu.SemaphoreType.DMA(()),
        ],
        compiler_params=params(8),
        cost_estimate=cost(tokens * width * HEAD_DIM, 3 * tokens * width),
        name="states",
    )(place, in_hbm(session_of), in_hbm(key_rows), in_hbm(values))


def kept_kernel(place_ref, key_ref, value_ref, query_ref, first_keys, first_vals, *refs):
    *state_refs, before_ref, keys, vals, queries, sems = refs
    early = first_keys.shape[0] // CHUNK
    chunks = early + keys.shape[0] // CHUNK
    copies = []
    fetch(copies, sems, place_ref, True, ((key_ref, keys), (value_ref, vals)), range(early, chunks), early)
    fetch(copies, sems, place_ref, True, ((query_ref, queries),), range(early))
    for c in range(early):
        add_chunk(c, first_keys, first_vals, chunk(c), state_refs, before_ref)
    for c in range(early, chunks):
        copies[2 * (c - early)].wait()
        copies[2 * (c - early) + 1].wait()
        add_chunk(c, keys, vals, chunk(c - early), state_refs, before_ref)
    for copy in copies[2 * (chunks - early) :]:
        copy.wait()


def kept_states(place, key_rows, values, queries, first_keys, first_vals):
    tokens, width = key_rows.shape
    half = width // 2
    chunks = tokens // CHUNK
    late = tokens - first_keys.shape[0]
    sizes = group_sizes(half // HEAD_DIM)
    out_shape = [pltpu.VMEM((n * HEAD_DIM, HEAD_DIM), F32) for n in sizes] + [
        pltpu.VMEM(((chunks - 1) * half, HEAD_DIM), BF16),
        pltpu.VMEM((late, half), BF16),
        pltpu.VMEM((late, half), BF16),
        pltpu.VMEM((tokens - late, half), BF16),
    ]
    results = pl.pallas_call(
        kept_kernel,
        in_specs=[SCALARS] + [ANYWHERE] * 3 + [WHOLE] * 2,
        out_specs=[WHOLE] * len(out_shape),
        out_shape=out_shape,
        scratch_shapes=[pltpu.SemaphoreType.DMA((chunks + late // CHUNK,))],
        compiler_params=params(8),
        cost_estimate=cost(tokens * width * HEAD_DIM, tokens * width),
        name="states",
    )(place, in_hbm(key_rows), in_hbm(values), in_hbm(queries), in_vmem(first_keys), in_vmem(first_vals))
    return results[: len(sizes)], results[len(sizes) :]


def write_weights(place_ref, session_ref, weight_ref):
    place = place_ref[0]
    core = place & 1
    chip = lax.shift_right_logical(place, 1)

    def flag(condition):
        return jnp.where(condition, 1.0, 0.0).astype(F32)

    def need(to, source):
        same = session_ref[2 * to] == session_ref[2 * source + 1]
        return flag(jnp.logical_and(source < to, same))

    even = core == 0
    rows = [flag(even), flag(core == 1)]
    if session_ref.shape[0] == 8:
        partner = jnp.where(even, chip ^ 1, chip ^ 2)
        to = jnp.where(even, chip ^ 2, chip ^ 1)
        rows += [need(to, chip), need(to, partner), need(chip, partner)]
    for r, value in enumerate(rows):
        weight_ref[r : r + 1, :] = jnp.full((1, HEAD_DIM), value, F32)


def half_heads(place_ref, mine, half):
    start = (place_ref[0] & 1 if mine else 1 - (place_ref[0] & 1)) * half
    return lambda h: pl.ds(pl.multiple_of(start + h * HEAD_DIM, HEAD_DIM), HEAD_DIM)


def chunk_in(refs, c):
    for ref in refs:
        chunks = ref.shape[0] // CHUNK
        if c < chunks:
            return ref, chunk(c)
        c -= chunks


def inner_body(chunks, waits, query_refs, key_refs, value_refs, before_ref, inner_refs, zero_ref, first_head=0):
    zero_ref[...] = jnp.zeros_like(zero_ref)
    rows_at = lax.broadcasted_iota(jnp.int32, (CHUNK, CHUNK), 0)
    cols_at = lax.broadcasted_iota(jnp.int32, (CHUNK, CHUNK), 1)
    causal = rows_at >= cols_at
    homes = [(ref, j) for ref in inner_refs for j in range(ref.shape[1] // HEAD_DIM)]
    heads = range(first_head, first_head + len(homes))
    half = key_refs[0].shape[1]
    for c in range(chunks):
        if c in waits:
            waits[c].wait()
        (query_ref, q), (key_ref, k), (value_ref, v) = (chunk_in(x, c) for x in (query_refs, key_refs, value_refs))
        scores = []
        for h in heads:
            full = dot_nt(query_ref[q, head(h)], key_ref[k, head(h)])
            scores.append(jnp.where(causal, full, 0.0).astype(BF16))
        for h, score, (inner_ref, j) in zip(heads, scores, homes):
            left, right = score, value_ref[v, head(h)]
            if c > 0:
                at = (c - 1) * half + h * HEAD_DIM
                left = jnp.concatenate([left, query_ref[q, head(h)]], axis=1)
                right = jnp.concatenate([right, before_ref[at : at + HEAD_DIM, :]], axis=0)
            inner_ref[chunk(c), head(j)] = dot_nn(left, right)


def mine_kernel(place_ref, query_ref, after_ref, first_queries, key_first, key_late, value_first, value_late,
                before_ref, late_queries, other_queries, *refs):
    *inner_refs, zero_ref, sems = refs
    chunks = other_queries.shape[0] // CHUNK
    early = first_queries.shape[0] // CHUNK
    copies = []
    fetch(copies, sems, place_ref, True, ((query_ref, late_queries),), range(early, chunks), early)
    fetch(copies, sems, place_ref, False, ((query_ref, other_queries),), range(chunks))
    waits = {c: copies[c - early] for c in range(early, chunks)}
    inner_body(
        chunks, waits, (first_queries, late_queries), (key_first, key_late), (value_first, value_late),
        before_ref, inner_refs, zero_ref,
    )
    for copy in copies[chunks - early :]:
        copy.wait()


def mine_inner(place, queries, first_queries, keys, vals, before, after, sizes):
    tokens, width = queries.shape
    half = width // 2
    late = tokens - first_queries.shape[0]
    out_shape = [pltpu.VMEM((late, half), BF16), pltpu.VMEM((tokens, half), BF16)]
    out_shape += [pltpu.VMEM((tokens, n * HEAD_DIM), F32) for n in sizes] + [pltpu.VMEM((1, HEAD_DIM), F32)]
    return pl.pallas_call(
        mine_kernel,
        in_specs=[SCALARS, ANYWHERE, ANYWHERE] + [WHOLE] * 6,
        out_specs=[WHOLE] * len(out_shape),
        out_shape=out_shape,
        scratch_shapes=[pltpu.SemaphoreType.DMA(((late + tokens) // CHUNK,))],
        compiler_params=params(8),
        cost_estimate=cost(tokens * half * 6 * CHUNK, 12 * tokens * half),
        name="inner",
    )(place, in_hbm(queries), after, *[in_vmem(x) for x in (first_queries, *keys, *vals, before)])


def other_kernel(first_head, after_ref, query_ref, key_ref, value_ref, before_ref, inner_ref, zero_ref):
    chunks = query_ref.shape[0] // CHUNK
    inner_body(chunks, {}, (query_ref,), (key_ref,), (value_ref,), before_ref, (inner_ref,), zero_ref, first_head)


def other_inner(queries, keys, vals, before, after, first_head, count):
    tokens = queries.shape[0]
    width = count * HEAD_DIM
    return pl.pallas_call(
        lambda *refs: other_kernel(first_head, *refs),
        in_specs=[ANYWHERE] + [WHOLE] * 4,
        out_specs=[WHOLE] * 2,
        out_shape=[pltpu.VMEM((tokens, width), F32), pltpu.VMEM((1, HEAD_DIM), F32)],
        compiler_params=params(8),
        cost_estimate=cost(tokens * width * 6 * CHUNK, 12 * tokens * width),
        name="inner",
    )(after, *[in_vmem(x) for x in (queries, keys, vals, before)])


def mix_kernel(parts, first_head, first, last, *refs):
    query_refs, (inner_ref, prefix_ref, *refs) = refs[:parts], refs[parts:]
    extra_ref, mixed_ref, result_ref = (None, *refs) if first else refs
    heads = range(inner_ref.shape[1] // HEAD_DIM)
    blocks = [prefix_ref[head(j), :].astype(BF16) for j in heads]
    for c in range(inner_ref.shape[0] // CHUNK):
        squares = None if first else extra_ref[chunk(c), :]
        query_ref, q = chunk_in(query_refs, c)
        for j in heads:
            mixed = inner_ref[chunk(c), head(j)] + dot_nn(query_ref[q, head(first_head + j)], blocks[j])
            square = mixed * mixed
            squares = square if squares is None else squares + square
            mixed_ref[chunk(c), head(j)] = mixed
        if last:
            result_ref[:, chunk(c)] = jnp.sum(jnp.transpose(squares), axis=0, keepdims=True)
        else:
            result_ref[chunk(c), :] = squares


def mix(queries, inner_group, prefix, squares, first_head, last):
    tokens = inner_group.shape[0]
    first = squares is None
    operands = [*queries, inner_group, prefix] + ([] if first else [squares])
    return pl.pallas_call(
        lambda *refs: mix_kernel(len(queries), first_head, first, last, *refs),
        in_specs=[WHOLE] * len(operands),
        out_specs=[WHOLE, WHOLE],
        out_shape=[
            pltpu.VMEM(inner_group.shape, F32),
            pltpu.VMEM((1, tokens) if last else (tokens, HEAD_DIM), F32),
        ],
        compiler_params=params(8),
        cost_estimate=cost(2 * tokens * prefix.size, 12 * inner_group.size),
        name="mix",
    )(*[in_vmem(x) for x in operands])


def gate_kernel(mine, place_ref, gate_ref, gain_ref, after_ref, *refs):
    *mixed_refs, gated_ref, zero_ref = refs
    tokens, half = gated_ref.shape
    zero_ref[...] = jnp.zeros_like(zero_ref)
    rows = HEAD_DIM
    columns_of = half_heads(place_ref, mine, half)
    homes = [(ref, j) for ref in mixed_refs for j in range(ref.shape[1] // HEAD_DIM)]

    def step(i, carry):
        at = pl.ds(pl.multiple_of(i * rows, rows), rows)
        for h, (mixed_ref, j) in enumerate(homes):
            gate = gate_ref[at, columns_of(h)].astype(F32)
            factor = (0.5 * gain_ref[:, columns_of(h)]) * (1.0 + jnp.tanh(0.5 * gate))
            gated_ref[at, head(h)] = mixed_ref[at, head(j)] * factor
        return carry

    lax.fori_loop(0, tokens // rows, step, 0)


def gated(place, mixed, gate_input, norm_gain, after, mine):
    tokens, width = gate_input.shape
    return pl.pallas_call(
        lambda *refs: gate_kernel(mine, *refs),
        in_specs=[SCALARS, WHOLE, WHOLE, ANYWHERE] + [WHOLE] * len(mixed),
        out_specs=[WHOLE, WHOLE],
        out_shape=[pltpu.VMEM((tokens, width // 2), F32), pltpu.VMEM((1, tokens), F32)],
        compiler_params=params(8),
        cost_estimate=cost(8 * tokens * width, 2 * tokens * width),
        name="gate",
    )(place, in_vmem(gate_input), norm_gain.reshape(1, width), after, *[in_vmem(x) for x in mixed])


def scale_kernel(features, place_ref, mine_ref, other_ref, power_ref, out_ref, mine_out, other_out, sems):
    tokens, half = mine_ref.shape
    rows = HEAD_DIM
    copies = []
    for c in range(tokens // rows):
        at = slice(c * rows, (c + 1) * rows)
        power = jnp.broadcast_to(power_ref[:, at], (HEAD_DIM, rows))
        factor = lax.rsqrt(jnp.transpose(power) / features + 1e-06)
        for j, (source, to) in enumerate(((mine_ref, mine_out), (other_ref, other_out))):
            for h in range(half // HEAD_DIM):
                to[at, head(h)] = (source[at, head(h)] * factor).astype(BF16)
            cols = columns(place_ref, j == 0, half)
            copies.append(pltpu.make_async_copy(to.at[at, :], out_ref.at[at, cols], sems.at[2 * c + j]))
            copies[-1].start()
    for copy in copies:
        copy.wait()


def scale(place, mine, other, power, features):
    tokens, half = mine.shape
    return pl.pallas_call(
        lambda *refs: scale_kernel(features, *refs),
        in_specs=[SCALARS, WHOLE, WHOLE, WHOLE],
        out_specs=ANYWHERE,
        out_shape=pltpu.HBM((tokens, 2 * half), BF16),
        scratch_shapes=[
            pltpu.VMEM((tokens, half), BF16),
            pltpu.VMEM((tokens, half), BF16),
            pltpu.SemaphoreType.DMA((2 * tokens // HEAD_DIM,)),
        ],
        compiler_params=params(8),
        cost_estimate=cost(4 * tokens * half, 4 * tokens * half),
        name="scale",
    )(place, in_vmem(mine), in_vmem(other), in_vmem(power))


def swap(count, bit):
    return [(i, i ^ bit) for i in range(count)]


def general_prefix(blocks, chip, session_of, chip_sum):
    total = chip_sum
    prefix = jnp.zeros_like(chip_sum)
    bit = 1
    while 2 * bit < blocks:
        there = lax.ppermute(total, "ctx", swap(blocks, 2 * bit))
        partner = chip ^ bit
        lower = partner < chip
        end_here = session_of[2 * (chip | (bit - 1)) + 1]
        end_there = session_of[2 * (partner | (bit - 1)) + 1]
        reaches = jnp.logical_and(lower, end_there == session_of[2 * chip])
        prefix = prefix + jnp.where(reaches, 1.0, 0.0) * there
        joined = jnp.where(end_here == end_there, 1.0, 0.0)
        total = jnp.where(lower, total + joined * there, joined * total + there)
        bit *= 2
    return prefix


def zero_after(x):
    def kernel(after_ref, zero_ref):
        zero_ref[...] = jnp.zeros_like(zero_ref)

    return pl.pallas_call(
        kernel,
        in_specs=[ANYWHERE],
        out_specs=WHOLE,
        out_shape=pltpu.VMEM((1, HEAD_DIM), F32),
        compiler_params=params(1),
        name="then",
    )(x)


def two_steps(sums, weight, between, beside):
    there = [lax.ppermute(x, "ctx", [(i, i ^ (2 if i % 2 == 0 else 4)) for i in range(8)]) for x in sums]
    zero = between(sums[0])
    onward = []
    for x, y in zip(sums, there):
        onward.append(weight[2:3] * x + weight[3:4] * y + zero)
        zero = zero_after(onward[-1])
    arrived = [lax.ppermute(x, "ctx", [(i, i ^ (5 if i % 2 == 0 else 3)) for i in range(8)]) for x in onward]
    zero = beside(onward[-1])
    return [weight[4:5] * x for x in there], [x + zero for x in arrived]


def on_device(blocks, features, queries, key_rows, values, gate_input, norm_gain, session_of):
    width = queries.shape[1]
    index = lax.axis_index("ctx").astype(jnp.int32)
    place = index.reshape(1)
    sizes = group_sizes(width // 2 // HEAD_DIM)
    starts = [sum(sizes[:g]) for g in range(GROUPS)]

    sent, sent_before, sent_keys, sent_vals, first_keys, first_vals, weight = sent_states(
        place, session_of, key_rows, values
    )
    got = lax.ppermute(sent, "ctx", swap(blocks, 1))
    kept, (kept_before, late_keys, late_vals, first_queries) = kept_states(
        place, key_rows, values, queries, first_keys, first_vals
    )
    got = [got[at * HEAD_DIM : (at + n) * HEAD_DIM] for at, n in zip(starts, sizes)]
    sums = [x + y for x, y in zip(kept, got)]
    inside, held = {}, {}

    def mine_inside(after):
        keys, vals = (first_keys, late_keys), (first_vals, late_vals)
        late_queries, other_queries, *inside[True], zero = mine_inner(
            place, queries, first_queries, keys, vals, kept_before, after, sizes
        )
        held[True], held[False] = (first_queries, late_queries), (other_queries,)
        return zero

    def other_inside(after, g=0):
        part, zero = other_inner(*held[False], sent_keys, sent_vals, sent_before, after, starts[g], sizes[g])
        inside.setdefault(False, []).append(part)
        return zero

    if blocks == 8:
        own, arrived = two_steps(sums, weight, mine_inside, other_inside)
    else:
        zero = other_inside(mine_inside(sums[0]))
        own = [general_prefix(blocks, index >> 1, session_of, x) + zero for x in sums]
        arrived = [jnp.zeros_like(x) for x in sums]
    even, odd = weight[0:1], weight[1:2]
    others = [lax.ppermute(x + even * k, "ctx", swap(blocks, 1)) for x, k in zip(own, kept)]

    mixed = {True: [], False: []}
    parts, backs = [], []
    squares = None

    def swap_part(g, zero):
        parts.append(arrived[g] + zero)
        backs.append(lax.ppermute(parts[g], "ctx", swap(blocks, 1)))
        return zero_after(parts[g])

    def mix_group(mine, zero, last=False):
        nonlocal squares
        g = len(mixed[mine])
        prefix = own[g] + odd * got[g] + backs[g] if mine else others[g] + parts[g]
        part, squares = mix(held[mine], inside[mine][g], prefix + zero, squares, starts[g], last)
        mixed[mine].append(part)
        return zero_after(squares)

    zero = swap_part(0, jnp.zeros((1, HEAD_DIM), F32))
    for g in range(1, GROUPS):
        zero = other_inside(parts[0], g) + zero
    for g in range(GROUPS):
        zero = mix_group(False, zero)
        if g + 1 < GROUPS:
            zero = swap_part(g + 1, zero)
        zero = mix_group(True, zero, g == GROUPS - 1)
    power = squares
    count = features // width

    def crossed(bit):
        pairs = [(c * count + z, (c ^ 1) * count + (z ^ bit)) for c in range(blocks) for z in range(count)]
        return lax.ppermute(power, ("ctx", "head"), pairs) + lax.ppermute(power, "ctx", swap(blocks, 1))

    gated_other, zero = gated(place, mixed[False], gate_input, norm_gain, power, False)
    power = crossed(1) + zero
    gated_mine, zero = gated(place, mixed[True], gate_input, norm_gain, power, True)
    power = crossed(2) + zero
    bit, swapped = 4, False
    while bit < count:
        power = crossed(bit)
        bit, swapped = 2 * bit, not swapped
    if swapped:
        power = lax.ppermute(power, "ctx", swap(blocks, 1))
    return scale(place, gated_mine, gated_other, power, features)


def solution(mesh):
    blocks = mesh.shape["ctx"]

    def whole(queries, key_rows, values, gate_input, norm_gain, session_of):
        features = queries.shape[1]
        return jax.shard_map(
            lambda *args: on_device(blocks, features, *args),
            mesh=mesh,
            in_specs=(
                P("ctx", "head"),
                P("ctx", "head"),
                P("ctx", "head"),
                P("ctx", "head"),
                P("head"),
                P(),
            ),
            out_specs=P("ctx", "head"),
            check_vma=False,
        )(queries, key_rows, values, gate_input, norm_gain, session_of)

    return whole
```

```python
import jax
import jax.numpy as jnp
from jax import lax
from jax.experimental import pallas as pl
from jax.experimental.pallas import tpu as pltpu
from jax.sharding import PartitionSpec as P

HEAD_DIM = 128
CHUNK = 256
GROUPS = 2
MIB = 1024 * 1024
F32 = jnp.float32
BF16 = jnp.bfloat16
WHOLE = pl.BlockSpec(memory_space=pltpu.VMEM)
SCALARS = pl.BlockSpec(memory_space=pltpu.SMEM)
ANYWHERE = pl.BlockSpec(memory_space=pl.ANY)


def params(mib):
    return pltpu.CompilerParams(vmem_limit_bytes=mib * MIB)


def in_hbm(x):
    return pltpu.with_memory_space_constraint(x, pltpu.HBM)


def in_vmem(x):
    return pltpu.with_memory_space_constraint(x, pltpu.VMEM)


def cost(flops, bytes_accessed):
    return pl.CostEstimate(flops=flops, bytes_accessed=bytes_accessed, transcendentals=0)


def dot_tn(a, b):
    return lax.dot_general(a, b, (((0,), (0,)), ((), ())), preferred_element_type=F32)


def dot_nt(a, b):
    return lax.dot_general(a, b, (((1,), (1,)), ((), ())), preferred_element_type=F32)


def dot_nn(a, b):
    return lax.dot_general(a, b, (((1,), (0,)), ((), ())), preferred_element_type=F32)


def head(h):
    return slice(h * HEAD_DIM, (h + 1) * HEAD_DIM)


def chunk(c):
    return slice(c * CHUNK, (c + 1) * CHUNK)


def columns(place_ref, mine, half):
    core = place_ref[0] & 1
    return pl.ds(pl.multiple_of((core if mine else 1 - core) * half, half), half)


def group_sizes(heads):
    return [(heads + GROUPS - 1 - g) // GROUPS for g in range(GROUPS)]


def fetch(copies, sems, place_ref, mine, pairs, chunks, base=0):
    for c in chunks:
        for source, to in pairs:
            cols = columns(place_ref, mine, to.shape[1])
            rows = slice((c - base) * CHUNK, (c - base + 1) * CHUNK)
            copies.append(pltpu.make_async_copy(source.at[chunk(c), cols], to.at[rows, :], sems.at[len(copies)]))
            copies[-1].start()


def add_chunk(c, keys, vals, rows, state_refs, before_ref):
    half = keys.shape[1]
    h = 0
    for state_ref in state_refs:
        for j in range(state_ref.shape[0] // HEAD_DIM):
            new = dot_tn(keys[rows, head(h)], vals[rows, head(h)])
            if c == 0:
                state_ref[head(j), :] = new
            else:
                old = state_ref[head(j), :]
                at = (c - 1) * half + h * HEAD_DIM
                before_ref[at : at + HEAD_DIM, :] = old.astype(BF16)
                state_ref[head(j), :] = old + new
            h += 1


def sent_kernel(place_ref, session_ref, key_ref, value_ref, state_ref, before_ref, keys, vals,
                next_keys, next_vals, weight_ref, sems, sessions, session_sem):
    chunks = keys.shape[0] // CHUNK
    early = next_keys.shape[0] // CHUNK
    session_copy = pltpu.make_async_copy(session_ref, sessions, session_sem)
    session_copy.start()
    copies = []
    fetch(copies, sems, place_ref, False, ((key_ref, keys), (value_ref, vals)), range(chunks))
    fetch(copies, sems, place_ref, True, ((key_ref, next_keys), (value_ref, next_vals)), range(early))
    session_copy.wait()
    write_weights(place_ref, sessions, weight_ref)
    for c in range(chunks):
        copies[2 * c].wait()
        copies[2 * c + 1].wait()
        add_chunk(c, keys, vals, chunk(c), [state_ref], before_ref)
    for copy in copies[2 * chunks :]:
        copy.wait()


def sent_states(place, session_of, key_rows, values):
    tokens, width = key_rows.shape
    half = width // 2
    chunks = tokens // CHUNK
    early = chunks // 2
    return pl.pallas_call(
        sent_kernel,
        in_specs=[SCALARS] + [ANYWHERE] * 3,
        out_specs=[WHOLE] * 7,
        out_shape=[
            pltpu.VMEM((half, HEAD_DIM), F32),
            pltpu.VMEM(((chunks - 1) * half, HEAD_DIM), BF16),
            pltpu.VMEM((tokens, half), BF16),
            pltpu.VMEM((tokens, half), BF16),
            pltpu.VMEM((early * CHUNK, half), BF16),
            pltpu.VMEM((early * CHUNK, half), BF16),
            pltpu.VMEM((8, HEAD_DIM), F32),
        ],
        scratch_shapes=[
            pltpu.SemaphoreType.DMA((2 * chunks + 2 * early,)),
            pltpu.SMEM(session_of.shape, jnp.int32),
            pltpu.SemaphoreType.DMA(()),
        ],
        compiler_params=params(8),
        cost_estimate=cost(tokens * width * HEAD_DIM, 3 * tokens * width),
        name="states",
    )(place, in_hbm(session_of), in_hbm(key_rows), in_hbm(values))


def kept_kernel(place_ref, key_ref, value_ref, query_ref, first_keys, first_vals, *refs):
    *state_refs, before_ref, keys, vals, queries, sems = refs
    early = first_keys.shape[0] // CHUNK
    chunks = early + keys.shape[0] // CHUNK
    copies = []
    fetch(copies, sems, place_ref, True, ((key_ref, keys), (value_ref, vals)), range(early, chunks), early)
    fetch(copies, sems, place_ref, True, ((query_ref, queries),), range(queries.shape[0] // CHUNK))
    for c in range(early):
        add_chunk(c, first_keys, first_vals, chunk(c), state_refs, before_ref)
    for c in range(early, chunks):
        copies[2 * (c - early)].wait()
        copies[2 * (c - early) + 1].wait()
        add_chunk(c, keys, vals, chunk(c - early), state_refs, before_ref)
    for copy in copies[2 * (chunks - early) :]:
        copy.wait()


def kept_states(place, key_rows, values, queries, first_keys, first_vals):
    tokens, width = key_rows.shape
    half = width // 2
    chunks = tokens // CHUNK
    late = tokens - first_keys.shape[0]
    sizes = group_sizes(half // HEAD_DIM)
    out_shape = [pltpu.VMEM((n * HEAD_DIM, HEAD_DIM), F32) for n in sizes] + [
        pltpu.VMEM(((chunks - 1) * half, HEAD_DIM), BF16),
        pltpu.VMEM((late, half), BF16),
        pltpu.VMEM((late, half), BF16),
        pltpu.VMEM((CHUNK, half), BF16),
    ]
    results = pl.pallas_call(
        kept_kernel,
        in_specs=[SCALARS] + [ANYWHERE] * 3 + [WHOLE] * 2,
        out_specs=[WHOLE] * len(out_shape),
        out_shape=out_shape,
        scratch_shapes=[pltpu.SemaphoreType.DMA((2 * late // CHUNK + 1,))],
        compiler_params=params(8),
        cost_estimate=cost(tokens * width * HEAD_DIM, tokens * width),
        name="states",
    )(place, in_hbm(key_rows), in_hbm(values), in_hbm(queries), in_vmem(first_keys), in_vmem(first_vals))
    return results[: len(sizes)], results[len(sizes) :]


def write_weights(place_ref, session_ref, weight_ref):
    place = place_ref[0]
    core = place & 1
    chip = lax.shift_right_logical(place, 1)

    def flag(condition):
        return jnp.where(condition, 1.0, 0.0).astype(F32)

    def need(to, source):
        same = session_ref[2 * to] == session_ref[2 * source + 1]
        return flag(jnp.logical_and(source < to, same))

    even = core == 0
    rows = [flag(even), flag(core == 1)]
    if session_ref.shape[0] == 8:
        partner = jnp.where(even, chip ^ 1, chip ^ 2)
        to = jnp.where(even, chip ^ 2, chip ^ 1)
        rows += [need(to, chip), need(to, partner), need(chip, partner)]
    for r, value in enumerate(rows):
        weight_ref[r : r + 1, :] = jnp.full((1, HEAD_DIM), value, F32)


def half_heads(place_ref, mine, half):
    start = (place_ref[0] & 1 if mine else 1 - (place_ref[0] & 1)) * half
    return lambda h: pl.ds(pl.multiple_of(start + h * HEAD_DIM, HEAD_DIM), HEAD_DIM)


def chunk_in(refs, c):
    for ref in refs:
        chunks = ref.shape[0] // CHUNK
        if c < chunks:
            return ref, chunk(c)
        c -= chunks


def inner_body(chunks, waits, query_refs, key_refs, value_refs, before_ref, inner_refs, zero_ref, first_head=0):
    zero_ref[...] = jnp.zeros_like(zero_ref)
    rows_at = lax.broadcasted_iota(jnp.int32, (CHUNK, CHUNK), 0)
    cols_at = lax.broadcasted_iota(jnp.int32, (CHUNK, CHUNK), 1)
    causal = rows_at >= cols_at
    homes = [(ref, j) for ref in inner_refs for j in range(ref.shape[1] // HEAD_DIM)]
    heads = range(first_head, first_head + len(homes))
    half = key_refs[0].shape[1]
    for c in range(chunks):
        if c in waits:
            waits[c].wait()
        (query_ref, q), (key_ref, k), (value_ref, v) = (chunk_in(x, c) for x in (query_refs, key_refs, value_refs))
        scores = []
        for h in heads:
            full = dot_nt(query_ref[q, head(h)], key_ref[k, head(h)])
            scores.append(jnp.where(causal, full, 0.0).astype(BF16))
        for h, score, (inner_ref, j) in zip(heads, scores, homes):
            left, right = score, value_ref[v, head(h)]
            if c > 0:
                at = (c - 1) * half + h * HEAD_DIM
                left = jnp.concatenate([left, query_ref[q, head(h)]], axis=1)
                right = jnp.concatenate([right, before_ref[at : at + HEAD_DIM, :]], axis=0)
            inner_ref[chunk(c), head(j)] = dot_nn(left, right)


def mine_kernel(place_ref, query_ref, after_ref, first_queries, key_first, key_late, value_first, value_late,
                before_ref, late_queries, other_queries, *refs):
    *inner_refs, zero_ref, sems = refs
    chunks = other_queries.shape[0] // CHUNK
    early = first_queries.shape[0] // CHUNK
    copies = []
    fetch(copies, sems, place_ref, True, ((query_ref, late_queries),), range(early, chunks), early)
    fetch(copies, sems, place_ref, False, ((query_ref, other_queries),), range(chunks))
    waits = {c: copies[c - early] for c in range(early, chunks)}
    inner_body(
        chunks, waits, (first_queries, late_queries), (key_first, key_late), (value_first, value_late),
        before_ref, inner_refs, zero_ref,
    )
    for copy in copies[chunks - early :]:
        copy.wait()


def mine_inner(place, queries, first_queries, keys, vals, before, after, sizes):
    tokens, width = queries.shape
    half = width // 2
    late = tokens - first_queries.shape[0]
    out_shape = [pltpu.VMEM((late, half), BF16), pltpu.VMEM((tokens, half), BF16)]
    out_shape += [pltpu.VMEM((tokens, n * HEAD_DIM), F32) for n in sizes] + [pltpu.VMEM((1, HEAD_DIM), F32)]
    return pl.pallas_call(
        mine_kernel,
        in_specs=[SCALARS, ANYWHERE, ANYWHERE] + [WHOLE] * 6,
        out_specs=[WHOLE] * len(out_shape),
        out_shape=out_shape,
        scratch_shapes=[pltpu.SemaphoreType.DMA(((late + tokens) // CHUNK,))],
        compiler_params=params(8),
        cost_estimate=cost(tokens * half * 6 * CHUNK, 12 * tokens * half),
        name="inner",
    )(place, in_hbm(queries), after, *[in_vmem(x) for x in (first_queries, *keys, *vals, before)])


def other_kernel(first_head, after_ref, query_ref, key_ref, value_ref, before_ref, inner_ref, zero_ref):
    chunks = query_ref.shape[0] // CHUNK
    inner_body(chunks, {}, (query_ref,), (key_ref,), (value_ref,), before_ref, (inner_ref,), zero_ref, first_head)


def other_inner(queries, keys, vals, before, after, first_head, count):
    tokens = queries.shape[0]
    width = count * HEAD_DIM
    return pl.pallas_call(
        lambda *refs: other_kernel(first_head, *refs),
        in_specs=[ANYWHERE] + [WHOLE] * 4,
        out_specs=[WHOLE] * 2,
        out_shape=[pltpu.VMEM((tokens, width), F32), pltpu.VMEM((1, HEAD_DIM), F32)],
        compiler_params=params(8),
        cost_estimate=cost(tokens * width * 6 * CHUNK, 12 * tokens * width),
        name="inner",
    )(after, *[in_vmem(x) for x in (queries, keys, vals, before)])


def mix_kernel(parts, first_head, first, last, *refs):
    query_refs, (inner_ref, prefix_ref, *refs) = refs[:parts], refs[parts:]
    extra_ref, mixed_ref, result_ref = (None, *refs) if first else refs
    heads = range(inner_ref.shape[1] // HEAD_DIM)
    blocks = [prefix_ref[head(j), :].astype(BF16) for j in heads]
    for c in range(inner_ref.shape[0] // CHUNK):
        squares = None if first else extra_ref[chunk(c), :]
        query_ref, q = chunk_in(query_refs, c)
        for j in heads:
            mixed = inner_ref[chunk(c), head(j)] + dot_nn(query_ref[q, head(first_head + j)], blocks[j])
            square = mixed * mixed
            squares = square if squares is None else squares + square
            mixed_ref[chunk(c), head(j)] = mixed
        if last:
            result_ref[:, chunk(c)] = jnp.sum(jnp.transpose(squares), axis=0, keepdims=True)
        else:
            result_ref[chunk(c), :] = squares


def mix(queries, inner_group, prefix, squares, first_head, last):
    tokens = inner_group.shape[0]
    first = squares is None
    operands = [*queries, inner_group, prefix] + ([] if first else [squares])
    return pl.pallas_call(
        lambda *refs: mix_kernel(len(queries), first_head, first, last, *refs),
        in_specs=[WHOLE] * len(operands),
        out_specs=[WHOLE, WHOLE],
        out_shape=[
            pltpu.VMEM(inner_group.shape, F32),
            pltpu.VMEM((1, tokens) if last else (tokens, HEAD_DIM), F32),
        ],
        compiler_params=params(8),
        cost_estimate=cost(2 * tokens * prefix.size, 12 * inner_group.size),
        name="mix",
    )(*[in_vmem(x) for x in operands])


def gate_kernel(mine, place_ref, gate_ref, gain_ref, after_ref, *refs):
    *mixed_refs, gated_ref, zero_ref = refs
    tokens, half = gated_ref.shape
    zero_ref[...] = jnp.zeros_like(zero_ref)
    rows = HEAD_DIM
    columns_of = half_heads(place_ref, mine, half)
    homes = [(ref, j) for ref in mixed_refs for j in range(ref.shape[1] // HEAD_DIM)]

    def step(i, carry):
        at = pl.ds(pl.multiple_of(i * rows, rows), rows)
        for h, (mixed_ref, j) in enumerate(homes):
            gate = gate_ref[at, columns_of(h)].astype(F32)
            factor = (0.5 * gain_ref[:, columns_of(h)]) * (1.0 + jnp.tanh(0.5 * gate))
            gated_ref[at, head(h)] = mixed_ref[at, head(j)] * factor
        return carry

    lax.fori_loop(0, tokens // rows, step, 0)


def gated(place, mixed, gate_input, norm_gain, after, mine):
    tokens, width = gate_input.shape
    return pl.pallas_call(
        lambda *refs: gate_kernel(mine, *refs),
        in_specs=[SCALARS, WHOLE, WHOLE, ANYWHERE] + [WHOLE] * len(mixed),
        out_specs=[WHOLE, WHOLE],
        out_shape=[pltpu.VMEM((tokens, width // 2), F32), pltpu.VMEM((1, tokens), F32)],
        compiler_params=params(8),
        cost_estimate=cost(8 * tokens * width, 2 * tokens * width),
        name="gate",
    )(place, in_vmem(gate_input), norm_gain.reshape(1, width), after, *[in_vmem(x) for x in mixed])


def scale_kernel(features, place_ref, mine_ref, other_ref, power_ref, out_ref, buffer, sems):
    tokens, half = mine_ref.shape
    rows = HEAD_DIM
    copies = []
    for c in range(tokens // rows):
        at = slice(c * rows, (c + 1) * rows)
        power = jnp.broadcast_to(power_ref[:, at], (HEAD_DIM, rows))
        factor = lax.rsqrt(jnp.transpose(power) / features + 1e-06)
        for mine, source in ((True, mine_ref), (False, other_ref)):
            columns_of = half_heads(place_ref, mine, half)
            for h in range(half // HEAD_DIM):
                buffer[at, columns_of(h)] = (source[at, head(h)] * factor).astype(BF16)
        copies.append(pltpu.make_async_copy(buffer.at[at, :], out_ref.at[at, :], sems.at[c]))
        copies[-1].start()
    for copy in copies:
        copy.wait()


def scale(place, mine, other, power, features):
    tokens, half = mine.shape
    return pl.pallas_call(
        lambda *refs: scale_kernel(features, *refs),
        in_specs=[SCALARS, WHOLE, WHOLE, WHOLE],
        out_specs=ANYWHERE,
        out_shape=pltpu.HBM((tokens, 2 * half), BF16),
        scratch_shapes=[pltpu.VMEM((tokens, 2 * half), BF16), pltpu.SemaphoreType.DMA((tokens // HEAD_DIM,))],
        compiler_params=params(8),
        cost_estimate=cost(4 * tokens * half, 4 * tokens * half),
        name="scale",
    )(place, in_vmem(mine), in_vmem(other), in_vmem(power))


def swap(count, bit):
    return [(i, i ^ bit) for i in range(count)]


def general_prefix(blocks, chip, session_of, chip_sum):
    total = chip_sum
    prefix = jnp.zeros_like(chip_sum)
    bit = 1
    while 2 * bit < blocks:
        there = lax.ppermute(total, "ctx", swap(blocks, 2 * bit))
        partner = chip ^ bit
        lower = partner < chip
        end_here = session_of[2 * (chip | (bit - 1)) + 1]
        end_there = session_of[2 * (partner | (bit - 1)) + 1]
        reaches = jnp.logical_and(lower, end_there == session_of[2 * chip])
        prefix = prefix + jnp.where(reaches, 1.0, 0.0) * there
        joined = jnp.where(end_here == end_there, 1.0, 0.0)
        total = jnp.where(lower, total + joined * there, joined * total + there)
        bit *= 2
    return prefix


def zero_after(x):
    def kernel(after_ref, zero_ref):
        zero_ref[...] = jnp.zeros_like(zero_ref)

    return pl.pallas_call(
        kernel,
        in_specs=[ANYWHERE],
        out_specs=WHOLE,
        out_shape=pltpu.VMEM((1, HEAD_DIM), F32),
        compiler_params=params(1),
        name="then",
    )(x)


def two_steps(sums, weight, between, beside):
    there = [lax.ppermute(x, "ctx", [(i, i ^ (2 if i % 2 == 0 else 4)) for i in range(8)]) for x in sums]
    zero = between(sums[0])
    onward = []
    for x, y in zip(sums, there):
        onward.append(weight[2:3] * x + weight[3:4] * y + zero)
        zero = zero_after(onward[-1])
    arrived = [lax.ppermute(x, "ctx", [(i, i ^ (5 if i % 2 == 0 else 3)) for i in range(8)]) for x in onward]
    zero = beside(onward[-1])
    return [weight[4:5] * x for x in there], [x + zero for x in arrived]


def on_device(blocks, features, queries, key_rows, values, gate_input, norm_gain, session_of):
    width = queries.shape[1]
    index = lax.axis_index("ctx").astype(jnp.int32)
    place = index.reshape(1)
    sizes = group_sizes(width // 2 // HEAD_DIM)
    starts = [sum(sizes[:g]) for g in range(GROUPS)]

    sent, sent_before, sent_keys, sent_vals, first_keys, first_vals, weight = sent_states(
        place, session_of, key_rows, values
    )
    got = lax.ppermute(sent, "ctx", swap(blocks, 1))
    kept, (kept_before, late_keys, late_vals, first_queries) = kept_states(
        place, key_rows, values, queries, first_keys, first_vals
    )
    got = [got[at * HEAD_DIM : (at + n) * HEAD_DIM] for at, n in zip(starts, sizes)]
    sums = [x + y for x, y in zip(kept, got)]
    inside, held = {}, {}

    def mine_inside(after):
        keys, vals = (first_keys, late_keys), (first_vals, late_vals)
        late_queries, other_queries, *inside[True], zero = mine_inner(
            place, queries, first_queries, keys, vals, kept_before, after, sizes
        )
        held[True], held[False] = (first_queries, late_queries), (other_queries,)
        return zero

    def other_inside(after, g=0):
        part, zero = other_inner(*held[False], sent_keys, sent_vals, sent_before, after, starts[g], sizes[g])
        inside.setdefault(False, []).append(part)
        return zero

    if blocks == 8:
        own, arrived = two_steps(sums, weight, mine_inside, other_inside)
    else:
        zero = other_inside(mine_inside(sums[0]))
        own = [general_prefix(blocks, index >> 1, session_of, x) + zero for x in sums]
        arrived = [jnp.zeros_like(x) for x in sums]
    even, odd = weight[0:1], weight[1:2]
    others = [lax.ppermute(x + even * k, "ctx", swap(blocks, 1)) for x, k in zip(own, kept)]

    mixed = {True: [], False: []}
    parts, backs = [], []
    squares = None

    def swap_part(g, zero):
        parts.append(arrived[g] + zero)
        backs.append(lax.ppermute(parts[g], "ctx", swap(blocks, 1)))
        return zero_after(parts[g])

    def mix_group(mine, zero, last=False):
        nonlocal squares
        g = len(mixed[mine])
        prefix = own[g] + odd * got[g] + backs[g] if mine else others[g] + parts[g]
        part, squares = mix(held[mine], inside[mine][g], prefix + zero, squares, starts[g], last)
        mixed[mine].append(part)
        return zero_after(squares)

    zero = swap_part(0, jnp.zeros((1, HEAD_DIM), F32))
    for g in range(1, GROUPS):
        zero = other_inside(parts[0], g) + zero
    for g in range(GROUPS):
        zero = mix_group(False, zero)
        if g + 1 < GROUPS:
            zero = swap_part(g + 1, zero)
        zero = mix_group(True, zero, g == GROUPS - 1)
    power = squares
    count = features // width

    def crossed(bit):
        pairs = [(c * count + z, (c ^ 1) * count + (z ^ bit)) for c in range(blocks) for z in range(count)]
        return lax.ppermute(power, ("ctx", "head"), pairs) + lax.ppermute(power, "ctx", swap(blocks, 1))

    gated_other, zero = gated(place, mixed[False], gate_input, norm_gain, power, False)
    power = crossed(1) + zero
    gated_mine, zero = gated(place, mixed[True], gate_input, norm_gain, power, True)
    power = crossed(2) + zero
    bit, swapped = 4, False
    while bit < count:
        power = crossed(bit)
        bit, swapped = 2 * bit, not swapped
    if swapped:
        power = lax.ppermute(power, "ctx", swap(blocks, 1))
    return scale(place, gated_mine, gated_other, power, features)


def solution(mesh):
    blocks = mesh.shape["ctx"]

    def whole(queries, key_rows, values, gate_input, norm_gain, session_of):
        features = queries.shape[1]
        return jax.shard_map(
            lambda *args: on_device(blocks, features, *args),
            mesh=mesh,
            in_specs=(
                P("ctx", "head"),
                P("ctx", "head"),
                P("ctx", "head"),
                P("ctx", "head"),
                P("head"),
                P(),
            ),
            out_specs=P("ctx", "head"),
            check_vma=False,
        )(queries, key_rows, values, gate_input, norm_gain, session_of)

    return whole
```

```python
import jax
import jax.numpy as jnp
from jax import lax
from jax.experimental import pallas as pl
from jax.experimental.pallas import tpu as pltpu
from jax.sharding import PartitionSpec as P

HEAD_DIM = 128
CHUNK = 256
GROUPS = 2
MIB = 1024 * 1024
F32 = jnp.float32
BF16 = jnp.bfloat16
WHOLE = pl.BlockSpec(memory_space=pltpu.VMEM)
SCALARS = pl.BlockSpec(memory_space=pltpu.SMEM)
ANYWHERE = pl.BlockSpec(memory_space=pl.ANY)


def params(mib):
    return pltpu.CompilerParams(vmem_limit_bytes=mib * MIB)


def in_hbm(x):
    return pltpu.with_memory_space_constraint(x, pltpu.HBM)


def in_vmem(x):
    return pltpu.with_memory_space_constraint(x, pltpu.VMEM)


def cost(flops, bytes_accessed):
    return pl.CostEstimate(flops=flops, bytes_accessed=bytes_accessed, transcendentals=0)


def dot_tn(a, b):
    return lax.dot_general(a, b, (((0,), (0,)), ((), ())), preferred_element_type=F32)


def dot_nt(a, b):
    return lax.dot_general(a, b, (((1,), (1,)), ((), ())), preferred_element_type=F32)


def dot_nn(a, b):
    return lax.dot_general(a, b, (((1,), (0,)), ((), ())), preferred_element_type=F32)


def head(h):
    return slice(h * HEAD_DIM, (h + 1) * HEAD_DIM)


def chunk(c):
    return slice(c * CHUNK, (c + 1) * CHUNK)


def columns(place_ref, mine, half):
    core = place_ref[0] & 1
    return pl.ds(pl.multiple_of((core if mine else 1 - core) * half, half), half)


def group_sizes(heads):
    return [(heads + GROUPS - 1 - g) // GROUPS for g in range(GROUPS)]


def fetch(copies, sems, place_ref, mine, pairs, chunks, base=0):
    for c in chunks:
        for source, to in pairs:
            cols = columns(place_ref, mine, to.shape[1])
            rows = slice((c - base) * CHUNK, (c - base + 1) * CHUNK)
            copies.append(pltpu.make_async_copy(source.at[chunk(c), cols], to.at[rows, :], sems.at[len(copies)]))
            copies[-1].start()


def add_chunk(c, keys, vals, rows, state_refs, before_ref):
    half = keys.shape[1]
    h = 0
    for state_ref in state_refs:
        for j in range(state_ref.shape[0] // HEAD_DIM):
            new = dot_tn(keys[rows, head(h)], vals[rows, head(h)])
            if c == 0:
                state_ref[head(j), :] = new
            else:
                old = state_ref[head(j), :]
                at = (c - 1) * half + h * HEAD_DIM
                before_ref[at : at + HEAD_DIM, :] = old.astype(BF16)
                state_ref[head(j), :] = old + new
            h += 1


def sent_kernel(place_ref, session_ref, key_ref, value_ref, state_ref, before_ref, keys, vals,
                next_keys, next_vals, weight_ref, sems, sessions, session_sem):
    chunks = keys.shape[0] // CHUNK
    early = next_keys.shape[0] // CHUNK
    session_copy = pltpu.make_async_copy(session_ref, sessions, session_sem)
    session_copy.start()
    copies = []
    fetch(copies, sems, place_ref, False, ((key_ref, keys), (value_ref, vals)), range(chunks))
    fetch(copies, sems, place_ref, True, ((key_ref, next_keys), (value_ref, next_vals)), range(early))
    session_copy.wait()
    write_weights(place_ref, sessions, weight_ref)
    for c in range(chunks):
        copies[2 * c].wait()
        copies[2 * c + 1].wait()
        add_chunk(c, keys, vals, chunk(c), [state_ref], before_ref)
    for copy in copies[2 * chunks :]:
        copy.wait()


def sent_states(place, session_of, key_rows, values):
    tokens, width = key_rows.shape
    half = width // 2
    chunks = tokens // CHUNK
    early = chunks // 2
    return pl.pallas_call(
        sent_kernel,
        in_specs=[SCALARS] + [ANYWHERE] * 3,
        out_specs=[WHOLE] * 7,
        out_shape=[
            pltpu.VMEM((half, HEAD_DIM), F32),
            pltpu.VMEM(((chunks - 1) * half, HEAD_DIM), BF16),
            pltpu.VMEM((tokens, half), BF16),
            pltpu.VMEM((tokens, half), BF16),
            pltpu.VMEM((early * CHUNK, half), BF16),
            pltpu.VMEM((early * CHUNK, half), BF16),
            pltpu.VMEM((8, HEAD_DIM), F32),
        ],
        scratch_shapes=[
            pltpu.SemaphoreType.DMA((2 * chunks + 2 * early,)),
            pltpu.SMEM(session_of.shape, jnp.int32),
            pltpu.SemaphoreType.DMA(()),
        ],
        compiler_params=params(8),
        cost_estimate=cost(tokens * width * HEAD_DIM, 3 * tokens * width),
        name="states",
    )(place, in_hbm(session_of), in_hbm(key_rows), in_hbm(values))


def kept_kernel(place_ref, key_ref, value_ref, query_ref, first_keys, first_vals, *refs):
    *state_refs, before_ref, keys, vals, queries, sems = refs
    early = first_keys.shape[0] // CHUNK
    chunks = early + keys.shape[0] // CHUNK
    copies = []
    fetch(copies, sems, place_ref, True, ((key_ref, keys), (value_ref, vals)), range(early, chunks), early)
    fetch(copies, sems, place_ref, True, ((query_ref, queries),), range(queries.shape[0] // CHUNK))
    for c in range(early):
        add_chunk(c, first_keys, first_vals, chunk(c), state_refs, before_ref)
    for c in range(early, chunks):
        copies[2 * (c - early)].wait()
        copies[2 * (c - early) + 1].wait()
        add_chunk(c, keys, vals, chunk(c - early), state_refs, before_ref)
    for copy in copies[2 * (chunks - early) :]:
        copy.wait()


def kept_states(place, key_rows, values, queries, first_keys, first_vals):
    tokens, width = key_rows.shape
    half = width // 2
    chunks = tokens // CHUNK
    late = tokens - first_keys.shape[0]
    sizes = group_sizes(half // HEAD_DIM)
    out_shape = [pltpu.VMEM((n * HEAD_DIM, HEAD_DIM), F32) for n in sizes] + [
        pltpu.VMEM(((chunks - 1) * half, HEAD_DIM), BF16),
        pltpu.VMEM((late, half), BF16),
        pltpu.VMEM((late, half), BF16),
        pltpu.VMEM((CHUNK, half), BF16),
    ]
    results = pl.pallas_call(
        kept_kernel,
        in_specs=[SCALARS] + [ANYWHERE] * 3 + [WHOLE] * 2,
        out_specs=[WHOLE] * len(out_shape),
        out_shape=out_shape,
        scratch_shapes=[pltpu.SemaphoreType.DMA((2 * late // CHUNK + 1,))],
        compiler_params=params(8),
        cost_estimate=cost(tokens * width * HEAD_DIM, tokens * width),
        name="states",
    )(place, in_hbm(key_rows), in_hbm(values), in_hbm(queries), in_vmem(first_keys), in_vmem(first_vals))
    return results[: len(sizes)], results[len(sizes) :]


def write_weights(place_ref, session_ref, weight_ref):
    place = place_ref[0]
    core = place & 1
    chip = lax.shift_right_logical(place, 1)

    def flag(condition):
        return jnp.where(condition, 1.0, 0.0).astype(F32)

    def need(to, source):
        same = session_ref[2 * to] == session_ref[2 * source + 1]
        return flag(jnp.logical_and(source < to, same))

    even = core == 0
    rows = [flag(even), flag(core == 1)]
    if session_ref.shape[0] == 8:
        partner = jnp.where(even, chip ^ 1, chip ^ 2)
        to = jnp.where(even, chip ^ 2, chip ^ 1)
        rows += [need(to, chip), need(to, partner), need(chip, partner)]
    for r, value in enumerate(rows):
        weight_ref[r : r + 1, :] = jnp.full((1, HEAD_DIM), value, F32)


def half_heads(place_ref, mine, half):
    start = (place_ref[0] & 1 if mine else 1 - (place_ref[0] & 1)) * half
    return lambda h: pl.ds(pl.multiple_of(start + h * HEAD_DIM, HEAD_DIM), HEAD_DIM)


def chunk_in(refs, c):
    for ref in refs:
        chunks = ref.shape[0] // CHUNK
        if c < chunks:
            return ref, chunk(c)
        c -= chunks


def inner_body(chunks, waits, query_refs, key_refs, value_refs, before_ref, inner_refs, zero_ref, first_head=0):
    zero_ref[...] = jnp.zeros_like(zero_ref)
    rows_at = lax.broadcasted_iota(jnp.int32, (CHUNK, CHUNK), 0)
    cols_at = lax.broadcasted_iota(jnp.int32, (CHUNK, CHUNK), 1)
    causal = rows_at >= cols_at
    homes = [(ref, j) for ref in inner_refs for j in range(ref.shape[1] // HEAD_DIM)]
    heads = range(first_head, first_head + len(homes))
    half = key_refs[0].shape[1]
    for c in range(chunks):
        if c in waits:
            waits[c].wait()
        (query_ref, q), (key_ref, k), (value_ref, v) = (chunk_in(x, c) for x in (query_refs, key_refs, value_refs))
        scores = []
        for h in heads:
            full = dot_nt(query_ref[q, head(h)], key_ref[k, head(h)])
            scores.append(jnp.where(causal, full, 0.0).astype(BF16))
        for h, score, (inner_ref, j) in zip(heads, scores, homes):
            left, right = score, value_ref[v, head(h)]
            if c > 0:
                at = (c - 1) * half + h * HEAD_DIM
                left = jnp.concatenate([left, query_ref[q, head(h)]], axis=1)
                right = jnp.concatenate([right, before_ref[at : at + HEAD_DIM, :]], axis=0)
            inner_ref[chunk(c), head(j)] = dot_nn(left, right)


def mine_kernel(place_ref, query_ref, after_ref, first_queries, key_first, key_late, value_first, value_late,
                before_ref, late_queries, other_queries, *refs):
    *inner_refs, zero_ref, sems = refs
    chunks = other_queries.shape[0] // CHUNK
    early = first_queries.shape[0] // CHUNK
    copies = []
    fetch(copies, sems, place_ref, True, ((query_ref, late_queries),), range(early, chunks), early)
    fetch(copies, sems, place_ref, False, ((query_ref, other_queries),), range(chunks))
    waits = {c: copies[c - early] for c in range(early, chunks)}
    inner_body(
        chunks, waits, (first_queries, late_queries), (key_first, key_late), (value_first, value_late),
        before_ref, inner_refs, zero_ref,
    )
    for copy in copies[chunks - early :]:
        copy.wait()


def mine_inner(place, queries, first_queries, keys, vals, before, after, sizes):
    tokens, width = queries.shape
    half = width // 2
    late = tokens - first_queries.shape[0]
    out_shape = [pltpu.VMEM((late, half), BF16), pltpu.VMEM((tokens, half), BF16)]
    out_shape += [pltpu.VMEM((tokens, n * HEAD_DIM), F32) for n in sizes] + [pltpu.VMEM((1, HEAD_DIM), F32)]
    return pl.pallas_call(
        mine_kernel,
        in_specs=[SCALARS, ANYWHERE, ANYWHERE] + [WHOLE] * 6,
        out_specs=[WHOLE] * len(out_shape),
        out_shape=out_shape,
        scratch_shapes=[pltpu.SemaphoreType.DMA(((late + tokens) // CHUNK,))],
        compiler_params=params(8),
        cost_estimate=cost(tokens * half * 6 * CHUNK, 12 * tokens * half),
        name="inner",
    )(place, in_hbm(queries), after, *[in_vmem(x) for x in (first_queries, *keys, *vals, before)])


def other_kernel(first_head, after_ref, query_ref, key_ref, value_ref, before_ref, inner_ref, zero_ref):
    chunks = query_ref.shape[0] // CHUNK
    inner_body(chunks, {}, (query_ref,), (key_ref,), (value_ref,), before_ref, (inner_ref,), zero_ref, first_head)


def other_inner(queries, keys, vals, before, after, first_head, count):
    tokens = queries.shape[0]
    width = count * HEAD_DIM
    return pl.pallas_call(
        lambda *refs: other_kernel(first_head, *refs),
        in_specs=[ANYWHERE] + [WHOLE] * 4,
        out_specs=[WHOLE] * 2,
        out_shape=[pltpu.VMEM((tokens, width), F32), pltpu.VMEM((1, HEAD_DIM), F32)],
        compiler_params=params(8),
        cost_estimate=cost(tokens * width * 6 * CHUNK, 12 * tokens * width),
        name="inner",
    )(after, *[in_vmem(x) for x in (queries, keys, vals, before)])


def mix_kernel(parts, first_head, first, last, *refs):
    query_refs, (inner_ref, prefix_ref, *refs) = refs[:parts], refs[parts:]
    extra_ref, mixed_ref, result_ref = (None, *refs) if first else refs
    heads = range(inner_ref.shape[1] // HEAD_DIM)
    blocks = [prefix_ref[head(j), :].astype(BF16) for j in heads]
    for c in range(inner_ref.shape[0] // CHUNK):
        squares = None if first else extra_ref[chunk(c), :]
        query_ref, q = chunk_in(query_refs, c)
        for j in heads:
            mixed = inner_ref[chunk(c), head(j)] + dot_nn(query_ref[q, head(first_head + j)], blocks[j])
            square = mixed * mixed
            squares = square if squares is None else squares + square
            mixed_ref[chunk(c), head(j)] = mixed
        if last:
            result_ref[:, chunk(c)] = jnp.sum(jnp.transpose(squares), axis=0, keepdims=True)
        else:
            result_ref[chunk(c), :] = squares


def mix(queries, inner_group, prefix, squares, first_head, last):
    tokens = inner_group.shape[0]
    first = squares is None
    operands = [*queries, inner_group, prefix] + ([] if first else [squares])
    return pl.pallas_call(
        lambda *refs: mix_kernel(len(queries), first_head, first, last, *refs),
        in_specs=[WHOLE] * len(operands),
        out_specs=[WHOLE, WHOLE],
        out_shape=[
            pltpu.VMEM(inner_group.shape, F32),
            pltpu.VMEM((1, tokens) if last else (tokens, HEAD_DIM), F32),
        ],
        compiler_params=params(8),
        cost_estimate=cost(2 * tokens * prefix.size, 12 * inner_group.size),
        name="mix",
    )(*[in_vmem(x) for x in operands])


def gate_kernel(mine, place_ref, gate_ref, gain_ref, after_ref, *refs):
    *mixed_refs, gated_ref, zero_ref = refs
    tokens, half = gated_ref.shape
    zero_ref[...] = jnp.zeros_like(zero_ref)
    rows = HEAD_DIM
    columns_of = half_heads(place_ref, mine, half)
    homes = [(ref, j) for ref in mixed_refs for j in range(ref.shape[1] // HEAD_DIM)]

    def step(i, carry):
        at = pl.ds(pl.multiple_of(i * rows, rows), rows)
        for h, (mixed_ref, j) in enumerate(homes):
            gate = gate_ref[at, columns_of(h)].astype(F32)
            factor = (0.5 * gain_ref[:, columns_of(h)]) * (1.0 + jnp.tanh(0.5 * gate))
            gated_ref[at, head(h)] = mixed_ref[at, head(j)] * factor
        return carry

    lax.fori_loop(0, tokens // rows, step, 0)


def gated(place, mixed, gate_input, norm_gain, after, mine):
    tokens, width = gate_input.shape
    return pl.pallas_call(
        lambda *refs: gate_kernel(mine, *refs),
        in_specs=[SCALARS, WHOLE, WHOLE, ANYWHERE] + [WHOLE] * len(mixed),
        out_specs=[WHOLE, WHOLE],
        out_shape=[pltpu.VMEM((tokens, width // 2), F32), pltpu.VMEM((1, tokens), F32)],
        compiler_params=params(8),
        cost_estimate=cost(8 * tokens * width, 2 * tokens * width),
        name="gate",
    )(place, in_vmem(gate_input), norm_gain.reshape(1, width), after, *[in_vmem(x) for x in mixed])


def scale_kernel(features, place_ref, mine_ref, other_ref, power_ref, out_ref, buffer, sems):
    tokens, half = mine_ref.shape
    rows = CHUNK
    copies = []
    for c in range(tokens // rows):
        at = slice(c * rows, (c + 1) * rows)
        power = jnp.broadcast_to(power_ref[:, at], (HEAD_DIM, rows))
        factor = lax.rsqrt(jnp.transpose(power) / features + 1e-06)
        for mine, source in ((True, mine_ref), (False, other_ref)):
            columns_of = half_heads(place_ref, mine, half)
            for h in range(half // HEAD_DIM):
                buffer[at, columns_of(h)] = (source[at, head(h)] * factor).astype(BF16)
        copies.append(pltpu.make_async_copy(buffer.at[at, :], out_ref.at[at, :], sems.at[c]))
        copies[-1].start()
    for copy in copies:
        copy.wait()


def scale(place, mine, other, power, features):
    tokens, half = mine.shape
    return pl.pallas_call(
        lambda *refs: scale_kernel(features, *refs),
        in_specs=[SCALARS, WHOLE, WHOLE, WHOLE],
        out_specs=ANYWHERE,
        out_shape=pltpu.HBM((tokens, 2 * half), BF16),
        scratch_shapes=[pltpu.VMEM((tokens, 2 * half), BF16), pltpu.SemaphoreType.DMA((tokens // CHUNK,))],
        compiler_params=params(8),
        cost_estimate=cost(4 * tokens * half, 4 * tokens * half),
        name="scale",
    )(place, in_vmem(mine), in_vmem(other), in_vmem(power))


def swap(count, bit):
    return [(i, i ^ bit) for i in range(count)]


def general_prefix(blocks, chip, session_of, chip_sum):
    total = chip_sum
    prefix = jnp.zeros_like(chip_sum)
    bit = 1
    while 2 * bit < blocks:
        there = lax.ppermute(total, "ctx", swap(blocks, 2 * bit))
        partner = chip ^ bit
        lower = partner < chip
        end_here = session_of[2 * (chip | (bit - 1)) + 1]
        end_there = session_of[2 * (partner | (bit - 1)) + 1]
        reaches = jnp.logical_and(lower, end_there == session_of[2 * chip])
        prefix = prefix + jnp.where(reaches, 1.0, 0.0) * there
        joined = jnp.where(end_here == end_there, 1.0, 0.0)
        total = jnp.where(lower, total + joined * there, joined * total + there)
        bit *= 2
    return prefix


def zero_after(x):
    def kernel(after_ref, zero_ref):
        zero_ref[...] = jnp.zeros_like(zero_ref)

    return pl.pallas_call(
        kernel,
        in_specs=[ANYWHERE],
        out_specs=WHOLE,
        out_shape=pltpu.VMEM((1, HEAD_DIM), F32),
        compiler_params=params(1),
        name="then",
    )(x)


def two_steps(sums, weight, between, beside):
    there = [lax.ppermute(x, "ctx", [(i, i ^ (2 if i % 2 == 0 else 4)) for i in range(8)]) for x in sums]
    zero = between(sums[0])
    onward = []
    for x, y in zip(sums, there):
        onward.append(weight[2:3] * x + weight[3:4] * y + zero)
        zero = zero_after(onward[-1])
    arrived = [lax.ppermute(x, "ctx", [(i, i ^ (5 if i % 2 == 0 else 3)) for i in range(8)]) for x in onward]
    zero = beside(onward[-1])
    return [weight[4:5] * x for x in there], [x + zero for x in arrived]


def on_device(blocks, features, queries, key_rows, values, gate_input, norm_gain, session_of):
    width = queries.shape[1]
    index = lax.axis_index("ctx").astype(jnp.int32)
    place = index.reshape(1)
    sizes = group_sizes(width // 2 // HEAD_DIM)
    starts = [sum(sizes[:g]) for g in range(GROUPS)]

    sent, sent_before, sent_keys, sent_vals, first_keys, first_vals, weight = sent_states(
        place, session_of, key_rows, values
    )
    got = lax.ppermute(sent, "ctx", swap(blocks, 1))
    kept, (kept_before, late_keys, late_vals, first_queries) = kept_states(
        place, key_rows, values, queries, first_keys, first_vals
    )
    got = [got[at * HEAD_DIM : (at + n) * HEAD_DIM] for at, n in zip(starts, sizes)]
    sums = [x + y for x, y in zip(kept, got)]
    inside, held = {}, {}

    def mine_inside(after):
        keys, vals = (first_keys, late_keys), (first_vals, late_vals)
        late_queries, other_queries, *inside[True], zero = mine_inner(
            place, queries, first_queries, keys, vals, kept_before, after, sizes
        )
        held[True], held[False] = (first_queries, late_queries), (other_queries,)
        return zero

    def other_inside(after, g=0):
        part, zero = other_inner(*held[False], sent_keys, sent_vals, sent_before, after, starts[g], sizes[g])
        inside.setdefault(False, []).append(part)
        return zero

    if blocks == 8:
        own, arrived = two_steps(sums, weight, mine_inside, other_inside)
    else:
        zero = other_inside(mine_inside(sums[0]))
        own = [general_prefix(blocks, index >> 1, session_of, x) + zero for x in sums]
        arrived = [jnp.zeros_like(x) for x in sums]
    even, odd = weight[0:1], weight[1:2]
    others = [lax.ppermute(x + even * k, "ctx", swap(blocks, 1)) for x, k in zip(own, kept)]

    mixed = {True: [], False: []}
    parts, backs = [], []
    squares = None

    def swap_part(g, zero):
        parts.append(arrived[g] + zero)
        backs.append(lax.ppermute(parts[g], "ctx", swap(blocks, 1)))
        return zero_after(parts[g])

    def mix_group(mine, zero, last=False):
        nonlocal squares
        g = len(mixed[mine])
        prefix = own[g] + odd * got[g] + backs[g] if mine else others[g] + parts[g]
        part, squares = mix(held[mine], inside[mine][g], prefix + zero, squares, starts[g], last)
        mixed[mine].append(part)
        return zero_after(squares)

    zero = swap_part(0, jnp.zeros((1, HEAD_DIM), F32))
    for g in range(1, GROUPS):
        zero = other_inside(parts[0], g) + zero
    for g in range(GROUPS):
        zero = mix_group(False, zero)
        if g + 1 < GROUPS:
            zero = swap_part(g + 1, zero)
        zero = mix_group(True, zero, g == GROUPS - 1)
    power = squares
    count = features // width

    def crossed(bit):
        pairs = [(c * count + z, (c ^ 1) * count + (z ^ bit)) for c in range(blocks) for z in range(count)]
        return lax.ppermute(power, ("ctx", "head"), pairs) + lax.ppermute(power, "ctx", swap(blocks, 1))

    gated_other, zero = gated(place, mixed[False], gate_input, norm_gain, power, False)
    power = crossed(1) + zero
    gated_mine, zero = gated(place, mixed[True], gate_input, norm_gain, power, True)
    power = crossed(2) + zero
    bit, swapped = 4, False
    while bit < count:
        power = crossed(bit)
        bit, swapped = 2 * bit, not swapped
    if swapped:
        power = lax.ppermute(power, "ctx", swap(blocks, 1))
    return scale(place, gated_mine, gated_other, power, features)


def solution(mesh):
    blocks = mesh.shape["ctx"]

    def whole(queries, key_rows, values, gate_input, norm_gain, session_of):
        features = queries.shape[1]
        return jax.shard_map(
            lambda *args: on_device(blocks, features, *args),
            mesh=mesh,
            in_specs=(
                P("ctx", "head"),
                P("ctx", "head"),
                P("ctx", "head"),
                P("ctx", "head"),
                P("head"),
                P(),
            ),
            out_specs=P("ctx", "head"),
            check_vma=False,
        )(queries, key_rows, values, gate_input, norm_gain, session_of)

    return whole
```
